32 devices in a mesh: rep: 2 (over y), ep: 4 (over x, core), ad: 4 (over z).
Axes of the slice: x: 2, y: 2, z: 4, core: 2. Of those that a mesh axis runs over, the one named last changes fastest.
Arguments:
- tokens: bfloat16 [1024, 3072], P(('rep', 'ep')), parts along dimension 0, may hold values from -6 to 6
- chosen_experts: int32 [1024, 2], P(('rep', 'ep')), parts along dimension 0, may hold values from 0 to 7, all different within a row; in each aligned block of 128 rows (0 to 127, 128 to 255, ...) at most 48 rows name the same one
- router_gate_logits: float32 [1024, 2], P(('rep', 'ep')), parts along dimension 0, may hold values from -6 to 6
- token_tenant: int32 [1024], P(('rep', 'ep')), parts along dimension 0, may hold values from 0 to 15
- adapter_of_tenant: int32 [32], P('rep'), parts along dimension 0, may hold values from 0 to 63
- adapter_pool_slot: int32 [64], replicated, may hold values from 0 to 63, each once
- gate_weight: bfloat16 [16, 3072, 4096], P('ep', None, 'ad'), may hold values from -0.109375 to 0.109375
- up_weight: bfloat16 [16, 3072, 4096], P('ep', None, 'ad'), may hold values from -0.109375 to 0.109375
- down_weight: bfloat16 [16, 4096, 3072], P('ep', 'ad'), may hold values from -0.0625 to 0.0625
- adapter_input_factors: bfloat16 [64, 16, 16, 4096], P(None, 'ep', None, 'ad'), may hold values from -0.0625 to 0.0625
- adapter_output_factors: bfloat16 [64, 8, 16, 3072], P('ep', None, None, 'ad'), may hold values from -1.5 to 1.5
Outputs:
- mixed: bfloat16 [1024, 3072], P(('rep', 'ep'), 'ad'), parts along dimension 0
The draws below stay inside these ranges and needn't reach their ends.
There are 2 independent parts, one for each index of `rep`. The reference program is written for one: setup_inputs(seed, part) draws one part's arguments, and reference() takes and returns one part's arrays. A program takes and returns all parts, laid end to end along the dimension named above; an argument that names none is the same for every part. Nothing has to cross between parts.
Inputs may be any that keep to these rules, and one draw needn't show every extreme that they name: `chosen_experts`: each row names 2 different experts. Among the 128 rows of one index of ep no expert is named by more than 48 rows, a bound that some block reaches of them. `adapter_pool_slot`: A permutation: every adapter has its own slot.
All inputs are finite; a program needn't handle non-finite values.
Results may differ from the reference program's by a relative error of at most 0.012.
Values may be sent and summed in bfloat16 or wider, within the bound.
No kernel may reach another device: no remote copies, remote signals or barrier semaphores. Data moves between devices by JAX's collectives and lax.ppermute only.
A program may use at most 256 MiB of HBM per device.

```python
import math
import jax
import jax.numpy as jnp
import numpy as np
from jax import lax

MODEL_WIDTH = 3072
EXPERT_HIDDEN = 8192
EXPERT_COUNT = 8
TOP = 2
ADAPTER_RANK = 16
POOL_SLOTS = 64
TENANTS = 16
TOK_DEV = 128
CAP = 48
TOKENS = 512
N_EP = 4
N_AD = 4


def plant(values, rng, low, largest):
    extent = values.shape
    index_at = [jax.random.randint(jax.random.fold_in(rng, axis), (), 0, extent[axis]) for axis in range(len(extent))]
    values = values.at[tuple(index_at)].set(low)
    longest = extent.index(max(extent))
    index_at[longest] = (index_at[longest] + 1) % extent[longest]
    return values.at[tuple(index_at)].set(largest)


def shard_levels(rng, dims, cuts, least, top_value):
    level, own = 1.0, jax.random.fold_in(rng, 6)
    for position, parts in cuts:
        heights = jnp.exp(jax.random.uniform(jax.random.fold_in(own, position), (parts,), jnp.float32, least / len(cuts), top_value / len(cuts)))
        level = level * jnp.repeat(heights, dims[position] // parts).reshape([-1 if axis == position else 1 for axis in range(len(dims))])
    return level


def deal_out(stream_key, own, number, rows, number_of, top, bound, skew):
    sequence = jax.random.permutation(stream_key, number_of)
    heavy_load, ordinary = load_shares(number_of, rows * top, bound, skew, True), load_shares(number_of, rows * top, bound, skew, False)
    places = jnp.arange(number_of)

    def named(lengths, rotation):
        used = int((lengths > 0).sum())
        fixed = max(1, used // 4)
        shifted = fixed + (places - fixed + rotation * (used - fixed)) % max(1, number_of - fixed)
        return jnp.zeros((number_of,), jnp.int32).at[sequence[jnp.where(places < fixed, places, shifted)]].set(jnp.asarray(lengths, jnp.int32))

    lengths = jnp.where(number % 4 == 0, named(heavy_load, number // 4), named(ordinary, number - number // 4 - 1))
    mixed = jax.random.permutation(jax.random.fold_in(own, 3), number_of)
    giver, receiver = mixed[0:number_of // 2 * 2:2], mixed[1:number_of // 2 * 2:2]
    margin = jnp.minimum(lengths[giver] - 1, bound - lengths[receiver]) // 2
    margin = jnp.where((giver == sequence[0]) | (receiver == sequence[0]) | (lengths[receiver] == 0), 0, jnp.maximum(margin, 0))
    shifted = jax.random.randint(jax.random.fold_in(own, 4), (number_of // 2,), 0, 1 << 20) % (margin + 1)
    lengths = lengths.at[giver].add(-shifted).at[receiver].add(shifted)
    items = jnp.searchsorted(jnp.cumsum(lengths), jnp.arange(rows * top), side="right").astype(jnp.int32)
    listing = items.reshape(top, rows).T
    listing = listing[jax.random.permutation(jax.random.fold_in(own, 1), rows)]
    rotation = jax.random.randint(jax.random.fold_in(own, 2), (rows, 1), 0, top)
    return jnp.take_along_axis(listing, (jnp.arange(top)[None, :] + rotation) % top, axis=1)


def load_shares(number_of, total, bound, skew, full):
    weights = [(1 << 20) // math.isqrt(standing ** skew) + 1 for standing in range(1, number_of + 1)]
    largest = bound if full else min(bound, max(-(-total // number_of), total * weights[0] // sum(weights)))
    least = 1 if total - largest >= number_of - 1 else 0
    given, spare = [largest] + [least] * (number_of - 1), total - largest - least * (number_of - 1)
    while spare > 0:
        free = [i for i in range(1, number_of) if given[i] < largest] or [i for i in range(1, number_of) if given[i] < bound]
        mass, left = sum([weights[i] for i in free]), spare
        for i in free:
            more = min(bound - given[i], max(1, left * weights[i] // mass), spare)
            given[i] = given[i] + more
            spare = spare - more
    return np.array(given)


def normal_values(rng, dims, width, most, shards=(), kind=jnp.bfloat16):
    gain = shard_levels(rng, dims, shards, -0.22, 0.18) if shards else 1.0
    values = jax.random.normal(rng, dims, jnp.float32) * width * gain
    return jnp.minimum(jnp.maximum(values, -most), most).astype(kind)


def setup_inputs(seed: int = 0, part: int = 0) -> dict:
    seeds = jax.random.split(jax.random.key(seed), 12)
    own_keys = jax.random.split(jax.random.fold_in(seeds[11], part), 12)
    tokens = normal_values(own_keys[0], (TOKENS, MODEL_WIDTH), 1.0, 6.0, ((0, 4),))
    chosen_experts_keys = jax.random.split(jax.random.fold_in(own_keys[1], 1), TOKENS // TOK_DEV)
    chosen_experts_turns = jax.random.permutation(jax.random.fold_in(own_keys[1], 3), TOKENS // TOK_DEV)
    chosen_experts = jax.vmap(lambda own, number: deal_out(jax.random.fold_in(own_keys[1], 2), own, number, TOK_DEV, EXPERT_COUNT, TOP, CAP, 2))(chosen_experts_keys, chosen_experts_turns).reshape((TOKENS, TOP))
    router_gate_logits = normal_values(own_keys[2], (TOKENS, TOP), 1.5, 6.0, ((0, 4),), jnp.float32)
    token_tenant = plant(jax.random.randint(own_keys[3], (TOKENS,), 0, TENANTS), jax.random.fold_in(own_keys[3], 1), 0, TENANTS - 1).astype(jnp.int32)
    adapter_of_tenant = plant(jax.random.randint(own_keys[4], (TENANTS,), 0, POOL_SLOTS), jax.random.fold_in(own_keys[4], 1), 0, POOL_SLOTS - 1).astype(jnp.int32)
    adapter_pool_slot = jax.random.permutation(seeds[5], POOL_SLOTS).astype(jnp.int32)
    gate_weight = normal_values(seeds[6], (2 * EXPERT_COUNT, MODEL_WIDTH, EXPERT_HIDDEN // 2), MODEL_WIDTH ** -0.5, 0.109375, ((0, 4), (2, 4)))
    up_weight = normal_values(seeds[7], (2 * EXPERT_COUNT, MODEL_WIDTH, EXPERT_HIDDEN // 2), MODEL_WIDTH ** -0.5, 0.109375, ((0, 4), (2, 4)))
    down_weight = normal_values(seeds[8], (2 * EXPERT_COUNT, EXPERT_HIDDEN // 2, MODEL_WIDTH), EXPERT_HIDDEN ** -0.5, 0.0625, ((0, 4), (1, 4)))
    adapter_input_factors = normal_values(seeds[9], (POOL_SLOTS, 2 * EXPERT_COUNT, ADAPTER_RANK, EXPERT_HIDDEN // 2), EXPERT_HIDDEN ** -0.5, 0.0625, ((1, 4), (3, 4)))
    adapter_output_factors = normal_values(seeds[10], (POOL_SLOTS, EXPERT_COUNT, ADAPTER_RANK, MODEL_WIDTH), ADAPTER_RANK ** -0.5, 1.5, ((0, 4), (3, 4)))
    return {"tokens": tokens, "chosen_experts": chosen_experts, "router_gate_logits": router_gate_logits, "token_tenant": token_tenant, "adapter_of_tenant": adapter_of_tenant, "adapter_pool_slot": adapter_pool_slot, "gate_weight": gate_weight, "up_weight": up_weight, "down_weight": down_weight, "adapter_input_factors": adapter_input_factors, "adapter_output_factors": adapter_output_factors}


def blocked_down(hidden_half, weight_half):
    block_width = hidden_half.shape[1] // N_AD
    total = jnp.zeros((hidden_half.shape[0], weight_half.shape[1]), jnp.float32)
    for block_index in range(N_AD):
        lo_edge = block_index * block_width
        part_sum = jnp.dot(hidden_half[:, lo_edge:lo_edge + block_width], weight_half[lo_edge:lo_edge + block_width], preferred_element_type=jnp.float32)
        total = total + part_sum.astype(jnp.bfloat16).astype(jnp.float32)
    return total.astype(jnp.bfloat16).astype(jnp.float32)


def reference(tokens, chosen_experts, router_gate_logits, token_tenant, adapter_of_tenant, adapter_pool_slot, gate_weight, up_weight, down_weight, adapter_input_factors, adapter_output_factors):
    slot_of_row = adapter_pool_slot[adapter_of_tenant[token_tenant]].astype(jnp.int32)
    weight = jax.nn.sigmoid(router_gate_logits - router_gate_logits[:, ::-1])
    capacity_rows = N_EP * CAP
    half_width = EXPERT_HIDDEN // 2
    slot_range = jnp.arange(POOL_SLOTS, dtype=jnp.int32)

    def expert_term(expert_number, running):
        chosen = chosen_experts == expert_number
        member = jnp.any(chosen, axis=1)
        row_order = jnp.argsort(jnp.where(member, 0, 1).astype(jnp.int32), stable=True)[:capacity_rows].astype(jnp.int32)
        coefficient = jnp.sum(jnp.where(chosen, weight, jnp.float32(0.0)), axis=1)[row_order]
        row_block = tokens[row_order]
        leading_half = 2 * expert_number
        gate_full = jnp.concatenate([gate_weight[leading_half], gate_weight[leading_half + 1]], axis=1)
        up_full = jnp.concatenate([up_weight[leading_half], up_weight[leading_half + 1]], axis=1)
        gate_value = jnp.dot(row_block, gate_full, preferred_element_type=jnp.float32)
        up_value = jnp.dot(row_block, up_full, preferred_element_type=jnp.float32)
        hidden_units = (jax.nn.silu(gate_value) * up_value).astype(jnp.bfloat16)
        low_half = blocked_down(hidden_units[:, :half_width], down_weight[leading_half])
        high_half = blocked_down(hidden_units[:, half_width:], down_weight[leading_half + 1])
        input_factor = jnp.concatenate([adapter_input_factors[:, leading_half], adapter_input_factors[:, leading_half + 1]], axis=2).reshape(POOL_SLOTS * ADAPTER_RANK, EXPERT_HIDDEN)
        down_projected = jnp.dot(hidden_units, input_factor.T, preferred_element_type=jnp.float32).reshape(capacity_rows, POOL_SLOTS, ADAPTER_RANK)
        slot_hit = (slot_of_row[row_order][:, None] == slot_range[None, :]).astype(jnp.float32)
        spread = (slot_hit[:, :, None] * down_projected).reshape(capacity_rows, POOL_SLOTS * ADAPTER_RANK)
        output_factor = adapter_output_factors[:, expert_number].reshape(POOL_SLOTS * ADAPTER_RANK, MODEL_WIDTH).astype(jnp.float32)
        adapter_out = jnp.dot(spread, output_factor, precision=lax.Precision.HIGHEST)
        contribution = coefficient[:, None] * (low_half + high_half + adapter_out)
        return running.at[row_order].add(contribution)

    mixed = lax.fori_loop(0, EXPERT_COUNT, expert_term, jnp.zeros((TOKENS, MODEL_WIDTH), jnp.float32))
    return mixed.astype(jnp.bfloat16)
```

```python
import functools

import jax
import jax.numpy as jnp
from jax import lax
from jax.experimental import pallas as pl
from jax.experimental.pallas import tpu as pltpu
from jax.sharding import PartitionSpec as P

EXPERT_COUNT = 8
TOP = 2
RANK = 16
CAP = 48
K_CHUNKS = 2
N_TILE = 512
MIB = 1 << 20

F32 = jnp.float32
BF16 = jnp.bfloat16


def mm(a, b):
    return jnp.dot(a, b, preferred_element_type=F32)


def mm_nt(a, b):
    return lax.dot_general(a, b, (((1,), (1,)), ((), ())), preferred_element_type=F32)


def cost(flops, moved, trans=0):
    return pl.CostEstimate(flops=int(flops), bytes_accessed=int(moved), transcendentals=int(trans))


def params(mib):
    return pltpu.CompilerParams(vmem_limit_bytes=mib * MIB)


def vmem():
    return pl.BlockSpec(memory_space=pltpu.VMEM)


def smem():
    return pl.BlockSpec(memory_space=pltpu.SMEM)


def meta_kernel(n_local, scalar_ref, slots_ref, *refs):
    blocks, (p_ref, pt_ref, cols_ref, rows_ref, tslot_ref) = refs[:-5], refs[-5:]
    info = jnp.concatenate([block[...] for block in blocks], axis=1)
    count = info.shape[1]
    first, second, tenant = info[0:1], info[1:2], info[4:5]
    weight_first = jax.nn.sigmoid(info[2:3] - info[3:4])
    weight_second = jax.nn.sigmoid(info[3:4] - info[2:3])
    slot = jnp.zeros_like(tenant)
    for number in range(slots_ref.shape[0]):
        slot = jnp.where(tenant == number, slots_ref[number].astype(F32), slot)
    members, weights = [], []
    for i in range(n_local):
        expert = (scalar_ref[0] + i).astype(F32)
        hit_first, hit_second = first == expert, second == expert
        members.append(jnp.where(hit_first | hit_second, 1.0, 0.0))
        weights.append(jnp.where(hit_first, weight_first, 0.0) + jnp.where(hit_second, weight_second, 0.0))
    member = jnp.concatenate(members + [jnp.zeros((8 - n_local, count), F32)], axis=0)
    before = (
        lax.broadcasted_iota(jnp.int32, (count, count), 0) < lax.broadcasted_iota(jnp.int32, (count, count), 1)
    ).astype(BF16)
    place = jnp.where(member > 0, mm(member.astype(BF16), before), -1.0)
    table = jnp.concatenate(
        [place[0:n_local]] + weights + [slot] + [jnp.zeros((127 - 2 * n_local, count), F32)], axis=0
    )
    columns = table.T
    cols_ref[...] = columns
    rows_ref[...] = table[0:8]
    row_count = p_ref.shape[1]
    tenant_rows = jnp.broadcast_to(tenant, (8, count)).astype(BF16)
    down = lax.broadcasted_iota(jnp.int32, (row_count, count), 0).astype(F32)
    across = lax.broadcasted_iota(jnp.int32, (count, row_count), 1).astype(F32)
    for i in range(n_local):
        picked = (down == place[i : i + 1]).astype(BF16)
        p_ref[i] = picked
        pt_ref[i] = (across == columns[:, i : i + 1]).astype(BF16)
        tslot_ref[i] = mm_nt(tenant_rows, picked)


def build_meta(blocks, expert_base, slots, n_local, row_count):
    count = sum(block.shape[1] for block in blocks)
    return pl.pallas_call(
        functools.partial(meta_kernel, n_local),
        out_shape=(
            jax.ShapeDtypeStruct((n_local, row_count, count), BF16),
            jax.ShapeDtypeStruct((n_local, count, row_count), BF16),
            jax.ShapeDtypeStruct((count, 128), F32),
            jax.ShapeDtypeStruct((8, count), F32),
            jax.ShapeDtypeStruct((n_local, 8, row_count), F32),
        ),
        in_specs=[smem(), smem()] + [vmem()] * len(blocks),
        out_specs=(vmem(),) * 5,
        compiler_params=params(48),
        cost_estimate=cost(2 * 8 * count * count, 4 * n_local * row_count * count),
        name="routing_tables",
    )(expert_base, slots, *blocks)


def factor_kernel(slots_ref, pool_ref, out_ref, sems):
    copies = []
    for number in range(out_ref.shape[0]):
        copies.append(pltpu.make_async_copy(pool_ref.at[slots_ref[number]], out_ref.at[number], sems.at[number]))
    for copy in copies:
        copy.start()
    for copy in copies:
        copy.wait()


def take_factors(slots, pool):
    tenants = slots.shape[0]
    shape = (tenants,) + pool.shape[1:]
    return pl.pallas_call(
        factor_kernel,
        out_shape=jax.ShapeDtypeStruct(shape, pool.dtype),
        in_specs=[smem(), pl.BlockSpec(memory_space=pl.ANY)],
        out_specs=pl.BlockSpec(memory_space=pl.ANY),
        scratch_shapes=[pltpu.SemaphoreType.DMA((tenants,))],
        cost_estimate=cost(0, 2 * shape[0] * shape[1] * shape[2] * shape[3] * 2),
        name="tenant_factors",
    )(slots, pool)


def expert_kernel(n_blocks, halves_each, is_first, is_last, *refs):
    blocks, refs = refs[:n_blocks], refs[n_blocks:]
    p_ref, gate_ref, up_ref, refs = refs[0], refs[1], refs[2], refs[3:]
    if not is_first:
        gate_in, up_in, refs = refs[0], refs[1], refs[2:]
    half, tile = pl.program_id(0), pl.program_id(1)
    if is_last:
        factor_ref, tslot_ref, rows_ref, hidden_ref, low_ref, packed, low_acc = refs
    else:
        gate_out, up_out, packed = refs

    @pl.when((tile == 0) & (half % halves_each == 0))
    def _():
        whole = jnp.concatenate([block[...] for block in blocks], axis=0)
        packed[...] = mm(p_ref[half // halves_each], whole).astype(BF16)

    rows = packed[...]
    gate = mm(rows, gate_ref[0])
    up = mm(rows, up_ref[0])
    if not is_first:
        gate = gate + gate_in[0]
        up = up + up_in[0]
    if not is_last:
        gate_out[0] = gate
        up_out[0] = up
        return
    hidden = (jax.nn.silu(gate) * up).astype(BF16)
    hidden_ref[0] = hidden
    tenants, rank = factor_ref.shape[0], factor_ref.shape[2]
    factors = factor_ref[:, 0].reshape(tenants * rank, factor_ref.shape[3])
    low = mm_nt(factors, hidden)
    starts = (tile == 0) & (half % halves_each == 0)

    @pl.when(starts)
    def _():
        low_acc[...] = low

    @pl.when(jnp.logical_not(starts))
    def _():
        low_acc[...] += low

    @pl.when((tile == pl.num_programs(1) - 1) & (half % halves_each == halves_each - 1))
    def _():
        for i in range(p_ref.shape[0]):

            @pl.when(half // halves_each == i)
            def _():
                owner = tslot_ref[i][0:1]
                total = jnp.zeros((rank, packed.shape[0]), F32)
                for number in range(tenants):
                    total = total + jnp.where(owner == number, low_acc[number * rank : (number + 1) * rank], 0.0)
                weight = rows_ref[p_ref.shape[0] + i : p_ref.shape[0] + i + 1]
                low_ref[i * rank : (i + 1) * rank] = (mm(total.astype(BF16), p_ref[i]) * weight).astype(BF16)


def expert_part(blocks, part, parts, picked, gate, up, sums, factors, tslot, table_rows):
    local_halves, width, hidden_count = gate.shape
    part_width = width // parts
    n_local, row_count, count = picked.shape
    halves_each = local_halves // n_local
    tile = min(N_TILE, hidden_count)
    is_first, is_last = part == 0, part == parts - 1

    def constant(array):
        return pl.BlockSpec(array.shape, lambda h, n: (0,) * array.ndim)

    weight_spec = pl.BlockSpec((1, part_width, tile), lambda h, n: (h, part, n))
    sum_spec = pl.BlockSpec((1, row_count, tile), lambda h, n: (h, 0, n))
    in_specs = [constant(block) for block in blocks] + [constant(picked), weight_spec, weight_spec]
    operands = list(blocks) + [picked, gate, up]
    aliases = {}
    if not is_first:
        if not is_last:
            aliases = {len(operands): 0, len(operands) + 1: 1}
        in_specs += [sum_spec, sum_spec]
        operands += list(sums)
    scratch = [pltpu.VMEM((row_count, part_width), BF16)]
    if is_last:
        tenants, _, rank, _ = factors.shape
        in_specs += [
            pl.BlockSpec((tenants, 1, rank, tile), lambda h, n: (0, h, 0, n)),
            constant(tslot),
            constant(table_rows),
        ]
        operands += [factors, tslot, table_rows]
        out_shape = (
            jax.ShapeDtypeStruct((local_halves, row_count, hidden_count), BF16),
            jax.ShapeDtypeStruct((n_local * rank, count), BF16),
        )
        out_specs = (sum_spec, pl.BlockSpec((n_local * rank, count), lambda h, n: (0, 0)))
        scratch.append(pltpu.VMEM((tenants * rank, row_count), F32))
    else:
        out_shape = (jax.ShapeDtypeStruct((local_halves, row_count, hidden_count), F32),) * 2
        out_specs = (sum_spec, sum_spec)
    return pl.pallas_call(
        functools.partial(expert_kernel, len(blocks), halves_each, is_first, is_last),
        grid=(local_halves, hidden_count // tile),
        out_shape=out_shape,
        in_specs=in_specs,
        out_specs=out_specs,
        scratch_shapes=scratch,
        input_output_aliases=aliases,
        compiler_params=params(48),
        cost_estimate=cost(
            4 * local_halves * row_count * part_width * hidden_count, 4 * local_halves * part_width * hidden_count
        ),
        name="gate_up_part",
    )(*operands)


def down_kernel(halves_each, raw, target_ref, hidden_ref, weight_ref, pt_ref, cols_ref, *refs):
    half = pl.program_id(0)
    outs, (part_sum, total) = refs[:-2], refs[-2:]
    product = mm(hidden_ref[0], weight_ref[0])
    n_local = pt_ref.shape[0]

    @pl.when(half % halves_each == 0)
    def _():
        part_sum[...] = product

    @pl.when(half % halves_each != 0)
    def _():
        part_sum[...] += product

    for i in range(n_local):

        @pl.when(half == (i + 1) * halves_each - 1)
        def _():
            laid = mm(pt_ref[i], part_sum[...].astype(BF16)) * cols_ref[:, n_local + i : n_local + i + 1]
            if i > 0:
                laid = laid + total[...]
            if i < n_local - 1:
                total[...] = laid
            elif raw:
                outs[0][...] = laid
            else:
                write_pairs(laid, outs)


def write_pairs(total, outs):
    keep, send = outs
    for b in range(total.shape[0] // 128):
        (send if b % 2 else keep)[b // 2 * 128 : b // 2 * 128 + 128] = total[b * 128 : b * 128 + 128].astype(BF16)


def down_part(target, hidden, down, pt, cols, span, raw):
    local_halves, row_count, hidden_count = hidden.shape
    n_local, count, _ = pt.shape
    halves_each = local_halves // n_local
    if raw:
        out_shape = (jax.ShapeDtypeStruct((count, span), F32),)
    else:
        out_shape = (jax.ShapeDtypeStruct((count // 2, span), BF16),) * 2
    return pl.pallas_call(
        functools.partial(down_kernel, halves_each, raw),
        grid_spec=pltpu.PrefetchScalarGridSpec(
            num_scalar_prefetch=1,
            grid=(local_halves,),
            in_specs=[
                pl.BlockSpec((1, row_count, hidden_count), lambda h, t: (h, 0, 0)),
                pl.BlockSpec((1, hidden_count, span), lambda h, t: (h, 0, t[0])),
                pl.BlockSpec(pt.shape, lambda h, t: (0, 0, 0)),
                pl.BlockSpec(cols.shape, lambda h, t: (0, 0)),
            ],
            out_specs=tuple(pl.BlockSpec(s.shape, lambda h, t: (0, 0)) for s in out_shape),
            scratch_shapes=[pltpu.VMEM((row_count, span), F32), pltpu.VMEM((count, span), F32)],
        ),
        out_shape=out_shape,
        compiler_params=params(48),
        cost_estimate=cost(
            2 * local_halves * row_count * hidden_count * span, 2 * local_halves * hidden_count * span
        ),
        name="down_part",
    )(target, hidden, down, pt, cols)


def adapter_kernel(scalar_ref, base_ref, factor_ref, cols_ref, slot_column, *refs):
    lows, (keep, send, wide) = refs[:-3], refs[-3:]
    wide[...] = jnp.zeros_like(wide)
    height = lows[0].shape[0]
    count = base_ref.shape[0]
    blocks = count // 128
    for m in range(len(lows)):
        start = pl.multiple_of(scalar_ref[1 + m], RANK)
        value = lows[m][...].astype(F32)
        value = jnp.concatenate([value[:, (m ^ b) * 128 : (m ^ b) * 128 + 128] for b in range(blocks)], axis=1)
        wide[pl.ds(start, height)] += value
    low = wide[...].T.astype(BF16)
    zero = jnp.zeros_like(low)
    slot = cols_ref[:, slot_column : slot_column + 1]
    depth = EXPERT_COUNT * RANK
    slot_count = factor_ref.shape[0] // depth
    total = base_ref[...]
    for j in range(0, slot_count, 2):
        spread = jnp.concatenate(
            [jnp.where(slot == (scalar_ref[0] + j + i).astype(F32), low, zero) for i in range(2)], axis=1
        )
        total = total + mm(spread, factor_ref[j * depth : (j + 2) * depth])
    write_pairs(total, (keep, send))


def adapter_part(scalars, base, factors, cols, slot_column, lows):
    count, span = base.shape

    def kernel(scalar_ref, base_ref, factor_ref, cols_ref, *refs):
        adapter_kernel(scalar_ref, base_ref, factor_ref, cols_ref, slot_column, *refs)

    return pl.pallas_call(
        kernel,
        out_shape=(jax.ShapeDtypeStruct((count // 2, span), BF16),) * 2,
        in_specs=[smem()] + [vmem()] * (3 + len(lows)),
        out_specs=(vmem(),) * 2,
        scratch_shapes=[pltpu.VMEM((EXPERT_COUNT * RANK, count), F32)],
        compiler_params=params(48),
        cost_estimate=cost(2 * count * factors.shape[0] * span, 2 * factors.shape[0] * span),
        name="adapter_part",
    )(scalars, base, factors, cols, *lows)


def per_device(
    n_ep,
    n_ad,
    tokens,
    chosen_experts,
    router_gate_logits,
    token_tenant,
    adapter_of_tenant,
    adapter_pool_slot,
    gate_weight,
    up_weight,
    down_weight,
    adapter_input_factors,
    adapter_output_factors,
):
    width = tokens.shape[1]
    span = width // n_ad
    local_halves = gate_weight.shape[0]
    n_local = max(1, local_halves // 2)
    row_count = n_ep * CAP
    bits = n_ep.bit_length() - 1
    ep_index, ad_index = lax.axis_index("ep"), lax.axis_index("ad")

    def swap(x, mask):
        return lax.ppermute(x, "ep", [(i, i ^ mask) for i in range(n_ep)])

    def shift(x, step):
        return lax.ppermute(x, "ad", [(i, (i + step) % n_ad) for i in range(n_ad)])

    info = jnp.concatenate(
        [
            chosen_experts.astype(F32).T,
            router_gate_logits.T,
            token_tenant.astype(F32)[None],
            jnp.zeros((3, tokens.shape[0]), F32),
        ],
        axis=0,
    )
    infos = [info] + [swap(info, mask) for mask in range(1, n_ep)]

    parts = K_CHUNKS
    part_width = width // parts
    token_parts = []
    for part in range(parts):
        blocks = {0: tokens[:, part * part_width : (part + 1) * part_width]}
        for bit in reversed(range(bits)):
            for mask in list(blocks):
                blocks[mask | 1 << bit] = swap(blocks[mask], 1 << bit)
        token_parts.append([blocks[mask] for mask in range(n_ep)])

    slots = adapter_pool_slot[adapter_of_tenant]
    expert_base = (ep_index * local_halves // 2).astype(jnp.int32).reshape(1)
    picked, pt, cols, table_rows, tslot = build_meta(infos, expert_base, slots, n_local, row_count)
    factors = take_factors(slots, adapter_input_factors)

    state = None
    for part in range(parts):
        state = expert_part(
            token_parts[part], part, parts, picked, gate_weight, up_weight, state, factors, tslot, table_rows
        )
    hidden, low = state

    arrived = [low] + [shift(low, step) for step in range(1, n_ad)]
    low_total = sum(x.astype(F32) for x in arrived).astype(BF16)
    lows = [low_total] + [swap(low_total, mask) for mask in range(1, n_ep)]

    def combine(keep, send):
        mine = (keep.astype(F32) + swap(send, 1).astype(F32)).astype(BF16)
        for bit in range(1, bits):
            half = mine.shape[0] // 128 // 2
            grouped = mine.reshape(half, 2, 128, mine.shape[1])
            keep = grouped[:, 0].reshape(half * 128, -1)
            send = grouped[:, 1].reshape(half * 128, -1)
            mine = (keep.astype(F32) + swap(send, 1 << bit).astype(F32)).astype(BF16)
        return mine

    results = []
    for step in range(1, n_ad):
        target = ((ad_index + step) % n_ad).astype(jnp.int32).reshape(1)
        keep, send = down_part(target, hidden, down_weight, pt, cols, span, False)
        results.append(shift(combine(keep, send), step))
    (base,) = down_part(ad_index.astype(jnp.int32).reshape(1), hidden, down_weight, pt, cols, span, True)
    slot_count = adapter_output_factors.shape[0]
    scalars = jnp.stack(
        [ep_index * slot_count] + [((ep_index ^ mask) * local_halves // 2) * RANK for mask in range(n_ep)]
    ).astype(jnp.int32)
    flat_factors = adapter_output_factors.reshape(slot_count * EXPERT_COUNT * RANK, span)
    keep, send = adapter_part(scalars, base, flat_factors, cols, 2 * n_local, lows)
    results.append(combine(keep, send))
    return sum(x.astype(F32) for x in results).astype(BF16)


def solution(mesh):
    placed = (
        P(("rep", "ep"), None),
        P(("rep", "ep"), None),
        P(("rep", "ep"), None),
        P(("rep", "ep")),
        P("rep"),
        P(),
        P("ep", None, "ad"),
        P("ep", None, "ad"),
        P("ep", "ad", None),
        P(None, "ep", None, "ad"),
        P("ep", None, None, "ad"),
    )
    return jax.shard_map(
        functools.partial(per_device, mesh.shape["ep"], mesh.shape["ad"]),
        mesh=mesh,
        in_specs=placed,
        out_specs=P(("rep", "ep"), "ad"),
        check_vma=False,
    )
```

```python
import functools

import jax
import jax.numpy as jnp
from jax import lax
from jax.experimental import pallas as pl
from jax.experimental.pallas import tpu as pltpu
from jax.sharding import PartitionSpec as P

EXPERT_COUNT = 8
TOP = 2
RANK = 16
CAP = 48
K_CHUNKS = 3
N_TILE = 512
MIB = 1 << 20

F32 = jnp.float32
BF16 = jnp.bfloat16


def mm(a, b):
    return jnp.dot(a, b, preferred_element_type=F32)


def mm_nt(a, b):
    return lax.dot_general(a, b, (((1,), (1,)), ((), ())), preferred_element_type=F32)


def cost(flops, moved, trans=0):
    return pl.CostEstimate(flops=int(flops), bytes_accessed=int(moved), transcendentals=int(trans))


def params(mib):
    return pltpu.CompilerParams(vmem_limit_bytes=mib * MIB)


def vmem():
    return pl.BlockSpec(memory_space=pltpu.VMEM)


def smem():
    return pl.BlockSpec(memory_space=pltpu.SMEM)


def meta_kernel(n_local, scalar_ref, slots_ref, *refs):
    blocks, (p_ref, pt_ref, cols_ref, rows_ref, tslot_ref) = refs[:-5], refs[-5:]
    info = jnp.concatenate([block[...] for block in blocks], axis=1)
    count = info.shape[1]
    first, second, tenant = info[0:1], info[1:2], info[4:5]
    weight_first = jax.nn.sigmoid(info[2:3] - info[3:4])
    weight_second = jax.nn.sigmoid(info[3:4] - info[2:3])
    slot = jnp.zeros_like(tenant)
    for number in range(slots_ref.shape[0]):
        slot = jnp.where(tenant == number, slots_ref[number].astype(F32), slot)
    members, weights = [], []
    for i in range(n_local):
        expert = (scalar_ref[0] + i).astype(F32)
        hit_first, hit_second = first == expert, second == expert
        members.append(jnp.where(hit_first | hit_second, 1.0, 0.0))
        weights.append(jnp.where(hit_first, weight_first, 0.0) + jnp.where(hit_second, weight_second, 0.0))
    member = jnp.concatenate(members + [jnp.zeros((8 - n_local, count), F32)], axis=0)
    before = (
        lax.broadcasted_iota(jnp.int32, (count, count), 0) < lax.broadcasted_iota(jnp.int32, (count, count), 1)
    ).astype(BF16)
    place = jnp.where(member > 0, mm(member.astype(BF16), before), -1.0)
    table = jnp.concatenate(
        [place[0:n_local]] + weights + [slot] + [jnp.zeros((127 - 2 * n_local, count), F32)], axis=0
    )
    columns = table.T
    cols_ref[...] = columns
    rows_ref[...] = table[0:8]
    row_count = p_ref.shape[1]
    tenant_rows = jnp.broadcast_to(tenant, (8, count)).astype(BF16)
    down = lax.broadcasted_iota(jnp.int32, (row_count, count), 0).astype(F32)
    across = lax.broadcasted_iota(jnp.int32, (count, row_count), 1).astype(F32)
    for i in range(n_local):
        picked = (down == place[i : i + 1]).astype(BF16)
        p_ref[i] = picked
        pt_ref[i] = (across == columns[:, i : i + 1]).astype(BF16)
        tslot_ref[i] = mm_nt(tenant_rows, picked)


def build_meta(blocks, expert_base, slots, n_local, row_count):
    count = sum(block.shape[1] for block in blocks)
    return pl.pallas_call(
        functools.partial(meta_kernel, n_local),
        out_shape=(
            jax.ShapeDtypeStruct((n_local, row_count, count), BF16),
            jax.ShapeDtypeStruct((n_local, count, row_count), BF16),
            jax.ShapeDtypeStruct((count, 128), F32),
            jax.ShapeDtypeStruct((8, count), F32),
            jax.ShapeDtypeStruct((n_local, 8, row_count), F32),
        ),
        in_specs=[smem(), smem()] + [vmem()] * len(blocks),
        out_specs=(vmem(),) * 5,
        compiler_params=params(max(8, 12 * count * count // MIB)),
        cost_estimate=cost(2 * 8 * count * count, 4 * n_local * row_count * count),
        name="routing_tables",
    )(expert_base, slots, *blocks)


def slab(ref, part, half, tile, ring_ref):
    depth, width = ring_ref.shape[1], ring_ref.shape[2]
    return ref.at[half, pl.ds(part * depth, depth), pl.ds(tile * width, width)]


def slab_copy(gate_ref, up_ref, ring_ref, sems, part, half, tile, which):
    tiles = gate_ref.shape[2] // ring_ref.shape[2]
    slot = (half * tiles + tile) * 2 + which
    source = slab((gate_ref, up_ref)[which], part, half, tile, ring_ref)
    return pltpu.make_async_copy(source, ring_ref.at[slot], sems.at[slot])


def prefetch_kernel(gate_ref, up_ref, ring_ref, mark_ref, sems):
    tiles = gate_ref.shape[2] // ring_ref.shape[2]
    copies = [
        slab_copy(gate_ref, up_ref, ring_ref, sems, 0, half, tile, which)
        for half in range(gate_ref.shape[0])
        for tile in range(tiles)
        for which in range(2)
    ]
    for copy in copies:
        copy.start()
    mark_ref[...] = jnp.zeros_like(mark_ref)
    for copy in copies:
        copy.wait()


def prefetch(gate, up, part_width):
    local_halves, _, hidden_count = gate.shape
    tile = min(N_TILE, hidden_count)
    slots = 2 * local_halves * (hidden_count // tile)
    return pl.pallas_call(
        prefetch_kernel,
        out_shape=(
            pltpu.VMEM((slots, part_width, tile), BF16),
            jax.ShapeDtypeStruct((8, 128), F32),
        ),
        in_specs=[pl.BlockSpec(memory_space=pltpu.HBM)] * 2,
        out_specs=(vmem(), vmem()),
        scratch_shapes=[pltpu.SemaphoreType.DMA((slots,))],
        compiler_params=params(4),
        cost_estimate=cost(0, 2 * slots * part_width * tile * 2),
        name="weight_prefetch",
    )(gate, up)


def expert_kernel(n_blocks, part, parts, *refs):
    is_first, is_last = part == 0, part == parts - 1
    blocks, refs = refs[:n_blocks], refs[n_blocks:]
    p_ref, gate_ref, up_ref, ring_ref, refs = refs[1], refs[2], refs[3], refs[4], refs[5:]
    if not is_first:
        gate_in, up_in, refs = refs[0], refs[1], refs[2:]
    if is_last:
        slots_ref, target_ref, pool_ref, tslot_ref, rows_ref, down_ref = refs[:6]
        ring_out, hidden_ref, low_ref, next_ref, packed, sems, factors, factor_sems, down_sems = refs[6:]
    else:
        ring_out, gate_out, up_out, packed, sems = refs
    n_local = p_ref.shape[0]
    local_halves, _, hidden_count = gate_ref.shape
    halves_each = local_halves // n_local
    width = ring_ref.shape[2]
    tiles = hidden_count // width
    last = (local_halves - 1, tiles - 1)

    def refill(number, half, tile, which):
        return slab_copy(gate_ref, up_ref, ring_out, sems, number, half, tile, which)

    if not is_first:
        for which in range(2):
            refill(part, *last, which).start()
    if is_last:
        down_copies = down_fetch(target_ref, down_ref, next_ref, down_sems)
        for copy in down_copies:
            copy.start()
        tenants, rank = slots_ref.shape[0], pool_ref.shape[2]
        factor_copies = [
            pltpu.make_async_copy(
                pool_ref.at[slots_ref[number]], factors.at[:, number * rank : (number + 1) * rank], factor_sems.at[number]
            )
            for number in range(tenants)
        ]
        for copy in factor_copies:
            copy.start()
    whole = jnp.concatenate([block[...] for block in blocks], axis=0)
    for i in range(n_local):
        packed[i] = mm(p_ref[i], whole).astype(BF16)

    def step(half, carry):
        rows = packed[half // halves_each]
        for tile in range(tiles):
            slot = (half * tiles + tile) * 2
            if tile == tiles - 1 and not is_first:

                @pl.when(half == local_halves - 1)
                def _():
                    for which in range(2):
                        refill(part, *last, which).wait()

            span = slice(tile * width, (tile + 1) * width)
            gate = mm(rows, ring_out[slot])
            up = mm(rows, ring_out[slot + 1])
            if not is_first:
                gate = gate + gate_in[half, :, span]
                up = up + up_in[half, :, span]
            if is_last:
                hidden_ref[half, :, span] = (jax.nn.silu(gate) * up).astype(BF16)
                continue
            gate_out[half, :, span] = gate
            up_out[half, :, span] = up
            if tile < tiles - 1:
                for which in range(2):
                    refill(part + 1, half, tile, which).start()
            else:

                @pl.when(half < local_halves - 1)
                def _():
                    for which in range(2):
                        refill(part + 1, half, tile, which).start()

        return carry

    lax.fori_loop(0, local_halves, step, 0)
    if not is_last:
        for half in range(local_halves):
            for tile in range(tiles):
                if (half, tile) != last:
                    for which in range(2):
                        refill(part + 1, half, tile, which).wait()
        return
    for copy in factor_copies:
        copy.wait()
    for i in range(n_local):
        low = mm_nt(factors[i * halves_each], hidden_ref[i * halves_each])
        for half in range(i * halves_each + 1, (i + 1) * halves_each):
            low = low + mm_nt(factors[half], hidden_ref[half])
        owner = tslot_ref[i][0:1]
        total = jnp.zeros((rank, low.shape[1]), F32)
        for number in range(tenants):
            total = total + jnp.where(owner == number, low[number * rank : (number + 1) * rank], 0.0)
        weight = rows_ref[n_local + i : n_local + i + 1]
        low_ref[i * rank : (i + 1) * rank] = (mm(total.astype(BF16), p_ref[i]) * weight).astype(BF16)
    for copy in down_copies:
        copy.wait()


def expert_part(blocks, part, parts, mark, picked, gate, up, ring, sums, slots, target, pool, tslot, table_rows, down, span):
    local_halves, width, hidden_count = gate.shape
    part_width = width // parts
    n_local, row_count, count = picked.shape
    is_first, is_last = part == 0, part == parts - 1
    hbm = pl.BlockSpec(memory_space=pltpu.HBM)
    in_specs = [vmem()] * (len(blocks) + 2) + [hbm, hbm, vmem()]
    operands = list(blocks) + [mark, picked, gate, up, ring]
    aliases = {len(operands) - 1: 0}
    if not is_first:
        if not is_last:
            aliases.update({len(operands): 1, len(operands) + 1: 2})
        in_specs += [vmem(), vmem()]
        operands += [pltpu.with_memory_space_constraint(x, pltpu.VMEM) for x in sums]
    scratch = [pltpu.VMEM((n_local, row_count, part_width), BF16), pltpu.SemaphoreType.DMA((ring.shape[0],))]
    if is_last:
        tenants, rank = slots.shape[0], pool.shape[2]
        in_specs += [smem(), smem(), hbm, vmem(), vmem(), hbm]
        operands += [slots, target, pool, tslot, table_rows, down]
        out_shape = (
            pltpu.VMEM(ring.shape, BF16),
            pltpu.VMEM((local_halves, row_count, hidden_count), BF16),
            jax.ShapeDtypeStruct((n_local * rank, count), BF16),
            pltpu.VMEM((local_halves, hidden_count, span), BF16),
        )
        scratch += [
            pltpu.VMEM((local_halves, tenants * rank, hidden_count), BF16),
            pltpu.SemaphoreType.DMA((tenants,)),
            pltpu.SemaphoreType.DMA((local_halves,)),
        ]
    else:
        out_shape = (pltpu.VMEM(ring.shape, BF16),) + (pltpu.VMEM((local_halves, row_count, hidden_count), F32),) * 2
    return pl.pallas_call(
        functools.partial(expert_kernel, len(blocks), part, parts),
        out_shape=out_shape,
        in_specs=in_specs,
        out_specs=(vmem(),) * len(out_shape),
        scratch_shapes=scratch,
        input_output_aliases=aliases,
        compiler_params=params(max(10, 10 * n_local * row_count * part_width // MIB)),
        cost_estimate=cost(
            4 * local_halves * row_count * part_width * hidden_count, 4 * local_halves * part_width * hidden_count
        ),
        name="gate_up_part",
    )(*operands)


def down_fetch(target_ref, down_ref, next_ref, sems):
    span = next_ref.shape[2]
    start = pl.multiple_of(target_ref[0] * span, span)
    return [
        pltpu.make_async_copy(down_ref.at[half, :, pl.ds(start, span)], next_ref.at[half], sems.at[half])
        for half in range(down_ref.shape[0])
    ]


def down_kernel(is_final, *refs):
    if is_final:
        hidden_ref, weight_ref, pt_ref, cols_ref, base_ref = refs
    else:
        target_ref, hidden_ref, weight_ref, down_ref, pt_ref, cols_ref, keep, send, next_ref, sems = refs
        copies = down_fetch(target_ref, down_ref, next_ref, sems)
        for copy in copies:
            copy.start()
    n_local = pt_ref.shape[0]
    halves_each = hidden_ref.shape[0] // n_local
    total = None
    for i in range(n_local):
        part_sum = mm(hidden_ref[i * halves_each], weight_ref[i * halves_each])
        for half in range(i * halves_each + 1, (i + 1) * halves_each):
            part_sum = part_sum + mm(hidden_ref[half], weight_ref[half])
        laid = mm(pt_ref[i], part_sum.astype(BF16)) * cols_ref[:, n_local + i : n_local + i + 1]
        total = laid if total is None else total + laid
    if is_final:
        base_ref[...] = total
    else:
        write_pairs(total, (keep, send))
        for copy in copies:
            copy.wait()


def down_part(next_target, hidden, weights, down, pt, cols):
    local_halves, row_count, hidden_count = hidden.shape
    count, span = pt.shape[1], weights.shape[2]
    is_final = next_target is None
    weights = pltpu.with_memory_space_constraint(weights, pltpu.VMEM)
    if is_final:
        out_shape = (jax.ShapeDtypeStruct((count, span), F32),)
        in_specs, operands = [vmem()] * 4, (hidden, weights, pt, cols)
        scratch = []
    else:
        out_shape = (jax.ShapeDtypeStruct((count // 2, span), BF16),) * 2 + (pltpu.VMEM(weights.shape, BF16),)
        in_specs = [smem(), vmem(), vmem(), pl.BlockSpec(memory_space=pltpu.HBM), vmem(), vmem()]
        operands = (next_target, hidden, weights, down, pt, cols)
        scratch = [pltpu.SemaphoreType.DMA((local_halves,))]
    return pl.pallas_call(
        functools.partial(down_kernel, is_final),
        out_shape=out_shape,
        in_specs=in_specs,
        out_specs=(vmem(),) * len(out_shape),
        scratch_shapes=scratch,
        compiler_params=params(max(10, 12 * count * span // MIB)),
        cost_estimate=cost(
            2 * local_halves * row_count * hidden_count * span, 2 * local_halves * hidden_count * span
        ),
        name="down_part",
    )(*operands)


def write_pairs(total, outs):
    keep, send = outs
    for b in range(total.shape[0] // 128):
        (send if b % 2 else keep)[b // 2 * 128 : b // 2 * 128 + 128] = total[b * 128 : b * 128 + 128].astype(BF16)


def adapter_kernel(scalar_ref, base_ref, factor_ref, cols_ref, slot_column, *refs):
    lows, (keep, send, wide) = refs[:-3], refs[-3:]
    wide[...] = jnp.zeros_like(wide)
    height = lows[0].shape[0]
    count = base_ref.shape[0]
    blocks = count // 128
    for m in range(len(lows)):
        start = pl.multiple_of(scalar_ref[1 + m], RANK)
        value = lows[m][...].astype(F32)
        value = jnp.concatenate([value[:, (m ^ b) * 128 : (m ^ b) * 128 + 128] for b in range(blocks)], axis=1)
        wide[pl.ds(start, height)] += value
    low = wide[...].T.astype(BF16)
    zero = jnp.zeros_like(low)
    slot = cols_ref[:, slot_column : slot_column + 1]
    depth = EXPERT_COUNT * RANK
    slot_count = factor_ref.shape[0] // depth
    total = base_ref[...]
    for j in range(0, slot_count, 2):
        spread = jnp.concatenate(
            [jnp.where(slot == (scalar_ref[0] + j + i).astype(F32), low, zero) for i in range(2)], axis=1
        )
        total = total + mm(spread, factor_ref[j * depth : (j + 2) * depth])
    write_pairs(total, (keep, send))


def adapter_part(scalars, base, factors, cols, slot_column, lows):
    count, span = base.shape

    def kernel(scalar_ref, base_ref, factor_ref, cols_ref, *refs):
        adapter_kernel(scalar_ref, base_ref, factor_ref, cols_ref, slot_column, *refs)

    return pl.pallas_call(
        kernel,
        out_shape=(jax.ShapeDtypeStruct((count // 2, span), BF16),) * 2,
        in_specs=[smem()] + [vmem()] * (3 + len(lows)),
        out_specs=(vmem(),) * 2,
        scratch_shapes=[pltpu.VMEM((EXPERT_COUNT * RANK, count), F32)],
        compiler_params=params(max(16, 24 * count * span // MIB)),
        cost_estimate=cost(2 * count * factors.shape[0] * span, 2 * factors.shape[0] * span),
        name="adapter_part",
    )(scalars, base, factors, cols, *lows)


def per_device(
    n_ep,
    n_ad,
    tokens,
    chosen_experts,
    router_gate_logits,
    token_tenant,
    adapter_of_tenant,
    adapter_pool_slot,
    gate_weight,
    up_weight,
    down_weight,
    adapter_input_factors,
    adapter_output_factors,
):
    gate_weight, up_weight, down_weight, adapter_input_factors = [
        pltpu.with_memory_space_constraint(x, pltpu.HBM)
        for x in (gate_weight, up_weight, down_weight, adapter_input_factors)
    ]
    width = tokens.shape[1]
    span = width // n_ad
    local_halves = gate_weight.shape[0]
    n_local = max(1, local_halves // 2)
    row_count = n_ep * CAP
    bits = n_ep.bit_length() - 1
    ep_index, ad_index = lax.axis_index("ep"), lax.axis_index("ad")

    def swap(x, mask):
        return lax.ppermute(x, "ep", [(i, i ^ mask) for i in range(n_ep)])

    def shift(x, step):
        return lax.ppermute(x, "ad", [(i, (i + step) % n_ad) for i in range(n_ad)])

    info = jnp.concatenate(
        [
            chosen_experts.astype(F32).T,
            router_gate_logits.T,
            token_tenant.astype(F32)[None],
            jnp.zeros((3, tokens.shape[0]), F32),
        ],
        axis=0,
    )
    infos = [info] + [swap(info, mask) for mask in range(1, n_ep)]

    parts = K_CHUNKS
    part_width = width // parts
    ring, mark = prefetch(gate_weight, up_weight, part_width)
    token_parts = []
    for part in range(parts):
        blocks = {0: tokens[:, part * part_width : (part + 1) * part_width]}
        for bit in reversed(range(bits)):
            for mask in list(blocks):
                blocks[mask | 1 << bit] = swap(blocks[mask], 1 << bit)
            if bit == bits - 1:
                high = 1 << bit
                blocks[high], mark = lax.optimization_barrier((blocks[high], mark))
        token_parts.append([blocks[mask] for mask in range(n_ep)])

    slots = adapter_pool_slot[adapter_of_tenant]
    expert_base = (ep_index * local_halves // 2).astype(jnp.int32).reshape(1)
    picked, pt, cols, table_rows, tslot = build_meta(infos, expert_base, slots, n_local, row_count)

    def target(step):
        return ((ad_index + step) % n_ad).astype(jnp.int32).reshape(1)

    sums = None
    for part in range(parts):
        state = expert_part(
            token_parts[part], part, parts, mark, picked, gate_weight, up_weight, ring, sums,
            slots, target(1), adapter_input_factors, tslot, table_rows, down_weight, span,
        )
        if part < parts - 1:
            ring, sums = state[0], state[1:]
    _, hidden, low, weights = state

    arrived = [low] + [shift(low, step) for step in range(1, n_ad)]
    low_total = sum(x.astype(F32) for x in arrived).astype(BF16)
    lows = [low_total] + [swap(low_total, mask) for mask in range(1, n_ep)]

    def between(keep, send):
        return (keep.astype(F32) + swap(send, 1).astype(F32)).astype(BF16)

    def across(mine):
        for bit in range(1, bits):
            half = mine.shape[0] // 128 // 2
            grouped = mine.reshape(half, 2, 128, mine.shape[1])
            keep = grouped[:, 0].reshape(half * 128, -1)
            send = grouped[:, 1].reshape(half * 128, -1)
            mine = (keep.astype(F32) + swap(send, 1 << bit).astype(F32)).astype(BF16)
        return mine

    results, pending = [], None
    for step in range(1, n_ad):
        following = target(step + 1)
        if pending is not None:
            pending, following = lax.optimization_barrier((pending, following))
            results.append(shift(across(pending), step - 1))
        keep, send, weights = down_part(following, hidden, weights, down_weight, pt, cols)
        pending = between(keep, send)
    results.append(shift(across(pending), n_ad - 1))
    (base,) = down_part(None, hidden, weights, down_weight, pt, cols)
    slot_count = adapter_output_factors.shape[0]
    scalars = jnp.stack(
        [ep_index * slot_count] + [((ep_index ^ mask) * local_halves // 2) * RANK for mask in range(n_ep)]
    ).astype(jnp.int32)
    flat_factors = adapter_output_factors.reshape(slot_count * EXPERT_COUNT * RANK, span)
    keep, send = adapter_part(scalars, base, flat_factors, cols, 2 * n_local, lows)
    results.append(across(between(keep, send)))
    return sum(x.astype(F32) for x in results).astype(BF16)


def solution(mesh):
    placed = (
        P(("rep", "ep"), None),
        P(("rep", "ep"), None),
        P(("rep", "ep"), None),
        P(("rep", "ep")),
        P("rep"),
        P(),
        P("ep", None, "ad"),
        P("ep", None, "ad"),
        P("ep", "ad", None),
        P(None, "ep", None, "ad"),
        P("ep", None, None, "ad"),
    )
    return jax.shard_map(
        functools.partial(per_device, mesh.shape["ep"], mesh.shape["ad"]),
        mesh=mesh,
        in_specs=placed,
        out_specs=P(("rep", "ep"), "ad"),
        check_vma=False,
    )
```

```python
import functools

import jax
import jax.numpy as jnp
from jax import lax
from jax.experimental import pallas as pl
from jax.experimental.pallas import tpu as pltpu
from jax.sharding import PartitionSpec as P

EXPERT_COUNT = 8
TOP = 2
RANK = 16
CAP = 48
PIECES = 4
LIMIT = 16
LIMIT_EARLY = 8
N_TILE = 512
MIB = 1 << 20

F32 = jnp.float32
BF16 = jnp.bfloat16


def mm(a, b):
    return jnp.dot(a, b, preferred_element_type=F32)


def mm_nt(a, b):
    return lax.dot_general(a, b, (((1,), (1,)), ((), ())), preferred_element_type=F32)


def cost(flops, moved, trans=0):
    return pl.CostEstimate(flops=int(flops), bytes_accessed=int(moved), transcendentals=int(trans))


def params(mib):
    return pltpu.CompilerParams(vmem_limit_bytes=mib * MIB)


def vmem():
    return pl.BlockSpec(memory_space=pltpu.VMEM)


def smem():
    return pl.BlockSpec(memory_space=pltpu.SMEM)


def fact_columns(chosen_experts, logits, tenant):
    pieces, rest = [], logits
    for _ in range(3):
        piece = lax.reduce_precision(rest, 8, 7)
        pieces.append(piece)
        rest = rest - piece
    facts = jnp.concatenate([chosen_experts.astype(F32), tenant.astype(F32)[:, None]] + pieces, axis=1)
    return jnp.pad(facts, ((0, 0), (0, 128 - facts.shape[1]))).astype(BF16)


def meta_kernel(n_local, local_halves, ids_ref, adapter_ref, pool_slot_ref, *refs):
    blocks, (p_ref, pt_ref, cols_ref, rows_ref, tslot_ref) = refs[:-5], refs[-5:]
    at = blocks[0].shape[1] - 128
    facts = jnp.concatenate([block[:, at:] for block in blocks], axis=0).astype(F32).T
    count = facts.shape[1]
    first, second, tenant = facts[0:1], facts[1:2], facts[2:3]
    logit_first = (facts[3:4] + facts[5:6]) + facts[7:8]
    logit_second = (facts[4:5] + facts[6:7]) + facts[8:9]
    weight_first = jax.nn.sigmoid(logit_first - logit_second)
    weight_second = jax.nn.sigmoid(logit_second - logit_first)
    slot = jnp.zeros_like(tenant)
    for number in range(adapter_ref.shape[0]):
        slot = jnp.where(tenant == number, pool_slot_ref[adapter_ref[number]].astype(F32), slot)
    members, weights = [], []
    for i in range(n_local):
        expert = (ids_ref[0] * local_halves // 2 + i).astype(F32)
        hit_first, hit_second = first == expert, second == expert
        members.append(jnp.where(hit_first | hit_second, 1.0, 0.0))
        weights.append(jnp.where(hit_first, weight_first, 0.0) + jnp.where(hit_second, weight_second, 0.0))
    member = jnp.concatenate(members + [jnp.zeros((8 - n_local, count), F32)], axis=0)
    before = (
        lax.broadcasted_iota(jnp.int32, (count, count), 0) < lax.broadcasted_iota(jnp.int32, (count, count), 1)
    ).astype(BF16)
    place = jnp.where(member > 0, mm(member.astype(BF16), before), -1.0)
    table = jnp.concatenate(
        [place[0:n_local]] + weights + [slot] + [jnp.zeros((127 - 2 * n_local, count), F32)], axis=0
    )
    columns = table.T
    cols_ref[...] = columns
    rows_ref[...] = table[0:8]
    row_count = p_ref.shape[1]
    tenant_rows = jnp.broadcast_to(tenant, (8, count)).astype(BF16)
    down = lax.broadcasted_iota(jnp.int32, (row_count, count), 0).astype(F32)
    across = lax.broadcasted_iota(jnp.int32, (count, row_count), 1).astype(F32)
    for i in range(n_local):
        picked = (down == place[i : i + 1]).astype(BF16)
        p_ref[i] = picked
        pt_ref[i] = (across == columns[:, i : i + 1]).astype(BF16)
        tslot_ref[i] = mm_nt(tenant_rows, picked)


def build_meta(blocks, ids, adapters, pool_slots, n_local, local_halves, row_count):
    count = sum(block.shape[0] for block in blocks)
    return pl.pallas_call(
        functools.partial(meta_kernel, n_local, local_halves),
        out_shape=(
            jax.ShapeDtypeStruct((n_local, row_count, count), BF16),
            jax.ShapeDtypeStruct((n_local, count, row_count), BF16),
            jax.ShapeDtypeStruct((count, 128), F32),
            jax.ShapeDtypeStruct((8, count), F32),
            jax.ShapeDtypeStruct((n_local, 8, row_count), F32),
        ),
        in_specs=[smem()] * 3 + [vmem()] * len(blocks),
        out_specs=(vmem(),) * 5,
        compiler_params=params(max(LIMIT_EARLY, 12 * count * count // MIB)),
        cost_estimate=cost(2 * 8 * count * count, 4 * n_local * row_count * count),
        name="routing_tables",
    )(ids, adapters, pool_slots, *blocks)


def slab_copies(gate_ref, up_ref, into_ref, sems, part, half):
    depth, width = into_ref.shape[1], into_ref.shape[2]
    copies = []
    for number in range(into_ref.shape[0]):
        source = (gate_ref, up_ref)[number % 2].at[half, pl.ds(part * depth, depth), pl.ds(number // 2 * width, width)]
        copies.append(pltpu.make_async_copy(source, into_ref.at[number], sems.at[half, number]))
    return copies


def prefetch_kernel(ids_ref, gate_ref, up_ref, *refs):
    slabs, mark_ref, sems = refs[:-2], refs[-2], refs[-1]
    copies = [copy for half, slab in enumerate(slabs) for copy in slab_copies(gate_ref, up_ref, slab, sems, 0, half)]
    for copy in copies:
        copy.start()
    mark_ref[...] = jnp.zeros_like(mark_ref)
    for copy in copies:
        copy.wait()


def prefetch(ids, gate, up, part_width):
    local_halves, _, hidden_count = gate.shape
    tile = min(N_TILE, hidden_count)
    each = 2 * hidden_count // tile
    return pl.pallas_call(
        prefetch_kernel,
        out_shape=(pltpu.VMEM((each, part_width, tile), BF16),) * local_halves + (jax.ShapeDtypeStruct((8, 128), F32),),
        in_specs=[smem()] + [pl.BlockSpec(memory_space=pltpu.HBM)] * 2,
        out_specs=(vmem(),) * (local_halves + 1),
        scratch_shapes=[pltpu.SemaphoreType.DMA((local_halves, each))],
        compiler_params=params(LIMIT_EARLY),
        cost_estimate=cost(0, 4 * local_halves * part_width * hidden_count * 2),
        name="weight_prefetch",
    )(ids, gate, up)


def pack(blocks, p_ref, packed):
    depth = packed.shape[2]
    whole = jnp.concatenate([block[:, :depth] for block in blocks], axis=0)
    for i in range(p_ref.shape[0]):
        packed[i] = mm(p_ref[i], whole).astype(BF16)


def first_kernel(n_blocks, local_halves, *refs):
    blocks, refs = refs[:n_blocks], refs[n_blocks:]
    _, p_ref, gate_ref, up_ref, refs = refs[0], refs[1], refs[2], refs[3], refs[4:]
    slabs, refs = refs[:local_halves], refs[local_halves:]
    ahead, (gate_out, up_out, packed, sems) = refs[:-4], refs[-4:]
    pack(blocks, p_ref, packed)
    slabs = list(ahead) + list(slabs[len(ahead) :])
    copies = [slab_copies(gate_ref, up_ref, slab, sems, 1, half) for half, slab in enumerate(ahead)]
    halves_each = local_halves // p_ref.shape[0]
    for half in range(local_halves):
        rows = packed[half // halves_each]
        tiles, _, width = slabs[half].shape
        for tile in range(tiles // 2):
            span = slice(tile * width, (tile + 1) * width)
            gate_out[half, :, span] = mm(rows, slabs[half][2 * tile])
            up_out[half, :, span] = mm(rows, slabs[half][2 * tile + 1])
            if half < len(ahead):
                copies[half][2 * tile].start()
                copies[half][2 * tile + 1].start()
    for copy in [copy for half in copies for copy in half]:
        copy.wait()


def first_part(blocks, mark, picked, gate, up, slabs):
    local_halves, _, hidden_count = gate.shape
    n_local, row_count, _ = picked.shape
    each, part_width, _ = slabs[0].shape
    hbm = pl.BlockSpec(memory_space=pltpu.HBM)
    sums = pltpu.VMEM((local_halves, row_count, hidden_count), F32)
    n_ahead = max(1, local_halves // 2)
    return pl.pallas_call(
        functools.partial(first_kernel, len(blocks), local_halves),
        out_shape=(pltpu.VMEM(slabs[0].shape, BF16),) * n_ahead + (sums, sums),
        in_specs=[vmem()] * (len(blocks) + 2) + [hbm, hbm] + [vmem()] * local_halves,
        out_specs=(vmem(),) * (n_ahead + 2),
        scratch_shapes=[
            pltpu.VMEM((n_local, row_count, part_width), BF16),
            pltpu.SemaphoreType.DMA((n_ahead, each)),
        ],
        input_output_aliases={len(blocks) + 4 + half: half for half in range(n_ahead)},
        compiler_params=params(max(LIMIT_EARLY, 10 * n_local * row_count * part_width // MIB)),
        cost_estimate=cost(
            4 * local_halves * row_count * part_width * hidden_count, 2 * local_halves * part_width * hidden_count
        ),
        name="gate_up_first",
    )(*blocks, mark, picked, gate, up, *[pltpu.with_memory_space_constraint(x, pltpu.VMEM) for x in slabs])


def second_kernel(n_blocks, n_ahead, n_ad, *refs):
    blocks, refs = refs[:n_blocks], refs[n_blocks:]
    p_ref, gate_ref, up_ref, refs = refs[0], refs[1], refs[2], refs[3:]
    ahead, gate_in, up_in, refs = refs[:n_ahead], refs[n_ahead], refs[n_ahead + 1], refs[n_ahead + 2 :]
    ids_ref, adapter_ref, pool_slot_ref, pool_ref, tslot_ref, rows_ref, down_ref, refs = *refs[:7], refs[7:]
    hidden_ref, low_ref, next_ref, packed, factors, factor_sems, down_sems, refs = *refs[:7], refs[7:]
    late, sems = refs
    n_local = p_ref.shape[0]
    local_halves, _, hidden_count = gate_ref.shape
    halves_each = local_halves // n_local
    slabs = list(ahead) + [late] * (local_halves - n_ahead)
    copies = {
        half: slab_copies(gate_ref, up_ref, slabs[half], sems, 1, half) for half in range(n_ahead, local_halves)
    }
    tenants, rank = adapter_ref.shape[0], pool_ref.shape[2]
    factor_copies = [
        pltpu.make_async_copy(
            pool_ref.at[pool_slot_ref[adapter_ref[number]]],
            factors.at[:, number * rank : (number + 1) * rank],
            factor_sems.at[number],
        )
        for number in range(tenants)
    ]
    down_copies = down_fetch(n_ad, 1, ids_ref, down_ref, next_ref, down_sems)
    for copy in copies.get(n_ahead, []) + factor_copies + down_copies:
        copy.start()
    pack(blocks, p_ref, packed)
    for half in range(local_halves):
        rows = packed[half // halves_each]
        tiles, _, width = slabs[half].shape
        for tile in range(tiles // 2):
            span = slice(tile * width, (tile + 1) * width)
            values = []
            for number in (2 * tile, 2 * tile + 1):
                if half in copies:
                    copies[half][number].wait()
                values.append(mm(rows, slabs[half][number]))
                if half in copies and half + 1 in copies:
                    copies[half + 1][number].start()
            gate = values[0] + gate_in[half, :, span]
            up = values[1] + up_in[half, :, span]
            hidden_ref[half, :, span] = (jax.nn.silu(gate) * up).astype(BF16)
    for copy in factor_copies:
        copy.wait()
    for i in range(n_local):
        low = mm_nt(factors[i * halves_each], hidden_ref[i * halves_each])
        for half in range(i * halves_each + 1, (i + 1) * halves_each):
            low = low + mm_nt(factors[half], hidden_ref[half])
        owner = tslot_ref[i][0:1]
        total = jnp.zeros((rank, low.shape[1]), F32)
        for number in range(tenants):
            total = total + jnp.where(owner == number, low[number * rank : (number + 1) * rank], 0.0)
        weight = rows_ref[n_local + i : n_local + i + 1]
        low_ref[i * rank : (i + 1) * rank] = (mm(total.astype(BF16), p_ref[i]) * weight).astype(BF16)
    for copy in down_copies:
        copy.wait()


def second_part(blocks, picked, gate, up, ahead, sums, ids, adapters, pool_slots, pool, tslot, table_rows, down, n_ad):
    local_halves, _, hidden_count = gate.shape
    n_local, row_count, count = picked.shape
    each, part_width, tile = ahead[0].shape
    tenants, rank = adapters.shape[0], pool.shape[2]
    span = down.shape[2] // n_ad
    hbm = pl.BlockSpec(memory_space=pltpu.HBM)
    held = [pltpu.with_memory_space_constraint(x, pltpu.VMEM) for x in (*ahead, *sums)]
    late_bytes = 2 * each * part_width * tile
    return pl.pallas_call(
        functools.partial(second_kernel, len(blocks), len(ahead), n_ad),
        out_shape=(
            pltpu.VMEM((local_halves, row_count, hidden_count), BF16),
            jax.ShapeDtypeStruct((n_local * rank, count), BF16),
            pltpu.VMEM((local_halves, hidden_count, span), BF16),
        ),
        in_specs=[vmem()] * (len(blocks) + 1) + [hbm, hbm] + [vmem()] * len(held) + [smem()] * 3 + [hbm, vmem(), vmem(), hbm],
        out_specs=(vmem(),) * 3,
        scratch_shapes=[
            pltpu.VMEM((n_local, row_count, part_width), BF16),
            pltpu.VMEM((local_halves, tenants * rank, hidden_count), BF16),
            pltpu.SemaphoreType.DMA((tenants,)),
            pltpu.SemaphoreType.DMA((local_halves * PIECES,)),
            pltpu.VMEM((each, part_width, tile), BF16),
            pltpu.SemaphoreType.DMA((local_halves, each)),
        ],
        compiler_params=params(
            max(LIMIT_EARLY, 10 * n_local * row_count * part_width // MIB) + late_bytes // MIB + 1
        ),
        cost_estimate=cost(
            4 * local_halves * row_count * part_width * hidden_count, 4 * local_halves * part_width * hidden_count
        ),
        name="gate_up_second",
    )(*blocks, picked, gate, up, *held, ids, adapters, pool_slots, pool, tslot, table_rows, down)


def down_fetch(n_ad, step, ids_ref, down_ref, next_ref, sems):
    span = next_ref.shape[2]
    rows = next_ref.shape[1] // PIECES
    start = pl.multiple_of(lax.rem(ids_ref[1] + step, n_ad) * span, span)
    return [
        pltpu.make_async_copy(
            down_ref.at[half, pl.ds(piece * rows, rows), pl.ds(start, span)],
            next_ref.at[half, pl.ds(piece * rows, rows)],
            sems.at[half * PIECES + piece],
        )
        for half in range(down_ref.shape[0])
        for piece in range(PIECES)
    ]


def weighted_down(hidden_ref, weight_ref, pt_ref, cols_ref):
    n_local = pt_ref.shape[0]
    halves_each = hidden_ref.shape[0] // n_local
    total = None
    for i in range(n_local):
        part_sum = mm(hidden_ref[i * halves_each], weight_ref[i * halves_each])
        for half in range(i * halves_each + 1, (i + 1) * halves_each):
            part_sum = part_sum + mm(hidden_ref[half], weight_ref[half])
        laid = mm(pt_ref[i], part_sum.astype(BF16)) * cols_ref[:, n_local + i : n_local + i + 1]
        total = laid if total is None else total + laid
    return total


def down_kernel(n_ad, step, ids_ref, hidden_ref, weight_ref, down_ref, pt_ref, cols_ref, keep, send, next_ref, sems):
    copies = down_fetch(n_ad, step + 1, ids_ref, down_ref, next_ref, sems)
    for copy in copies:
        copy.start()
    write_pairs(weighted_down(hidden_ref, weight_ref, pt_ref, cols_ref), (keep, send))
    for copy in copies:
        copy.wait()


def down_part(n_ad, step, ids, hidden, weights, down, pt, cols):
    local_halves, row_count, hidden_count = hidden.shape
    count, span = pt.shape[1], weights.shape[2]
    weights = pltpu.with_memory_space_constraint(weights, pltpu.VMEM)
    return pl.pallas_call(
        functools.partial(down_kernel, n_ad, step),
        out_shape=(jax.ShapeDtypeStruct((count // 2, span), BF16),) * 2 + (pltpu.VMEM(weights.shape, BF16),),
        in_specs=[smem(), vmem(), vmem(), pl.BlockSpec(memory_space=pltpu.HBM), vmem(), vmem()],
        out_specs=(vmem(),) * 3,
        scratch_shapes=[pltpu.SemaphoreType.DMA((local_halves * PIECES,))],
        compiler_params=params(max(LIMIT, 12 * count * span // MIB)),
        cost_estimate=cost(
            2 * local_halves * row_count * hidden_count * span, 2 * local_halves * hidden_count * span
        ),
        name="down_part",
    )(ids, hidden, weights, down, pt, cols)


def write_pairs(total, outs):
    keep, send = outs
    for b in range(total.shape[0] // 128):
        (send if b % 2 else keep)[b // 2 * 128 : b // 2 * 128 + 128] = total[b * 128 : b * 128 + 128].astype(BF16)


def final_kernel(local_halves, slot_column, ids_ref, hidden_ref, weight_ref, pt_ref, cols_ref, factor_ref, low_ref, *refs):
    keep, send, wide = refs
    count = pt_ref.shape[1]
    blocks = count // 128
    height = low_ref.shape[0] // blocks
    wide[...] = jnp.zeros_like(wide)
    for m in range(blocks):
        start = pl.multiple_of(((ids_ref[0] ^ m) * local_halves // 2) * RANK, RANK)
        value = low_ref[m * height : (m + 1) * height].astype(F32)
        value = jnp.concatenate([value[:, (m ^ b) * 128 : (m ^ b) * 128 + 128] for b in range(blocks)], axis=1)
        wide[pl.ds(start, height)] += value
    low = wide[...].T.astype(BF16)
    zero = jnp.zeros_like(low)
    slot = cols_ref[:, slot_column : slot_column + 1]
    depth = EXPERT_COUNT * RANK
    slot_count = factor_ref.shape[0] // depth
    total = weighted_down(hidden_ref, weight_ref, pt_ref, cols_ref)
    for j in range(0, slot_count, 2):
        spread = jnp.concatenate(
            [jnp.where(slot == (ids_ref[0] * slot_count + j + i).astype(F32), low, zero) for i in range(2)], axis=1
        )
        total = total + mm(spread, factor_ref[j * depth : (j + 2) * depth])
    write_pairs(total, (keep, send))


def final_part(ids, hidden, weights, pt, cols, slot_column, factors, lows):
    local_halves, row_count, hidden_count = hidden.shape
    count, span = pt.shape[1], weights.shape[2]
    weights = pltpu.with_memory_space_constraint(weights, pltpu.VMEM)
    return pl.pallas_call(
        functools.partial(final_kernel, local_halves, slot_column),
        out_shape=(jax.ShapeDtypeStruct((count // 2, span), BF16),) * 2,
        in_specs=[smem()] + [vmem()] * 6,
        out_specs=(vmem(),) * 2,
        scratch_shapes=[pltpu.VMEM((EXPERT_COUNT * RANK, count), F32)],
        compiler_params=params(max(LIMIT, 24 * count * span // MIB)),
        cost_estimate=cost(
            2 * (count * factors.shape[0] + local_halves * row_count * hidden_count) * span,
            2 * (factors.shape[0] + local_halves * hidden_count) * span,
        ),
        name="down_and_adapters",
    )(ids, hidden, weights, pt, cols, factors, lows)


def per_device(
    n_ep,
    n_ad,
    tokens,
    chosen_experts,
    router_gate_logits,
    token_tenant,
    adapter_of_tenant,
    adapter_pool_slot,
    gate_weight,
    up_weight,
    down_weight,
    adapter_input_factors,
    adapter_output_factors,
):
    gate_weight, up_weight, down_weight, adapter_input_factors = [
        pltpu.with_memory_space_constraint(x, pltpu.HBM)
        for x in (gate_weight, up_weight, down_weight, adapter_input_factors)
    ]
    width = tokens.shape[1]
    span = width // n_ad
    local_halves = gate_weight.shape[0]
    n_local = max(1, local_halves // 2)
    row_count = n_ep * CAP
    bits = n_ep.bit_length() - 1
    ids = jnp.stack([lax.axis_index("ep"), lax.axis_index("ad")]).astype(jnp.int32)

    def swap(x, mask):
        return lax.ppermute(x, "ep", [(i, i ^ mask) for i in range(n_ep)])

    def shift(x, step):
        return lax.ppermute(x, "ad", [(i, (i + step) % n_ad) for i in range(n_ad)])

    parts = 2
    part_width = width // parts
    *slabs, mark = prefetch(ids, gate_weight, up_weight, part_width)
    facts = fact_columns(chosen_experts, router_gate_logits, token_tenant)
    token_parts = []
    for part in range(parts):
        own = tokens[:, part * part_width : (part + 1) * part_width]
        blocks = {0: jnp.concatenate([own, facts], axis=1) if part == 0 else own}
        for bit in reversed(range(bits)):
            for mask in list(blocks):
                blocks[mask | 1 << bit] = swap(blocks[mask], 1 << bit)
            if bit == bits - 1:
                high = 1 << bit
                blocks[high], mark = lax.optimization_barrier((blocks[high], mark))
        token_parts.append([blocks[mask] for mask in range(n_ep)])

    picked, pt, cols, table_rows, tslot = build_meta(
        token_parts[0], ids, adapter_of_tenant, adapter_pool_slot, n_local, local_halves, row_count
    )
    *ahead, gate_sum, up_sum = first_part(token_parts[0], mark, picked, gate_weight, up_weight, slabs)
    hidden, low, weights = second_part(
        token_parts[1], picked, gate_weight, up_weight, ahead, (gate_sum, up_sum), ids, adapter_of_tenant, adapter_pool_slot,
        adapter_input_factors, tslot, table_rows, down_weight, n_ad,
    )

    def low_sum(low):
        for bit in range(n_ad.bit_length() - 1):
            other = lax.ppermute(low, "ad", [(i, i ^ 1 << bit) for i in range(n_ad)])
            low = (low.astype(F32) + other.astype(F32)).astype(BF16)
        for bit in range(bits):
            low = jnp.concatenate([low, swap(low, 1 << bit)], axis=0)
        return low

    def between(keep, send):
        return (keep.astype(F32) + swap(send, 1).astype(F32)).astype(BF16)

    def across(mine):
        for bit in range(1, bits):
            half = mine.shape[0] // 128 // 2
            grouped = mine.reshape(half, 2, 128, mine.shape[1])
            keep = grouped[:, 0].reshape(half * 128, -1)
            send = grouped[:, 1].reshape(half * 128, -1)
            mine = (keep.astype(F32) + swap(send, 1 << bit).astype(F32)).astype(BF16)
        return mine

    slot_count = adapter_output_factors.shape[0]
    flat_factors = adapter_output_factors.reshape(slot_count * EXPERT_COUNT * RANK, span)
    mines, crossed, results = [], [], []
    for step in range(1, n_ad + 1):
        if step > 2:
            mines[step - 3], hidden = lax.optimization_barrier((mines[step - 3], hidden))
            crossed.append(across(mines[step - 3]))
        if step < n_ad:
            keep, send, weights = down_part(n_ad, step, ids, hidden, weights, down_weight, pt, cols)
        else:
            keep, send = final_part(ids, hidden, weights, pt, cols, 2 * n_local, flat_factors, low_sum(low))
        if step > 2:
            crossed[-1], keep = lax.optimization_barrier((crossed[-1], keep))
            results.append(shift(crossed[-1], step - 2))
        mines.append(between(keep, send))
    for step in range(n_ad - 2, n_ad):
        results.append(across(mines[step]))
        if step < n_ad - 1:
            results[-1] = shift(results[-1], step + 1)
    return sum(x.astype(F32) for x in results).astype(BF16)


def solution(mesh):
    placed = (
        P(("rep", "ep"), None),
        P(("rep", "ep"), None),
        P(("rep", "ep"), None),
        P(("rep", "ep")),
        P("rep"),
        P(),
        P("ep", None, "ad"),
        P("ep", None, "ad"),
        P("ep", "ad", None),
        P(None, "ep", None, "ad"),
        P("ep", None, None, "ad"),
    )
    return jax.shard_map(
        functools.partial(per_device, mesh.shape["ep"], mesh.shape["ad"]),
        mesh=mesh,
        in_specs=placed,
        out_specs=P(("rep", "ep"), "ad"),
        check_vma=False,
    )
```

```python
import functools
import math

import jax
import jax.numpy as jnp
from jax import lax
from jax.experimental import pallas as pl
from jax.experimental.pallas import tpu as pltpu
from jax.sharding import PartitionSpec as P

EXPERT_COUNT = 8
TOP = 2
RANK = 16
CAP = 48
LIMIT = 16
LIMIT_EARLY = 24
N_TILE = 512
HELD_EACH = 2
HELD_ARRAYS = 4
RING = 4
MIB = 1 << 20

F32 = jnp.float32
BF16 = jnp.bfloat16


def mm(a, b):
    return jnp.dot(a, b, preferred_element_type=F32)


def mm_nt(a, b):
    return lax.dot_general(a, b, (((1,), (1,)), ((), ())), preferred_element_type=F32)


SMALL = pl.CostEstimate(flops=1, bytes_accessed=1, transcendentals=0)


def params(mib):
    return pltpu.CompilerParams(vmem_limit_bytes=mib * MIB)


def vmem():
    return pl.BlockSpec(memory_space=pltpu.VMEM)


def smem():
    return pl.BlockSpec(memory_space=pltpu.SMEM)


def facts_kernel(tokens_ref, chosen_ref, logits_ref, tenant_ref, out_ref, sem):
    rows, width = tokens_ref.shape
    copy = pltpu.make_async_copy(tokens_ref, out_ref.at[:, pl.ds(0, width)], sem)
    copy.start()
    diagonal = lax.broadcasted_iota(jnp.int32, (rows, rows), 0) == lax.broadcasted_iota(jnp.int32, (rows, rows), 1)
    tenant = jnp.sum(jnp.where(diagonal, tenant_ref[...].astype(F32), 0.0), axis=1, keepdims=True)
    chosen = chosen_ref[...].astype(F32)
    columns, rest = [chosen[:, 0:1], chosen[:, 1:2], tenant], logits_ref[...]
    for _ in range(3):
        piece = rest.astype(BF16).astype(F32)
        columns += [piece[:, 0:1], piece[:, 1:2]]
        rest = rest - piece
    lane = lax.broadcasted_iota(jnp.int32, (rows, 128), 1)
    facts = jnp.zeros((rows, 128), F32)
    for number, column in enumerate(columns):
        facts = jnp.where(lane == number, column, facts)
    out_ref[:, width:] = facts.astype(BF16)
    copy.wait()


def with_facts(tokens, chosen_experts, logits, tenant):
    rows, width = tokens.shape
    return pl.pallas_call(
        facts_kernel,
        out_shape=jax.ShapeDtypeStruct((rows, width + 128), BF16),
        in_specs=[pl.BlockSpec(memory_space=pltpu.HBM)] + [vmem()] * 3,
        out_specs=vmem(),
        scratch_shapes=[pltpu.SemaphoreType.DMA],
        cost_estimate=SMALL,
        compiler_params=params(LIMIT_EARLY),
        name="tokens_with_facts",
    )(pltpu.with_memory_space_constraint(tokens, pltpu.HBM), chosen_experts, logits, tenant.reshape(1, rows))


def meta_kernel(n_local, local_halves, ids_ref, adapter_ref, pool_slot_ref, *refs):
    blocks, (p_ref, pt_ref, cols_ref, rows_ref, tslot_ref) = refs[:-5], refs[-5:]
    at = blocks[0].shape[1] - 128
    facts = jnp.concatenate([block[:, at:] for block in blocks], axis=0).astype(F32).T
    count = facts.shape[1]
    first, second, tenant = facts[0:1], facts[1:2], facts[2:3]
    logit_first = (facts[3:4] + facts[5:6]) + facts[7:8]
    logit_second = (facts[4:5] + facts[6:7]) + facts[8:9]
    weight_first = jax.nn.sigmoid(logit_first - logit_second)
    weight_second = jax.nn.sigmoid(logit_second - logit_first)
    slot = jnp.zeros_like(tenant)
    for number in range(adapter_ref.shape[0]):
        slot = jnp.where(tenant == number, pool_slot_ref[adapter_ref[number]].astype(F32), slot)
    members, weights = [], []
    for i in range(n_local):
        expert = (ids_ref[0] * local_halves // 2 + i).astype(F32)
        hit_first, hit_second = first == expert, second == expert
        members.append(jnp.where(hit_first | hit_second, 1.0, 0.0))
        weights.append(jnp.where(hit_first, weight_first, 0.0) + jnp.where(hit_second, weight_second, 0.0))
    member = jnp.concatenate(members + [jnp.zeros((8 - n_local, count), F32)], axis=0)
    before = (
        lax.broadcasted_iota(jnp.int32, (count, count), 0) < lax.broadcasted_iota(jnp.int32, (count, count), 1)
    ).astype(BF16)
    place = jnp.where(member > 0, mm(member.astype(BF16), before), -1.0)
    table = jnp.concatenate(
        [place[0:n_local]] + weights + [slot] + [jnp.zeros((127 - 2 * n_local, count), F32)], axis=0
    )
    columns = table.T
    cols_ref[...] = columns
    rows_ref[...] = table[0:8]
    row_count = p_ref.shape[1]
    tenant_rows = jnp.broadcast_to(tenant, (8, count)).astype(BF16)
    down = lax.broadcasted_iota(jnp.int32, (row_count, count), 0).astype(F32)
    across = lax.broadcasted_iota(jnp.int32, (count, row_count), 1).astype(F32)
    for i in range(n_local):
        picked = (down == place[i : i + 1]).astype(BF16)
        p_ref[i] = picked
        pt_ref[i] = (across == columns[:, i : i + 1]).astype(BF16)
        tslot_ref[i] = mm_nt(tenant_rows, picked)


def build_meta(blocks, ids, adapters, pool_slots, n_local, local_halves, row_count):
    count = sum(block.shape[0] for block in blocks)
    return pl.pallas_call(
        functools.partial(meta_kernel, n_local, local_halves),
        out_shape=(
            jax.ShapeDtypeStruct((n_local, row_count, count), BF16),
            jax.ShapeDtypeStruct((n_local, count, row_count), BF16),
            jax.ShapeDtypeStruct((count, 128), F32),
            jax.ShapeDtypeStruct((8, count), F32),
            jax.ShapeDtypeStruct((n_local, 8, row_count), F32),
        ),
        in_specs=[smem()] * 3 + [vmem()] * len(blocks),
        out_specs=(vmem(),) * 5,
        cost_estimate=SMALL,
        compiler_params=params(min(38, LIMIT_EARLY * count // 512)),
        name="routing_tables",
    )(ids, adapters, pool_slots, *blocks)


class Slabs:
    def __init__(self, gate_ref, up_ref, down_ref, resident, ring, sems):
        self.sources, self.down, self.resident, self.ring, self.sems = (gate_ref, up_ref), down_ref, resident, ring, sems
        self.halves, self.depth, self.hidden = gate_ref.shape
        self.width = resident[0].shape[2]
        self.each = resident[0].shape[0]
        self.first = len(resident) * self.each
        self.capacity = 1 if ring is None else ring.shape[0]
        self.tiles = self.hidden // self.width
        self.early = 2 * self.halves * self.tiles
        self.held = self.depth // self.hidden
        self.columns = down_ref.shape[2] // self.width
        self.count = self.early + -(-self.columns * self.halves // self.held)

    def place(self, number):
        if number < self.first:
            return self.resident[number // self.each].at[number % self.each]
        return self.ring.at[(number - self.first) % self.capacity]

    def copies(self, number):
        place = self.place(number)
        slot = number if number < self.first else (number - self.first) % self.capacity
        if number < self.early:
            half, tile, which = number // (2 * self.tiles), number // 2 % self.tiles, number % 2
            source = self.sources[which].at[half, :, pl.ds(tile * self.width, self.width)]
            return [pltpu.make_async_copy(source, place, self.sems.at[slot, 0])]
        made = []
        for i in range(self.held):
            piece = (number - self.early) * self.held + i
            if piece < self.columns * self.halves:
                source = self.down.at[piece % self.halves, :, pl.ds(piece // self.halves * self.width, self.width)]
                into = place.at[pl.ds(i * self.hidden, self.hidden)]
                made.append(pltpu.make_async_copy(source, into, self.sems.at[slot, i]))
        return made

    def start(self, number):
        for copy in self.copies(number):
            copy.start()

    def wait(self, number):
        for copy in self.copies(number):
            copy.wait()

    def down_piece(self, column, half):
        piece = column * self.halves + half
        return self.early + piece // self.held, piece % self.held


def resident_shapes(gate, down):
    local_halves, width, hidden_count = gate.shape
    tile = min(N_TILE, hidden_count)
    pieces = local_halves * down.shape[2] // tile
    count = 2 * local_halves * hidden_count // tile + -(-pieces * hidden_count // width)
    each = min(HELD_EACH, count)
    return [(each, width, tile)] * min(HELD_ARRAYS, count // each)


def ring_size(gate, down, resident):
    pieces = gate.shape[0] * down.shape[2] // resident[0].shape[2]
    count = 2 * gate.shape[0] * gate.shape[2] // resident[0].shape[2] + -(-pieces * gate.shape[2] // gate.shape[1])
    return max(1, min(RING, count - len(resident) * resident[0].shape[0]))


def semaphores(gate, slots):
    return pltpu.SemaphoreType.DMA((slots, max(1, gate.shape[1] // gate.shape[2])))


def prefetch_kernel(ids_ref, gate_ref, up_ref, down_ref, *refs):
    resident, mark_ref, sems = refs[:-2], refs[-2], refs[-1]
    slabs = Slabs(gate_ref, up_ref, down_ref, resident, None, sems)
    for number in range(slabs.first):
        slabs.start(number)
    mark_ref[...] = jnp.zeros_like(mark_ref)
    for number in range(slabs.first):
        slabs.wait(number)


def prefetch(ids, gate, up, down, count):
    shapes = resident_shapes(gate, down)
    return pl.pallas_call(
        prefetch_kernel,
        out_shape=(*[pltpu.VMEM(shape, BF16) for shape in shapes], jax.ShapeDtypeStruct((8, 128), F32)),
        in_specs=[smem()] + [pl.BlockSpec(memory_space=pltpu.HBM)] * 3,
        out_specs=(vmem(),) * (len(shapes) + 1),
        scratch_shapes=[semaphores(gate, len(shapes) * shapes[0][0])],
        cost_estimate=SMALL,
        compiler_params=params(min(38, LIMIT_EARLY * count // 512)),
        name="weight_prefetch",
    )(ids, gate, up, down)


def expert_kernel(n_blocks, n_resident, n_ad, order, *refs):
    blocks, refs = refs[:n_blocks], refs[n_blocks:]
    ids_ref, adapter_ref, pool_slot_ref, p_ref, pt_ref, cols_ref, tslot_ref, rows_ref = refs[1:9]
    gate_ref, up_ref, down_ref, pool_ref = refs[9:13]
    resident, refs = refs[13 : 13 + n_resident], refs[13 + n_resident :]
    keep, send, base, packed, hidden, factors, factor_sems, ring, sems = refs
    slabs = Slabs(gate_ref, up_ref, down_ref, resident, ring, sems)
    n_local = p_ref.shape[0]
    local_halves, depth, _ = gate_ref.shape
    halves_each = local_halves // n_local
    tenants, rank = adapter_ref.shape[0], pool_ref.shape[2]
    factor_copies = [
        pltpu.make_async_copy(
            pool_ref.at[pool_slot_ref[adapter_ref[number]]],
            factors.at[:, number * rank : (number + 1) * rank],
            factor_sems.at[number],
        )
        for number in range(tenants)
    ]
    for copy in factor_copies:
        copy.start()
    for number in range(slabs.first, min(slabs.count, slabs.first + slabs.capacity)):
        slabs.start(number)

    def ready(number):
        if number >= slabs.first:
            slabs.wait(number)

    def used(number):
        if slabs.first <= number < slabs.count - slabs.capacity:
            slabs.start(number + slabs.capacity)

    whole = jnp.concatenate([block[:, :depth] for block in blocks], axis=0)
    for i in range(n_local):
        packed[i] = mm(p_ref[i], whole).astype(BF16)
    for half in range(local_halves):
        rows = packed[half // halves_each]
        for tile in range(slabs.tiles):
            values = []
            for which in range(2):
                number = (half * slabs.tiles + tile) * 2 + which
                ready(number)
                values.append(mm(rows, slabs.place(number)[...]))
                used(number)
            span = slice(tile * slabs.width, (tile + 1) * slabs.width)
            hidden[half, :, span] = (jax.nn.silu(values[0]) * values[1]).astype(BF16)
    span = base.shape[1]
    at = span * len(order)
    for copy in factor_copies:
        copy.wait()
    for out in (keep, send):
        out[:, at:] = jnp.zeros((out.shape[0], 256), BF16)
    for i in range(n_local):
        low = mm_nt(factors[i * halves_each], hidden[i * halves_each])
        for half in range(i * halves_each + 1, (i + 1) * halves_each):
            low = low + mm_nt(factors[half], hidden[half])
        owner = tslot_ref[i][0:1]
        total = jnp.zeros((rank, low.shape[1]), F32)
        for number in range(tenants):
            total = total + jnp.where(owner == number, low[number * rank : (number + 1) * rank], 0.0)
        weight = rows_ref[n_local + i : n_local + i + 1]
        value = (mm(total.astype(BF16), p_ref[i]) * weight).astype(BF16)
        row = pl.multiple_of((ids_ref[0] * local_halves // 2 + i) * rank, rank)
        for place, out in enumerate((keep, send)):
            for b in range(value.shape[1] // 128):
                lane = at + (b % 2 ^ place) * 128
                out[pl.ds(b // 2 * 128 + row, rank), lane : lane + 128] = value[:, b * 128 : b * 128 + 128]
    part = math.gcd(span, slabs.width)
    for column in range(slabs.columns):
        total = None
        for i in range(n_local):
            part_sum = None
            for half in range(i * halves_each, (i + 1) * halves_each):
                number, piece = slabs.down_piece(column, half)
                if piece == 0:
                    ready(number)
                value = mm(hidden[half], slabs.place(number)[piece * slabs.hidden : (piece + 1) * slabs.hidden])
                if piece == slabs.held - 1:
                    used(number)
                part_sum = value if part_sum is None else part_sum + value
            laid = mm(pt_ref[i], part_sum.astype(BF16)) * cols_ref[:, n_local + i : n_local + i + 1]
            total = laid if total is None else total + laid
        for first in range(0, slabs.width, part):
            feature = column * slabs.width + first
            owner, inside = feature // span, feature % span
            step = lax.rem(owner - ids_ref[1] + n_ad, n_ad)
            position = sum(jnp.where(step == s, position, 0) for position, s in enumerate(order))
            value = total[:, first : first + part]

            @pl.when(step == 0)
            def _():
                base[:, inside : inside + part] = value

            @pl.when(step != 0)
            def _():
                write_pairs(value, (keep, send), pl.multiple_of(position * span + inside, 128))


def expert_part(
    blocks, mark, ids, adapters, pool_slots, picked, pt, cols, tslot, table_rows, gate, up, down, pool, resident, n_ad, order
):
    local_halves, width, hidden_count = gate.shape
    n_local, row_count, count = picked.shape
    tenants, rank = adapters.shape[0], pool.shape[2]
    span = down.shape[2] // n_ad
    hbm = pl.BlockSpec(memory_space=pltpu.HBM)
    ring = ring_size(gate, down, resident)
    outs = [pltpu.VMEM((count // 2, span * len(order) + 256), BF16)] * 2
    outs.append(pltpu.VMEM((count, span), F32))
    return pl.pallas_call(
        functools.partial(expert_kernel, len(blocks), len(resident), n_ad, order),
        out_shape=tuple(outs),
        in_specs=[vmem()] * (len(blocks) + 1) + [smem()] * 3 + [vmem()] * 5 + [hbm] * 4 + [vmem()] * len(resident),
        out_specs=(vmem(),) * len(outs),
        scratch_shapes=[
            pltpu.VMEM((n_local, row_count, width), BF16),
            pltpu.VMEM((local_halves, row_count, hidden_count), BF16),
            pltpu.VMEM((local_halves, tenants * rank, hidden_count), BF16),
            pltpu.SemaphoreType.DMA((tenants,)),
            pltpu.VMEM((ring, *resident[0].shape[1:]), BF16),
            semaphores(gate, ring),
        ],
        cost_estimate=SMALL,
        compiler_params=params(min(38, LIMIT_EARLY * count // 512)),
        name="experts",
    )(
        *blocks, mark, ids, adapters, pool_slots, picked, pt, cols, tslot, table_rows, gate, up, down, pool,
        *[pltpu.with_memory_space_constraint(x, pltpu.VMEM) for x in resident],
    )


def write_pairs(total, outs, at=0):
    keep, send = outs
    for b in range(total.shape[0] // 128):
        block = total[b * 128 : b * 128 + 128].astype(BF16)
        (send if b % 2 else keep)[b // 2 * 128 : b // 2 * 128 + 128, pl.ds(at, total.shape[1])] = block


def adapter_kernel(slot_column, ids_ref, base_ref, cols_ref, factor_ref, low_ref, keep, send):
    low = low_ref[0].astype(F32)
    for a in range(1, low_ref.shape[0]):
        low = low + low_ref[a].astype(F32)
    low = low.T.astype(BF16)
    zero = jnp.zeros_like(low)
    slot = cols_ref[:, slot_column : slot_column + 1]
    depth = EXPERT_COUNT * RANK
    slot_count = factor_ref.shape[0] // depth
    total = base_ref[...]
    for j in range(0, slot_count, 2):
        spread = jnp.concatenate(
            [jnp.where(slot == (ids_ref[0] * slot_count + j + i).astype(F32), low, zero) for i in range(2)], axis=1
        )
        total = total + mm(spread, factor_ref[j * depth : (j + 2) * depth])
    write_pairs(total, (keep, send))


def adapter_part(ids, base, cols, slot_column, factors, lows):
    count, span = base.shape
    return pl.pallas_call(
        functools.partial(adapter_kernel, slot_column),
        out_shape=(jax.ShapeDtypeStruct((count // 2, span), BF16),) * 2,
        in_specs=[smem()] + [vmem()] * 4,
        out_specs=(vmem(),) * 2,
        cost_estimate=SMALL,
        compiler_params=params(max(LIMIT, 24 * count * span // MIB)),
        name="adapters",
    )(ids, base, cols, factors, lows)


def per_device(
    n_ep,
    n_ad,
    tokens,
    chosen_experts,
    router_gate_logits,
    token_tenant,
    adapter_of_tenant,
    adapter_pool_slot,
    gate_weight,
    up_weight,
    down_weight,
    adapter_input_factors,
    adapter_output_factors,
):
    gate_weight, up_weight, down_weight, adapter_input_factors = [
        pltpu.with_memory_space_constraint(x, pltpu.HBM)
        for x in (gate_weight, up_weight, down_weight, adapter_input_factors)
    ]
    width = tokens.shape[1]
    span = width // n_ad
    local_halves = gate_weight.shape[0]
    n_local = max(1, local_halves // 2)
    row_count = n_ep * CAP
    bits = n_ep.bit_length() - 1
    ids = jnp.stack([lax.axis_index("ep"), lax.axis_index("ad")]).astype(jnp.int32)

    def swap(x, mask):
        return lax.ppermute(x, "ep", [(i, i ^ mask) for i in range(n_ep)])

    def tie(x, y):
        return lax.optimization_barrier((x, y))

    def shift(x, step):
        return lax.ppermute(x, "ad", [(i, (i + step) % n_ad) for i in range(n_ad)])

    order = sorted(range(1, n_ad), key=lambda step: (step != n_ad // 2, step))
    own = with_facts(tokens, chosen_experts, router_gate_logits, token_tenant)
    *resident, mark = prefetch(ids, gate_weight, up_weight, down_weight, n_ep * tokens.shape[0])
    blocks = {0: own}
    for bit in reversed(range(bits)):
        for mask in list(blocks):
            blocks[mask | 1 << bit] = swap(blocks[mask], 1 << bit)
        if bit == bits - 1:
            blocks[1 << bit], mark = tie(blocks[1 << bit], mark)
    blocks = [blocks[mask] for mask in range(n_ep)]
    picked, pt, cols, table_rows, tslot = build_meta(
        blocks, ids, adapter_of_tenant, adapter_pool_slot, n_local, local_halves, row_count
    )
    keep, send, base = expert_part(
        blocks, mark, ids, adapter_of_tenant, adapter_pool_slot, picked, pt, cols, tslot, table_rows, gate_weight,
        up_weight, down_weight, adapter_input_factors, resident, n_ad, order,
    )

    def added(x, y):
        return (x.astype(F32) + y.astype(F32)).astype(BF16)

    def halves(x, fold):
        grouped = x.reshape(x.shape[0] // 256, 2, 128, x.shape[1])
        low, high = (grouped[:, i].reshape(-1, x.shape[1]) for i in range(2))
        if fold:
            return jnp.concatenate([low, high], axis=1), jnp.concatenate([high, low], axis=1)
        return low, high

    def across(mine, low=None):
        for bit in range(1, bits):
            keep, send = halves(mine, False)
            if low is not None:
                parts = halves(low, True)
                keep, send = (jnp.concatenate([x, part], axis=1) for x, part in zip((keep, send), parts))
            mine = added(keep, swap(send, 1 << bit))
            if low is not None:
                mine, low = mine[:, : keep.shape[1] - parts[0].shape[1]], mine[:, keep.shape[1] - parts[0].shape[1] :]
        return mine, low

    mine = added(keep, swap(send, 1))
    at = span * len(order)
    sums, low = across(mine[:, :span], mine[:, at:])
    results = [shift(sums, order[0])]
    rest, _ = across(mine[:, span:at])
    lows = lax.all_to_all(jnp.broadcast_to(low, (n_ad, *low.shape)), "ad", 0, 0, tiled=True)
    slot_count = adapter_output_factors.shape[0]
    flat_factors = adapter_output_factors.reshape(slot_count * EXPERT_COUNT * RANK, span)
    keep, send = adapter_part(ids, base, cols, 2 * n_local, flat_factors, lows)
    results += [shift(rest[:, i * span : (i + 1) * span], step) for i, step in enumerate(order[1:])]
    results.append(across(added(keep, swap(send, 1)))[0])
    return sum(x.astype(F32) for x in results).astype(BF16)


def solution(mesh):
    placed = (
        P(("rep", "ep"), None),
        P(("rep", "ep"), None),
        P(("rep", "ep"), None),
        P(("rep", "ep")),
        P("rep"),
        P(),
        P("ep", None, "ad"),
        P("ep", None, "ad"),
        P("ep", "ad", None),
        P(None, "ep", None, "ad"),
        P("ep", None, None, "ad"),
    )
    return jax.shard_map(
        functools.partial(per_device, mesh.shape["ep"], mesh.shape["ad"]),
        mesh=mesh,
        in_specs=placed,
        out_specs=P(("rep", "ep"), "ad"),
        check_vma=False,
    )
```

```python
import functools
import math

import jax
import jax.numpy as jnp
from jax import lax
from jax.experimental import pallas as pl
from jax.experimental.pallas import tpu as pltpu
from jax.sharding import PartitionSpec as P

EXPERT_COUNT = 8
TOP = 2
RANK = 16
CAP = 48
LIMIT = 16
LIMIT_EARLY = 21
N_TILE = 512
HELD_EACH = 2
HELD_ARRAYS = 4
RING = 4
MIB = 1 << 20

F32 = jnp.float32
BF16 = jnp.bfloat16


def mm(a, b):
    return jnp.dot(a, b, preferred_element_type=F32)


def mm_nt(a, b):
    return lax.dot_general(a, b, (((1,), (1,)), ((), ())), preferred_element_type=F32)


SMALL = pl.CostEstimate(flops=1, bytes_accessed=1, transcendentals=0)


def params(mib):
    return pltpu.CompilerParams(vmem_limit_bytes=mib * MIB)


def vmem():
    return pl.BlockSpec(memory_space=pltpu.VMEM)


def smem():
    return pl.BlockSpec(memory_space=pltpu.SMEM)


def facts_kernel(tokens_ref, chosen_ref, logits_ref, tenant_ref, out_ref, sem):
    rows, width = tokens_ref.shape
    copy = pltpu.make_async_copy(tokens_ref, out_ref.at[:, pl.ds(0, width)], sem)
    copy.start()
    diagonal = lax.broadcasted_iota(jnp.int32, (rows, rows), 0) == lax.broadcasted_iota(jnp.int32, (rows, rows), 1)
    tenant = jnp.sum(jnp.where(diagonal, tenant_ref[...].astype(F32), 0.0), axis=1, keepdims=True)
    chosen = chosen_ref[...].astype(F32)
    columns, rest = [chosen[:, 0:1], chosen[:, 1:2], tenant], logits_ref[...]
    for _ in range(3):
        piece = rest.astype(BF16).astype(F32)
        columns += [piece[:, 0:1], piece[:, 1:2]]
        rest = rest - piece
    lane = lax.broadcasted_iota(jnp.int32, (rows, 128), 1)
    facts = jnp.zeros((rows, 128), F32)
    for number, column in enumerate(columns):
        facts = jnp.where(lane == number, column, facts)
    out_ref[:, width:] = facts.astype(BF16)
    copy.wait()


def with_facts(tokens, chosen_experts, logits, tenant):
    rows, width = tokens.shape
    return pl.pallas_call(
        facts_kernel,
        out_shape=jax.ShapeDtypeStruct((rows, width + 128), BF16),
        in_specs=[pl.BlockSpec(memory_space=pltpu.HBM)] + [vmem()] * 3,
        out_specs=vmem(),
        scratch_shapes=[pltpu.SemaphoreType.DMA],
        cost_estimate=SMALL,
        compiler_params=params(LIMIT_EARLY),
        name="tokens_with_facts",
    )(pltpu.with_memory_space_constraint(tokens, pltpu.HBM), chosen_experts, logits, tenant.reshape(1, rows))


def meta_kernel(n_local, local_halves, ids_ref, adapter_ref, pool_slot_ref, *refs):
    blocks, (p_ref, pt_ref, cols_ref, rows_ref, tslot_ref) = refs[:-5], refs[-5:]
    at = blocks[0].shape[1] - 128
    facts = jnp.concatenate([block[:, at:] for block in blocks], axis=0).astype(F32).T
    count = facts.shape[1]
    first, second, tenant = facts[0:1], facts[1:2], facts[2:3]
    logit_first = (facts[3:4] + facts[5:6]) + facts[7:8]
    logit_second = (facts[4:5] + facts[6:7]) + facts[8:9]
    weight_first = jax.nn.sigmoid(logit_first - logit_second)
    weight_second = jax.nn.sigmoid(logit_second - logit_first)
    slot = jnp.zeros_like(tenant)
    for number in range(adapter_ref.shape[0]):
        slot = jnp.where(tenant == number, pool_slot_ref[adapter_ref[number]].astype(F32), slot)
    members, weights = [], []
    for i in range(n_local):
        expert = (ids_ref[0] * local_halves // 2 + i).astype(F32)
        hit_first, hit_second = first == expert, second == expert
        members.append(jnp.where(hit_first | hit_second, 1.0, 0.0))
        weights.append(jnp.where(hit_first, weight_first, 0.0) + jnp.where(hit_second, weight_second, 0.0))
    member = jnp.concatenate(members + [jnp.zeros((8 - n_local, count), F32)], axis=0)
    before = (
        lax.broadcasted_iota(jnp.int32, (count, count), 0) < lax.broadcasted_iota(jnp.int32, (count, count), 1)
    ).astype(BF16)
    place = jnp.where(member > 0, mm(member.astype(BF16), before), -1.0)
    table = jnp.concatenate(
        [place[0:n_local]] + weights + [slot] + [jnp.zeros((127 - 2 * n_local, count), F32)], axis=0
    )
    columns = table.T
    cols_ref[...] = columns
    rows_ref[...] = table[0:8]
    row_count = p_ref.shape[1]
    tenant_rows = jnp.broadcast_to(tenant, (8, count)).astype(BF16)
    down = lax.broadcasted_iota(jnp.int32, (row_count, count), 0).astype(F32)
    across = lax.broadcasted_iota(jnp.int32, (count, row_count), 1).astype(F32)
    for i in range(n_local):
        picked = (down == place[i : i + 1]).astype(BF16)
        p_ref[i] = picked
        pt_ref[i] = (across == columns[:, i : i + 1]).astype(BF16)
        tslot_ref[i] = mm_nt(tenant_rows, picked)


def build_meta(blocks, ids, adapters, pool_slots, n_local, local_halves, row_count):
    count = sum(block.shape[0] for block in blocks)
    return pl.pallas_call(
        functools.partial(meta_kernel, n_local, local_halves),
        out_shape=(
            jax.ShapeDtypeStruct((n_local, row_count, count), BF16),
            jax.ShapeDtypeStruct((n_local, count, row_count), BF16),
            jax.ShapeDtypeStruct((count, 128), F32),
            jax.ShapeDtypeStruct((8, count), F32),
            jax.ShapeDtypeStruct((n_local, 8, row_count), F32),
        ),
        in_specs=[smem()] * 3 + [vmem()] * len(blocks),
        out_specs=(vmem(),) * 5,
        cost_estimate=SMALL,
        compiler_params=params(min(38, LIMIT_EARLY * count // 512)),
        name="routing_tables",
    )(ids, adapters, pool_slots, *blocks)


class Slabs:
    def __init__(self, gate_ref, up_ref, down_ref, resident, ring, sems):
        self.sources, self.down, self.resident, self.ring, self.sems = (gate_ref, up_ref), down_ref, resident, ring, sems
        self.halves, self.depth, self.hidden = gate_ref.shape
        self.width = resident[0].shape[2]
        self.each = resident[0].shape[0]
        self.first = len(resident) * self.each
        self.capacity = 1 if ring is None else ring.shape[0]
        self.tiles = self.hidden // self.width
        self.early = 2 * self.halves * self.tiles
        self.held = self.depth // self.hidden
        self.columns = down_ref.shape[2] // self.width
        self.count = self.early + -(-self.columns * self.halves // self.held)

    def place(self, number):
        if number < self.first:
            return self.resident[number // self.each].at[number % self.each]
        return self.ring.at[(number - self.first) % self.capacity]

    def copies(self, number):
        place = self.place(number)
        slot = number if number < self.first else (number - self.first) % self.capacity
        if number < self.early:
            half, tile, which = number // (2 * self.tiles), number // 2 % self.tiles, number % 2
            rows = self.depth // 2
            return [
                pltpu.make_async_copy(
                    self.sources[which].at[half, pl.ds(i * rows, rows), pl.ds(tile * self.width, self.width)],
                    place.at[pl.ds(i * rows, rows)],
                    self.sems.at[slot, i],
                )
                for i in range(2)
            ]
        made = []
        for i in range(self.held):
            piece = (number - self.early) * self.held + i
            if piece < self.columns * self.halves:
                source = self.down.at[piece % self.halves, :, pl.ds(piece // self.halves * self.width, self.width)]
                into = place.at[pl.ds(i * self.hidden, self.hidden)]
                made.append(pltpu.make_async_copy(source, into, self.sems.at[slot, i]))
        return made

    def start(self, number):
        for copy in self.copies(number):
            copy.start()

    def wait(self, number):
        for copy in self.copies(number):
            copy.wait()

    def down_piece(self, column, half):
        piece = column * self.halves + half
        return self.early + piece // self.held, piece % self.held


def resident_shapes(gate, down):
    local_halves, width, hidden_count = gate.shape
    tile = min(N_TILE, hidden_count)
    pieces = local_halves * down.shape[2] // tile
    count = 2 * local_halves * hidden_count // tile + -(-pieces * hidden_count // width)
    each = min(HELD_EACH, count)
    return [(each, width, tile)] * min(HELD_ARRAYS, count // each)


def ring_size(gate, down, resident):
    pieces = gate.shape[0] * down.shape[2] // resident[0].shape[2]
    count = 2 * gate.shape[0] * gate.shape[2] // resident[0].shape[2] + -(-pieces * gate.shape[2] // gate.shape[1])
    return max(1, min(RING, count - len(resident) * resident[0].shape[0]))


def semaphores(gate, slots):
    return pltpu.SemaphoreType.DMA((slots, max(2, gate.shape[1] // gate.shape[2])))


def prefetch_kernel(ids_ref, gate_ref, up_ref, down_ref, *refs):
    resident, mark_ref, sems = refs[:-2], refs[-2], refs[-1]
    slabs = Slabs(gate_ref, up_ref, down_ref, resident, None, sems)
    for number in range(slabs.first):
        slabs.start(number)
    mark_ref[...] = jnp.zeros_like(mark_ref)
    for number in range(slabs.first):
        slabs.wait(number)


def prefetch(ids, gate, up, down, count):
    shapes = resident_shapes(gate, down)
    return pl.pallas_call(
        prefetch_kernel,
        out_shape=(*[pltpu.VMEM(shape, BF16) for shape in shapes], jax.ShapeDtypeStruct((8, 128), F32)),
        in_specs=[smem()] + [pl.BlockSpec(memory_space=pltpu.HBM)] * 3,
        out_specs=(vmem(),) * (len(shapes) + 1),
        scratch_shapes=[semaphores(gate, len(shapes) * shapes[0][0])],
        cost_estimate=SMALL,
        compiler_params=params(min(38, LIMIT_EARLY * count // 512)),
        name="weight_prefetch",
    )(ids, gate, up, down)


def expert_kernel(n_blocks, n_resident, n_ad, order, *refs):
    blocks, refs = refs[:n_blocks], refs[n_blocks:]
    ids_ref, adapter_ref, pool_slot_ref, p_ref, pt_ref, cols_ref, tslot_ref, rows_ref = refs[1:9]
    gate_ref, up_ref, down_ref, pool_ref = refs[9:13]
    resident, refs = refs[13 : 13 + n_resident], refs[13 + n_resident :]
    keep, send, keep_rest, send_rest, base, packed, hidden, factors, factor_sems, ring, sems = refs
    slabs = Slabs(gate_ref, up_ref, down_ref, resident, ring, sems)
    n_local = p_ref.shape[0]
    local_halves, depth, _ = gate_ref.shape
    halves_each = local_halves // n_local
    tenants, rank = adapter_ref.shape[0], pool_ref.shape[2]
    factor_copies = [
        pltpu.make_async_copy(
            pool_ref.at[pool_slot_ref[adapter_ref[number]]],
            factors.at[:, number * rank : (number + 1) * rank],
            factor_sems.at[number],
        )
        for number in range(tenants)
    ]
    for copy in factor_copies:
        copy.start()
    for number in range(slabs.first, min(slabs.count, slabs.first + slabs.capacity)):
        slabs.start(number)

    def ready(number):
        if number >= slabs.first:
            slabs.wait(number)

    def used(number):
        if slabs.first <= number < slabs.count - slabs.capacity:
            slabs.start(number + slabs.capacity)

    whole = jnp.concatenate([block[:, :depth] for block in blocks], axis=0)
    for i in range(n_local):
        packed[i] = mm(p_ref[i], whole).astype(BF16)
    for half in range(local_halves):
        rows = packed[half // halves_each]
        for tile in range(slabs.tiles):
            values = []
            for which in range(2):
                number = (half * slabs.tiles + tile) * 2 + which
                ready(number)
                values.append(mm(rows, slabs.place(number)[...]))
                used(number)
            span = slice(tile * slabs.width, (tile + 1) * slabs.width)
            hidden[half, :, span] = (jax.nn.silu(values[0]) * values[1]).astype(BF16)
    span = base.shape[1]
    at = span
    for copy in factor_copies:
        copy.wait()
    for out in (keep, send):
        out[:, at:] = jnp.zeros((out.shape[0], 256), BF16)
    for i in range(n_local):
        low = mm_nt(factors[i * halves_each], hidden[i * halves_each])
        for half in range(i * halves_each + 1, (i + 1) * halves_each):
            low = low + mm_nt(factors[half], hidden[half])
        owner = tslot_ref[i][0:1]
        total = jnp.zeros((rank, low.shape[1]), F32)
        for number in range(tenants):
            total = total + jnp.where(owner == number, low[number * rank : (number + 1) * rank], 0.0)
        weight = rows_ref[n_local + i : n_local + i + 1]
        value = (mm(total.astype(BF16), p_ref[i]) * weight).astype(BF16)
        row = pl.multiple_of((ids_ref[0] * local_halves // 2 + i) * rank, rank)
        for place, out in enumerate((keep, send)):
            for b in range(value.shape[1] // 128):
                lane = at + (b % 2 ^ place) * 128
                out[pl.ds(b // 2 * 128 + row, rank), lane : lane + 128] = value[:, b * 128 : b * 128 + 128]
    part = math.gcd(span, slabs.width)
    for column in range(slabs.columns):
        total = None
        for i in range(n_local):
            part_sum = None
            for half in range(i * halves_each, (i + 1) * halves_each):
                number, piece = slabs.down_piece(column, half)
                if piece == 0:
                    ready(number)
                value = mm(hidden[half], slabs.place(number)[piece * slabs.hidden : (piece + 1) * slabs.hidden])
                if piece == slabs.held - 1:
                    used(number)
                part_sum = value if part_sum is None else part_sum + value
            laid = mm(pt_ref[i], part_sum.astype(BF16)) * cols_ref[:, n_local + i : n_local + i + 1]
            total = laid if total is None else total + laid
        for first in range(0, slabs.width, part):
            feature = column * slabs.width + first
            owner, inside = feature // span, feature % span
            step = lax.rem(owner - ids_ref[1] + n_ad, n_ad)
            position = sum(jnp.where(step == s, position, 0) for position, s in enumerate(order))
            value = total[:, first : first + part]

            @pl.when(step == 0)
            def _():
                base[:, inside : inside + part] = value

            @pl.when(step == order[0])
            def _():
                write_pairs(value, (keep, send), inside)

            @pl.when((step != 0) & (step != order[0]))
            def _():
                write_pairs(value, (keep_rest, send_rest), pl.multiple_of((position - 1) * span + inside, 128))


def expert_part(
    blocks, mark, ids, adapters, pool_slots, picked, pt, cols, tslot, table_rows, gate, up, down, pool, resident, n_ad, order
):
    local_halves, width, hidden_count = gate.shape
    n_local, row_count, count = picked.shape
    tenants, rank = adapters.shape[0], pool.shape[2]
    span = down.shape[2] // n_ad
    hbm = pl.BlockSpec(memory_space=pltpu.HBM)
    ring = ring_size(gate, down, resident)
    outs = [pltpu.VMEM((count // 2, span + 256), BF16)] * 2
    outs += [pltpu.VMEM((count // 2, span * (len(order) - 1)), BF16)] * 2
    outs.append(pltpu.VMEM((count, span), F32))
    return pl.pallas_call(
        functools.partial(expert_kernel, len(blocks), len(resident), n_ad, order),
        out_shape=tuple(outs),
        in_specs=[vmem()] * (len(blocks) + 1) + [smem()] * 3 + [vmem()] * 5 + [hbm] * 4 + [vmem()] * len(resident),
        out_specs=(vmem(),) * len(outs),
        scratch_shapes=[
            pltpu.VMEM((n_local, row_count, width), BF16),
            pltpu.VMEM((local_halves, row_count, hidden_count), BF16),
            pltpu.VMEM((local_halves, tenants * rank, hidden_count), BF16),
            pltpu.SemaphoreType.DMA((tenants,)),
            pltpu.VMEM((ring, *resident[0].shape[1:]), BF16),
            semaphores(gate, ring),
        ],
        cost_estimate=SMALL,
        compiler_params=params(min(38, LIMIT_EARLY * count // 512)),
        name="experts",
    )(
        *blocks, mark, ids, adapters, pool_slots, picked, pt, cols, tslot, table_rows, gate, up, down, pool,
        *[pltpu.with_memory_space_constraint(x, pltpu.VMEM) for x in resident],
    )


def write_pairs(total, outs, at=0):
    keep, send = outs
    for b in range(total.shape[0] // 128):
        block = total[b * 128 : b * 128 + 128].astype(BF16)
        (send if b % 2 else keep)[b // 2 * 128 : b // 2 * 128 + 128, pl.ds(at, total.shape[1])] = block


def adapter_kernel(slot_column, ids_ref, base_ref, cols_ref, factor_ref, low_ref, other_ref, keep, send):
    low = (low_ref[...].astype(F32) + other_ref[...].astype(F32)).T.astype(BF16)
    zero = jnp.zeros_like(low)
    slot = cols_ref[:, slot_column : slot_column + 1]
    depth = EXPERT_COUNT * RANK
    slot_count = factor_ref.shape[0] // depth
    total = base_ref[...]
    for j in range(0, slot_count, 2):
        spread = jnp.concatenate(
            [jnp.where(slot == (ids_ref[0] * slot_count + j + i).astype(F32), low, zero) for i in range(2)], axis=1
        )
        total = total + mm(spread, factor_ref[j * depth : (j + 2) * depth])
    write_pairs(total, (keep, send))


def adapter_part(ids, base, cols, slot_column, factors, low, other):
    count, span = base.shape
    return pl.pallas_call(
        functools.partial(adapter_kernel, slot_column),
        out_shape=(jax.ShapeDtypeStruct((count // 2, span), BF16),) * 2,
        in_specs=[smem()] + [vmem()] * 5,
        out_specs=(vmem(),) * 2,
        cost_estimate=SMALL,
        compiler_params=params(max(LIMIT, 24 * count * span // MIB)),
        name="adapters",
    )(ids, base, cols, factors, low, other)


def split_kernel(wide, keep_ref, came_ref, keep, send):
    blocks = keep_ref.shape[0] // 128
    low = keep_ref.shape[1] - wide
    for b in range(blocks):
        total = keep_ref[b * 128 : b * 128 + 128].astype(F32) + came_ref[b * 128 : b * 128 + 128].astype(F32)
        total = total.astype(BF16)
        rows = slice(b // 2 * 128, b // 2 * 128 + 128)
        (send if b % 2 else keep)[rows, 0:wide] = total[:, 0:wide]
        if low:
            for place, out in enumerate((keep, send)):
                lane = wide + (b % 2 ^ place) * low
                out[rows, lane : lane + low] = total[:, wide:]


def split_sum(keep, came, wide):
    rows, columns = keep.shape
    shape = jax.ShapeDtypeStruct((rows // 2, wide + 2 * (columns - wide)), BF16)
    return pl.pallas_call(
        functools.partial(split_kernel, wide),
        out_shape=(shape, shape),
        in_specs=[vmem()] * 2,
        out_specs=(vmem(),) * 2,
        cost_estimate=SMALL,
        compiler_params=params(LIMIT),
        name="sum_and_split",
    )(keep, came)


def cut_kernel(edges, keep_ref, came_ref, *outs):
    for first, last, out in zip(edges, edges[1:], outs):
        out[...] = (keep_ref[:, first:last].astype(F32) + came_ref[:, first:last].astype(F32)).astype(BF16)


def cut_sum(keep, came, edges):
    return pl.pallas_call(
        functools.partial(cut_kernel, edges),
        out_shape=tuple(
            jax.ShapeDtypeStruct((keep.shape[0], last - first), BF16) for first, last in zip(edges, edges[1:])
        ),
        in_specs=[vmem()] * 2,
        out_specs=(vmem(),) * (len(edges) - 1),
        cost_estimate=SMALL,
        compiler_params=params(LIMIT),
        name="sum_and_cut",
    )(keep, came)


def per_device(
    n_ep,
    n_ad,
    tokens,
    chosen_experts,
    router_gate_logits,
    token_tenant,
    adapter_of_tenant,
    adapter_pool_slot,
    gate_weight,
    up_weight,
    down_weight,
    adapter_input_factors,
    adapter_output_factors,
):
    gate_weight, up_weight, down_weight, adapter_input_factors = [
        pltpu.with_memory_space_constraint(x, pltpu.HBM)
        for x in (gate_weight, up_weight, down_weight, adapter_input_factors)
    ]
    width = tokens.shape[1]
    span = width // n_ad
    local_halves = gate_weight.shape[0]
    n_local = max(1, local_halves // 2)
    row_count = n_ep * CAP
    bits = n_ep.bit_length() - 1
    ids = jnp.stack([lax.axis_index("ep"), lax.axis_index("ad")]).astype(jnp.int32)

    def swap(x, mask):
        return lax.ppermute(x, "ep", [(i, i ^ mask) for i in range(n_ep)])

    def tie(x, y):
        return lax.optimization_barrier((x, y))

    def shift(x, step):
        return lax.ppermute(x, "ad", [(i, (i + step) % n_ad) for i in range(n_ad)])

    order = sorted(range(1, n_ad), key=lambda step: (step != n_ad // 2, step))
    own = with_facts(tokens, chosen_experts, router_gate_logits, token_tenant)
    *resident, mark = prefetch(ids, gate_weight, up_weight, down_weight, n_ep * tokens.shape[0])
    blocks = {0: own}
    for bit in reversed(range(bits)):
        for mask in list(blocks):
            blocks[mask | 1 << bit] = swap(blocks[mask], 1 << bit)
        if bit == bits - 1:
            blocks[1 << bit], mark = tie(blocks[1 << bit], mark)
    blocks = [blocks[mask] for mask in range(n_ep)]
    picked, pt, cols, table_rows, tslot = build_meta(
        blocks, ids, adapter_of_tenant, adapter_pool_slot, n_local, local_halves, row_count
    )
    keep, send, keep_rest, send_rest, base = expert_part(
        blocks, mark, ids, adapter_of_tenant, adapter_pool_slot, picked, pt, cols, tslot, table_rows, gate_weight,
        up_weight, down_weight, adapter_input_factors, resident, n_ad, order,
    )

    def across(keep, came, wide, edges):
        for bit in range(2, bits):
            keep, send = split_sum(keep, came, wide)
            came = swap(send, 1 << bit)
        return cut_sum(keep, came, edges)

    came, came_rest = swap(send, 1), swap(send_rest, 1)
    wide = span * (n_ad - 2)
    if bits > 1:
        keep, send = split_sum(keep, came, span)
        keep_rest, send_rest = split_sum(keep_rest, came_rest, wide)
        came = swap(send, 2)
        came, keep_rest = tie(came, keep_rest)
        came_rest = swap(send_rest, 2)
    sums, low = across(keep, came, span, (0, span, span + n_ep * 128))
    low_steps = n_ad.bit_length() - 1
    for bit in range(low_steps):
        other = lax.ppermute(low, "ad", [(i, i ^ 1 << bit) for i in range(n_ad)])
        if bit < low_steps - 1:
            low = (low.astype(F32) + other.astype(F32)).astype(BF16)
    came_rest, other = tie(came_rest, other)
    rest = across(keep_rest, came_rest, wide, [span * i for i in range(n_ad - 1)])
    results = [shift(sums, order[0])]
    slot_count = adapter_output_factors.shape[0]
    flat_factors = adapter_output_factors.reshape(slot_count * EXPERT_COUNT * RANK, span)
    keep, send = adapter_part(ids, base, cols, 2 * n_local, flat_factors, low, other)
    results += [shift(x, step) for x, step in zip(rest, order[1:])]
    came = swap(send, 1)
    for bit in range(1, bits):
        keep, send = split_sum(keep, came, span)
        came = swap(send, 1 << bit)
    return sum(x.astype(F32) for x in [keep, came] + results).astype(BF16)


def solution(mesh):
    placed = (
        P(("rep", "ep"), None),
        P(("rep", "ep"), None),
        P(("rep", "ep"), None),
        P(("rep", "ep")),
        P("rep"),
        P(),
        P("ep", None, "ad"),
        P("ep", None, "ad"),
        P("ep", "ad", None),
        P(None, "ep", None, "ad"),
        P("ep", None, None, "ad"),
    )
    return jax.shard_map(
        functools.partial(per_device, mesh.shape["ep"], mesh.shape["ad"]),
        mesh=mesh,
        in_specs=placed,
        out_specs=P(("rep", "ep"), "ad"),
        check_vma=False,
    )
```

```python
import functools
import math

import jax
import jax.numpy as jnp
from jax import lax
from jax.experimental import pallas as pl
from jax.experimental.pallas import tpu as pltpu
from jax.sharding import PartitionSpec as P

EXPERT_COUNT = 8
TOP = 2
RANK = 16
CAP = 48
LIMIT = 16
LIMIT_EARLY = 21
N_TILE = 512
HELD_EACH = 2
HELD_ARRAYS = 4
RING = 4
MIB = 1 << 20

F32 = jnp.float32
BF16 = jnp.bfloat16


def mm(a, b):
    return jnp.dot(a, b, preferred_element_type=F32)


def mm_nt(a, b):
    return lax.dot_general(a, b, (((1,), (1,)), ((), ())), preferred_element_type=F32)


SMALL = pl.CostEstimate(flops=1, bytes_accessed=1, transcendentals=0)


def params(mib):
    return pltpu.CompilerParams(vmem_limit_bytes=mib * MIB)


def vmem():
    return pl.BlockSpec(memory_space=pltpu.VMEM)


def smem():
    return pl.BlockSpec(memory_space=pltpu.SMEM)


def facts_kernel(tokens_ref, chosen_ref, logits_ref, tenant_ref, out_ref, sem):
    rows, width = tokens_ref.shape
    copy = pltpu.make_async_copy(tokens_ref, out_ref.at[:, pl.ds(0, width)], sem)
    copy.start()
    diagonal = lax.broadcasted_iota(jnp.int32, (rows, rows), 0) == lax.broadcasted_iota(jnp.int32, (rows, rows), 1)

    def column(row):
        return jnp.sum(jnp.where(diagonal, row, 0.0), axis=1, keepdims=True)

    chosen, logits = chosen_ref[...].astype(F32), logits_ref[...]
    columns = [column(chosen[0:1]), column(chosen[1:2]), column(tenant_ref[...].astype(F32))]
    rests = [column(logits[0:1]), column(logits[1:2])]
    for _ in range(3):
        pieces = [rest.astype(BF16).astype(F32) for rest in rests]
        columns += pieces
        rests = [rest - piece for rest, piece in zip(rests, pieces)]
    lane = lax.broadcasted_iota(jnp.int32, (rows, 128), 1)
    facts = jnp.zeros((rows, 128), F32)
    for number, value in enumerate(columns):
        facts = jnp.where(lane == number, value, facts)
    out_ref[:, width:] = facts.astype(BF16)
    copy.wait()


def with_facts(tokens, chosen_experts, logits, tenant):
    rows, width = tokens.shape
    return pl.pallas_call(
        facts_kernel,
        out_shape=jax.ShapeDtypeStruct((rows, width + 128), BF16),
        in_specs=[pl.BlockSpec(memory_space=pltpu.HBM)] + [vmem()] * 3,
        out_specs=vmem(),
        scratch_shapes=[pltpu.SemaphoreType.DMA],
        cost_estimate=SMALL,
        compiler_params=params(LIMIT_EARLY),
        name="tokens_with_facts",
    )(pltpu.with_memory_space_constraint(tokens, pltpu.HBM), chosen_experts.T, logits.T, tenant.reshape(1, rows))


def meta_kernel(n_local, local_halves, ids_ref, adapter_ref, pool_slot_ref, *refs):
    blocks, (p_ref, pt_ref, cols_ref, rows_ref, tslot_ref) = refs[:-5], refs[-5:]
    at = blocks[0].shape[1] - 128
    facts = jnp.concatenate([block[:, at:] for block in blocks], axis=0).astype(F32).T
    count = facts.shape[1]
    first, second, tenant = facts[0:1], facts[1:2], facts[2:3]
    logit_first = (facts[3:4] + facts[5:6]) + facts[7:8]
    logit_second = (facts[4:5] + facts[6:7]) + facts[8:9]
    weight_first = jax.nn.sigmoid(logit_first - logit_second)
    weight_second = jax.nn.sigmoid(logit_second - logit_first)
    slot = jnp.zeros_like(tenant)
    for number in range(adapter_ref.shape[0]):
        slot = jnp.where(tenant == number, pool_slot_ref[adapter_ref[number]].astype(F32), slot)
    members, weights = [], []
    for i in range(n_local):
        expert = (ids_ref[0] * local_halves // 2 + i).astype(F32)
        hit_first, hit_second = first == expert, second == expert
        members.append(jnp.where(hit_first | hit_second, 1.0, 0.0))
        weights.append(jnp.where(hit_first, weight_first, 0.0) + jnp.where(hit_second, weight_second, 0.0))
    member = jnp.concatenate(members + [jnp.zeros((8 - n_local, count), F32)], axis=0)
    before = (
        lax.broadcasted_iota(jnp.int32, (count, count), 0) < lax.broadcasted_iota(jnp.int32, (count, count), 1)
    ).astype(BF16)
    place = jnp.where(member > 0, mm(member.astype(BF16), before), -1.0)
    table = jnp.concatenate(
        [place[0:n_local]] + weights + [slot] + [jnp.zeros((127 - 2 * n_local, count), F32)], axis=0
    )
    columns = table.T
    cols_ref[...] = columns
    rows_ref[...] = table[0:8]
    row_count = p_ref.shape[1]
    tenant_rows = jnp.broadcast_to(tenant, (8, count)).astype(BF16)
    down = lax.broadcasted_iota(jnp.int32, (row_count, count), 0).astype(F32)
    across = lax.broadcasted_iota(jnp.int32, (count, row_count), 1).astype(F32)
    for i in range(n_local):
        picked = (down == place[i : i + 1]).astype(BF16)
        p_ref[i] = picked
        pt_ref[i] = (across == columns[:, i : i + 1]).astype(BF16)
        tslot_ref[i] = mm_nt(tenant_rows, picked)


def build_meta(blocks, ids, adapters, pool_slots, n_local, local_halves, row_count):
    count = sum(block.shape[0] for block in blocks)
    return pl.pallas_call(
        functools.partial(meta_kernel, n_local, local_halves),
        out_shape=(
            jax.ShapeDtypeStruct((n_local, row_count, count), BF16),
            jax.ShapeDtypeStruct((n_local, count, row_count), BF16),
            jax.ShapeDtypeStruct((count, 128), F32),
            jax.ShapeDtypeStruct((8, count), F32),
            jax.ShapeDtypeStruct((n_local, 8, row_count), F32),
        ),
        in_specs=[smem()] * 3 + [vmem()] * len(blocks),
        out_specs=(vmem(),) * 5,
        cost_estimate=SMALL,
        compiler_params=params(min(38, LIMIT_EARLY * count // 512)),
        name="routing_tables",
    )(ids, adapters, pool_slots, *blocks)


class Slabs:
    def __init__(self, gate_ref, up_ref, resident, ring, sems):
        self.sources, self.resident, self.ring, self.sems = (gate_ref, up_ref), resident, ring, sems
        self.halves, self.depth, hidden = gate_ref.shape
        self.width = resident[0].shape[2]
        self.each = resident[0].shape[0]
        self.first = len(resident) * self.each
        self.capacity = 1 if ring is None else ring.shape[0]
        self.tiles = hidden // self.width
        self.count = 2 * self.halves * self.tiles

    def place(self, number):
        if number < self.first:
            return self.resident[number // self.each].at[number % self.each]
        return self.ring.at[(number - self.first) % self.capacity]

    def copies(self, number):
        place, rows = self.place(number), self.depth // 2
        slot = number if number < self.first else (number - self.first) % self.capacity
        half, tile, which = number // (2 * self.tiles), number // 2 % self.tiles, number % 2
        return [
            pltpu.make_async_copy(
                self.sources[which].at[half, pl.ds(i * rows, rows), pl.ds(tile * self.width, self.width)],
                place.at[pl.ds(i * rows, rows)],
                self.sems.at[slot, i],
            )
            for i in range(2)
        ]

    def start(self, number):
        for copy in self.copies(number):
            copy.start()

    def wait(self, number):
        for copy in self.copies(number):
            copy.wait()


def resident_shapes(gate):
    local_halves, width, hidden_count = gate.shape
    tile = min(N_TILE, hidden_count)
    count = 2 * local_halves * hidden_count // tile
    each = min(HELD_EACH, count)
    return [(each, width, tile)] * min(HELD_ARRAYS, count // each)


def down_slabs(down, n_ad):
    return pltpu.VMEM((down.shape[0], down.shape[1], down.shape[2] // n_ad), BF16)


def down_fetch(n_ad, step, ids_ref, down_ref, into_ref, sems):
    _, rows, span = into_ref.shape
    rows = rows // 2
    start = pl.multiple_of(lax.rem(ids_ref[1] + step, n_ad) * span, span)
    return [
        pltpu.make_async_copy(
            down_ref.at[half, pl.ds(i * rows, rows), pl.ds(start, span)],
            into_ref.at[half, pl.ds(i * rows, rows)],
            sems.at[half, i],
        )
        for half in range(down_ref.shape[0])
        for i in range(2)
    ]


def prefetch_kernel(ids_ref, gate_ref, up_ref, *refs):
    resident, mark_ref, sems = refs[:-2], refs[-2], refs[-1]
    slabs = Slabs(gate_ref, up_ref, resident, None, sems)
    for number in range(slabs.first):
        slabs.start(number)
    mark_ref[...] = jnp.zeros_like(mark_ref)
    for number in range(slabs.first):
        slabs.wait(number)


def prefetch(ids, gate, up, count):
    shapes = resident_shapes(gate)
    return pl.pallas_call(
        prefetch_kernel,
        out_shape=(*[pltpu.VMEM(shape, BF16) for shape in shapes], jax.ShapeDtypeStruct((8, 128), F32)),
        in_specs=[smem()] + [pl.BlockSpec(memory_space=pltpu.HBM)] * 2,
        out_specs=(vmem(),) * (len(shapes) + 1),
        scratch_shapes=[pltpu.SemaphoreType.DMA((len(shapes) * shapes[0][0], 2))],
        cost_estimate=SMALL,
        compiler_params=params(min(38, LIMIT_EARLY * count // 512)),
        name="weight_prefetch",
    )(ids, gate, up)


def expert_kernel(n_blocks, n_resident, n_ad, step, *refs):
    blocks, refs = refs[:n_blocks], refs[n_blocks:]
    ids_ref, adapter_ref, pool_slot_ref, p_ref, tslot_ref, rows_ref = refs[1:7]
    gate_ref, up_ref, down_ref, pool_ref = refs[7:11]
    resident, refs = refs[11 : 11 + n_resident], refs[11 + n_resident :]
    hidden, low_ref, next_ref, packed, factors, factor_sems, down_sems, ring, sems = refs
    slabs = Slabs(gate_ref, up_ref, resident, ring, sems)
    n_local = p_ref.shape[0]
    local_halves, depth, _ = gate_ref.shape
    halves_each = local_halves // n_local
    tenants, rank = adapter_ref.shape[0], pool_ref.shape[2]
    factor_copies = [
        pltpu.make_async_copy(
            pool_ref.at[pool_slot_ref[adapter_ref[number]]],
            factors.at[:, number * rank : (number + 1) * rank],
            factor_sems.at[number],
        )
        for number in range(tenants)
    ]
    for copy in factor_copies:
        copy.start()
    for number in range(slabs.first, min(slabs.count, slabs.first + slabs.capacity)):
        slabs.start(number)

    def ready(number):
        if number >= slabs.first:
            slabs.wait(number)

    def used(number):
        if slabs.first <= number < slabs.count - slabs.capacity:
            slabs.start(number + slabs.capacity)

    whole = jnp.concatenate([block[:, :depth] for block in blocks], axis=0)
    for i in range(n_local):
        packed[i] = mm(p_ref[i], whole).astype(BF16)
    for half in range(local_halves):
        rows = packed[half // halves_each]
        for tile in range(slabs.tiles):
            values = []
            for which in range(2):
                number = (half * slabs.tiles + tile) * 2 + which
                ready(number)
                values.append(mm(rows, slabs.place(number)[...]))
                used(number)
            span = slice(tile * slabs.width, (tile + 1) * slabs.width)
            hidden[half, :, span] = (jax.nn.silu(values[0]) * values[1]).astype(BF16)
    down_copies = down_fetch(n_ad, step, ids_ref, down_ref, next_ref, down_sems)
    for copy in down_copies:
        copy.start()
    for copy in factor_copies:
        copy.wait()
    for i in range(n_local):
        low = mm_nt(factors[i * halves_each], hidden[i * halves_each])
        for half in range(i * halves_each + 1, (i + 1) * halves_each):
            low = low + mm_nt(factors[half], hidden[half])
        owner = tslot_ref[i][0:1]
        total = jnp.zeros((rank, low.shape[1]), F32)
        for number in range(tenants):
            total = total + jnp.where(owner == number, low[number * rank : (number + 1) * rank], 0.0)
        weight = rows_ref[n_local + i : n_local + i + 1]
        low_ref[i * rank : (i + 1) * rank] = (mm(total.astype(BF16), p_ref[i]) * weight).astype(BF16)
    for copy in down_copies:
        copy.wait()


def expert_part(
    blocks, mark, ids, adapters, pool_slots, picked, tslot, table_rows, gate, up, down, pool, resident, n_ad, step
):
    local_halves, width, hidden_count = gate.shape
    n_local, row_count, count = picked.shape
    tenants, rank = adapters.shape[0], pool.shape[2]
    hbm = pl.BlockSpec(memory_space=pltpu.HBM)
    each, _, tile = resident[0].shape
    ring = max(1, min(RING, 2 * local_halves * hidden_count // tile - len(resident) * each))
    return pl.pallas_call(
        functools.partial(expert_kernel, len(blocks), len(resident), n_ad, step),
        out_shape=(
            pltpu.VMEM((local_halves, row_count, hidden_count), BF16),
            jax.ShapeDtypeStruct((n_local * rank, count), BF16),
            down_slabs(down, n_ad),
        ),
        in_specs=[vmem()] * (len(blocks) + 1) + [smem()] * 3 + [vmem()] * 3 + [hbm] * 4 + [vmem()] * len(resident),
        out_specs=(vmem(),) * 3,
        scratch_shapes=[
            pltpu.VMEM((n_local, row_count, width), BF16),
            pltpu.VMEM((local_halves, tenants * rank, hidden_count), BF16),
            pltpu.SemaphoreType.DMA((tenants,)),
            pltpu.SemaphoreType.DMA((local_halves, 2)),
            pltpu.VMEM((ring, width, tile), BF16),
            pltpu.SemaphoreType.DMA((ring, 2)),
        ],
        cost_estimate=SMALL,
        compiler_params=params(min(38, LIMIT_EARLY * count // 512)),
        name="experts",
    )(
        *blocks, mark, ids, adapters, pool_slots, picked, tslot, table_rows, gate, up, down, pool,
        *[pltpu.with_memory_space_constraint(x, pltpu.VMEM) for x in resident],
    )


def weighted_down(hidden_ref, weight_ref, pt_ref, cols_ref):
    n_local = pt_ref.shape[0]
    halves_each = hidden_ref.shape[0] // n_local
    total = None
    for i in range(n_local):
        part_sum = mm(hidden_ref[i * halves_each], weight_ref[i * halves_each])
        for half in range(i * halves_each + 1, (i + 1) * halves_each):
            part_sum = part_sum + mm(hidden_ref[half], weight_ref[half])
        laid = mm(pt_ref[i], part_sum.astype(BF16)) * cols_ref[:, n_local + i : n_local + i + 1]
        total = laid if total is None else total + laid
    return total


def down_first_kernel(n_ad, step, ids_ref, hidden_ref, weight_ref, pt_ref, cols_ref, down_ref, keep, send, next_ref, sems):
    copies = down_fetch(n_ad, step, ids_ref, down_ref, next_ref, sems)
    for copy in copies:
        copy.start()
    write_pairs(weighted_down(hidden_ref, weight_ref, pt_ref, cols_ref), (keep, send))
    for copy in copies:
        copy.wait()


def down_first(ids, hidden, weights, pt, cols, down, n_ad, step):
    count, span = pt.shape[1], weights.shape[2]
    return pl.pallas_call(
        functools.partial(down_first_kernel, n_ad, step),
        out_shape=(jax.ShapeDtypeStruct((count // 2, span), BF16),) * 2 + (down_slabs(down, n_ad),),
        in_specs=[smem()] + [vmem()] * 4 + [pl.BlockSpec(memory_space=pltpu.HBM)],
        out_specs=(vmem(),) * 3,
        scratch_shapes=[pltpu.SemaphoreType.DMA((down.shape[0], 2))],
        cost_estimate=SMALL,
        compiler_params=params(max(LIMIT, 12 * count * span // MIB)),
        name="down_first",
    )(ids, hidden, pltpu.with_memory_space_constraint(weights, pltpu.VMEM), pt, cols, down)


def down_rest_kernel(n_ad, steps, ids_ref, hidden_ref, weight_ref, pt_ref, cols_ref, down_ref, keep, send, base, *refs):
    held, sems = refs[:-1], refs[-1]
    copies = [
        down_fetch(n_ad, step, ids_ref, down_ref, into, sems.at[number])
        for number, (step, into) in enumerate(zip(steps[1:], held))
    ]
    for copy in [copy for group in copies for copy in group]:
        copy.start()
    span = weight_ref.shape[2]
    for number in range(len(steps)):
        if number:
            for copy in copies[number - 1]:
                copy.wait()
        total = weighted_down(hidden_ref, held[number - 1] if number else weight_ref, pt_ref, cols_ref)
        if number < len(steps) - 1:
            write_pairs(total, (keep, send), number * span)
        else:
            base[...] = total


def down_rest(ids, hidden, weights, pt, cols, down, n_ad, steps):
    count, span = pt.shape[1], weights.shape[2]
    return pl.pallas_call(
        functools.partial(down_rest_kernel, n_ad, steps),
        out_shape=(jax.ShapeDtypeStruct((count // 2, span * (len(steps) - 1)), BF16),) * 2
        + (jax.ShapeDtypeStruct((count, span), F32),),
        in_specs=[smem()] + [vmem()] * 4 + [pl.BlockSpec(memory_space=pltpu.HBM)],
        out_specs=(vmem(),) * 3,
        scratch_shapes=[pltpu.VMEM(weights.shape, BF16)] * (len(steps) - 1)
        + [pltpu.SemaphoreType.DMA((len(steps) - 1, down.shape[0], 2))],
        cost_estimate=SMALL,
        compiler_params=params(max(LIMIT, 12 * count * span // MIB) + (len(steps) - 1) * weights.size * 2 // MIB),
        name="down_rest",
    )(ids, hidden, pltpu.with_memory_space_constraint(weights, pltpu.VMEM), pt, cols, down)


def write_pairs(total, outs, at=0):
    keep, send = outs
    for b in range(total.shape[0] // 128):
        block = total[b * 128 : b * 128 + 128].astype(BF16)
        (send if b % 2 else keep)[b // 2 * 128 : b // 2 * 128 + 128, pl.ds(at, total.shape[1])] = block


def adapter_kernel(slot_column, local_halves, ids_ref, base_ref, cols_ref, factor_ref, low_ref, keep, send, wide):
    blocks = base_ref.shape[0] // 128
    height = low_ref.shape[0] // blocks
    wide[...] = jnp.zeros_like(wide)
    for m in range(blocks):
        row = pl.multiple_of(((ids_ref[0] ^ m) * local_halves // 2) * RANK, RANK)
        value = low_ref[m * height : (m + 1) * height].astype(F32)
        value = jnp.concatenate([value[:, (m ^ b) * 128 : (m ^ b) * 128 + 128] for b in range(blocks)], axis=1)
        wide[pl.ds(row, height)] += value
    low = wide[...].T.astype(BF16)
    zero = jnp.zeros_like(low)
    slot = cols_ref[:, slot_column : slot_column + 1]
    depth = EXPERT_COUNT * RANK
    slot_count = factor_ref.shape[0] // depth
    total = base_ref[...]
    for j in range(0, slot_count, 2):
        spread = jnp.concatenate(
            [jnp.where(slot == (ids_ref[0] * slot_count + j + i).astype(F32), low, zero) for i in range(2)], axis=1
        )
        total = total + mm(spread, factor_ref[j * depth : (j + 2) * depth])
    write_pairs(total, (keep, send))


def adapter_part(ids, base, cols, slot_column, local_halves, factors, low):
    count, span = base.shape
    return pl.pallas_call(
        functools.partial(adapter_kernel, slot_column, local_halves),
        out_shape=(jax.ShapeDtypeStruct((count // 2, span), BF16),) * 2,
        in_specs=[smem()] + [vmem()] * 4,
        out_specs=(vmem(),) * 2,
        scratch_shapes=[pltpu.VMEM((EXPERT_COUNT * RANK, count), F32)],
        cost_estimate=SMALL,
        compiler_params=params(max(LIMIT, 24 * count * span // MIB)),
        name="adapters",
    )(ids, base, cols, factors, low)


def split_kernel(keep_ref, came_ref, keep, send):
    for b in range(keep_ref.shape[0] // 128):
        total = keep_ref[b * 128 : b * 128 + 128].astype(F32) + came_ref[b * 128 : b * 128 + 128].astype(F32)
        (send if b % 2 else keep)[b // 2 * 128 : b // 2 * 128 + 128] = total.astype(BF16)


def split_sum(keep, came):
    return pl.pallas_call(
        split_kernel,
        out_shape=(jax.ShapeDtypeStruct((keep.shape[0] // 2, keep.shape[1]), BF16),) * 2,
        in_specs=[vmem()] * 2,
        out_specs=(vmem(),) * 2,
        cost_estimate=SMALL,
        compiler_params=params(LIMIT),
        name="sum_and_split",
    )(keep, came)


def cut_kernel(edges, keep_ref, came_ref, *outs):
    for first, last, out in zip(edges, edges[1:], outs):
        out[...] = (keep_ref[:, first:last].astype(F32) + came_ref[:, first:last].astype(F32)).astype(BF16)


def cut_sum(keep, came, edges):
    return pl.pallas_call(
        functools.partial(cut_kernel, edges),
        out_shape=tuple(
            jax.ShapeDtypeStruct((keep.shape[0], last - first), BF16) for first, last in zip(edges, edges[1:])
        ),
        in_specs=[vmem()] * 2,
        out_specs=(vmem(),) * (len(edges) - 1),
        cost_estimate=SMALL,
        compiler_params=params(LIMIT),
        name="sum_and_cut",
    )(keep, came)


def per_device(
    n_ep,
    n_ad,
    tokens,
    chosen_experts,
    router_gate_logits,
    token_tenant,
    adapter_of_tenant,
    adapter_pool_slot,
    gate_weight,
    up_weight,
    down_weight,
    adapter_input_factors,
    adapter_output_factors,
):
    gate_weight, up_weight, down_weight, adapter_input_factors = [
        pltpu.with_memory_space_constraint(x, pltpu.HBM)
        for x in (gate_weight, up_weight, down_weight, adapter_input_factors)
    ]
    width = tokens.shape[1]
    span = width // n_ad
    local_halves = gate_weight.shape[0]
    n_local = max(1, local_halves // 2)
    row_count = n_ep * CAP
    bits = n_ep.bit_length() - 1
    ids = jnp.stack([lax.axis_index("ep"), lax.axis_index("ad")]).astype(jnp.int32)

    def swap(x, mask):
        return lax.ppermute(x, "ep", [(i, i ^ mask) for i in range(n_ep)])

    def tie(x, y):
        return lax.optimization_barrier((x, y))

    def shift(x, step):
        return lax.ppermute(x, "ad", [(i, (i + step) % n_ad) for i in range(n_ad)])

    order = sorted(range(1, n_ad), key=lambda step: (step != n_ad // 2, step))
    own = with_facts(tokens, chosen_experts, router_gate_logits, token_tenant)
    *resident, mark = prefetch(ids, gate_weight, up_weight, n_ep * tokens.shape[0])
    blocks = {0: own}
    for bit in reversed(range(bits)):
        for mask in list(blocks):
            blocks[mask | 1 << bit] = swap(blocks[mask], 1 << bit)
        if bit == bits - 1:
            blocks[1 << bit], mark = tie(blocks[1 << bit], mark)
    blocks = [blocks[mask] for mask in range(n_ep)]
    picked, pt, cols, table_rows, tslot = build_meta(
        blocks, ids, adapter_of_tenant, adapter_pool_slot, n_local, local_halves, row_count
    )
    hidden, low, weights = expert_part(
        blocks, mark, ids, adapter_of_tenant, adapter_pool_slot, picked, tslot, table_rows, gate_weight, up_weight,
        down_weight, adapter_input_factors, resident, n_ad, order[0],
    )

    def onward(keep, came, first=1):
        for bit in range(first, bits):
            keep, send = split_sum(keep, came)
            came = swap(send, 1 << bit)
        return keep, came

    def other_of(low, bit):
        return lax.ppermute(low, "ad", [(i, i ^ 1 << bit) for i in range(n_ad)])

    def added(x, y):
        return (x.astype(F32) + y.astype(F32)).astype(BF16)

    far_steps = range(1, n_ad.bit_length() - 1)
    others = [other_of(low, bit) for bit in far_steps[:1]]
    keep, send, weights = down_first(ids, hidden, weights, pt, cols, down_weight, n_ad, order[1])
    others, keep, send, weights = lax.optimization_barrier((others, keep, send, weights))
    for bit in far_steps:
        low = added(low, others[0] if bit == 1 else other_of(low, bit))
    for bit in range(bits - 1):
        low = jnp.concatenate([low, swap(low, 1 << bit)], axis=0)
    crossed = swap(low, 1 << (bits - 1))
    keep, came = onward(keep, swap(send, 1), 1)
    keep, hidden = tie(keep, hidden)
    keep_rest, send_rest, base = down_rest(ids, hidden, weights, pt, cols, down_weight, n_ad, (*order[1:], 0))
    came, crossed, keep_rest, send_rest, base = lax.optimization_barrier((came, crossed, keep_rest, send_rest, base))
    low = jnp.concatenate([low, crossed], axis=0)
    low = added(low, other_of(low, 0))
    (sums,) = cut_sum(keep, came, (0, span))
    results = [shift(sums, order[0])]
    keep_rest, came_rest = onward(keep_rest, swap(send_rest, 1))
    slot_count = adapter_output_factors.shape[0]
    flat_factors = adapter_output_factors.reshape(slot_count * EXPERT_COUNT * RANK, span)
    keep, send = adapter_part(ids, base, cols, 2 * n_local, local_halves, flat_factors, low)
    came = swap(send, 1)
    if bits > 1:
        keep, send = split_sum(keep, came)
        came_rest, keep, send = lax.optimization_barrier((came_rest, keep, send))
        came = swap(send, 2)
    keep, came = onward(keep, came, 2)
    parts = cut_sum(keep_rest, came_rest, [span * i for i in range(n_ad - 1)])
    results += [shift(x, step) for x, step in zip(parts, order[1:])]
    return sum(x.astype(F32) for x in [keep, came] + results).astype(BF16)


def solution(mesh):
    placed = (
        P(("rep", "ep"), None),
        P(("rep", "ep"), None),
        P(("rep", "ep"), None),
        P(("rep", "ep")),
        P("rep"),
        P(),
        P("ep", None, "ad"),
        P("ep", None, "ad"),
        P("ep", "ad", None),
        P(None, "ep", None, "ad"),
        P("ep", None, None, "ad"),
    )
    return jax.shard_map(
        functools.partial(per_device, mesh.shape["ep"], mesh.shape["ad"]),
        mesh=mesh,
        in_specs=placed,
        out_specs=P(("rep", "ep"), "ad"),
        check_vma=False,
    )
```

```python
import functools
import math

import jax
import jax.numpy as jnp
from jax import lax
from jax.experimental import pallas as pl
from jax.experimental.pallas import tpu as pltpu
from jax.sharding import PartitionSpec as P

EXPERT_COUNT = 8
TOP = 2
RANK = 16
CAP = 48
LIMIT = 16
LIMIT_EARLY = 21
N_TILE = 512
HELD_EACH = 2
HELD_ARRAYS = 4
RING = 4
MIB = 1 << 20

F32 = jnp.float32
BF16 = jnp.bfloat16


def mm(a, b):
    return jnp.dot(a, b, preferred_element_type=F32)


def mm_nt(a, b):
    return lax.dot_general(a, b, (((1,), (1,)), ((), ())), preferred_element_type=F32)


SMALL = pl.CostEstimate(flops=1, bytes_accessed=1, transcendentals=0)


def params(mib):
    return pltpu.CompilerParams(vmem_limit_bytes=mib * MIB)


def vmem():
    return pl.BlockSpec(memory_space=pltpu.VMEM)


def smem():
    return pl.BlockSpec(memory_space=pltpu.SMEM)


def facts_kernel(tokens_ref, chosen_ref, logits_ref, tenant_ref, out_ref, sem):
    rows, width = tokens_ref.shape
    copy = pltpu.make_async_copy(tokens_ref, out_ref.at[:, pl.ds(0, width)], sem)
    copy.start()
    diagonal = lax.broadcasted_iota(jnp.int32, (rows, rows), 0) == lax.broadcasted_iota(jnp.int32, (rows, rows), 1)

    def column(row):
        return jnp.sum(jnp.where(diagonal, row, 0.0), axis=1, keepdims=True)

    chosen, logits = chosen_ref[...].astype(F32), logits_ref[...]
    columns = [column(chosen[0:1]), column(chosen[1:2]), column(tenant_ref[...].astype(F32))]
    rests = [column(logits[0:1]), column(logits[1:2])]
    for _ in range(3):
        pieces = [rest.astype(BF16).astype(F32) for rest in rests]
        columns += pieces
        rests = [rest - piece for rest, piece in zip(rests, pieces)]
    lane = lax.broadcasted_iota(jnp.int32, (rows, 128), 1)
    facts = jnp.zeros((rows, 128), F32)
    for number, value in enumerate(columns):
        facts = jnp.where(lane == number, value, facts)
    out_ref[:, width:] = facts.astype(BF16)
    copy.wait()


def with_facts(tokens, chosen_experts, logits, tenant):
    rows, width = tokens.shape
    return pl.pallas_call(
        facts_kernel,
        out_shape=jax.ShapeDtypeStruct((rows, width + 128), BF16),
        in_specs=[pl.BlockSpec(memory_space=pltpu.HBM)] + [vmem()] * 3,
        out_specs=vmem(),
        scratch_shapes=[pltpu.SemaphoreType.DMA],
        cost_estimate=SMALL,
        compiler_params=params(LIMIT_EARLY),
        name="tokens_with_facts",
    )(pltpu.with_memory_space_constraint(tokens, pltpu.HBM), chosen_experts.T, logits.T, tenant.reshape(1, rows))


def meta_kernel(n_local, local_halves, ids_ref, adapter_ref, pool_slot_ref, *refs):
    blocks, (p_ref, pt_ref, cols_ref, rows_ref, tslot_ref) = refs[:-5], refs[-5:]
    at = blocks[0].shape[1] - 128
    facts = jnp.concatenate([block[:, at:] for block in blocks], axis=0).astype(F32).T
    count = facts.shape[1]
    first, second, tenant = facts[0:1], facts[1:2], facts[2:3]
    logit_first = (facts[3:4] + facts[5:6]) + facts[7:8]
    logit_second = (facts[4:5] + facts[6:7]) + facts[8:9]
    weight_first = jax.nn.sigmoid(logit_first - logit_second)
    weight_second = jax.nn.sigmoid(logit_second - logit_first)
    slot = jnp.zeros_like(tenant)
    for number in range(adapter_ref.shape[0]):
        slot = jnp.where(tenant == number, pool_slot_ref[adapter_ref[number]].astype(F32), slot)
    members, weights = [], []
    for i in range(n_local):
        expert = (ids_ref[0] * local_halves // 2 + i).astype(F32)
        hit_first, hit_second = first == expert, second == expert
        members.append(jnp.where(hit_first | hit_second, 1.0, 0.0))
        weights.append(jnp.where(hit_first, weight_first, 0.0) + jnp.where(hit_second, weight_second, 0.0))
    member = jnp.concatenate(members + [jnp.zeros((8 - n_local, count), F32)], axis=0)
    before = (
        lax.broadcasted_iota(jnp.int32, (count, count), 0) < lax.broadcasted_iota(jnp.int32, (count, count), 1)
    ).astype(BF16)
    place = jnp.where(member > 0, mm(member.astype(BF16), before), -1.0)
    table = jnp.concatenate(
        [place[0:n_local]] + weights + [slot] + [jnp.zeros((127 - 2 * n_local, count), F32)], axis=0
    )
    columns = table.T
    cols_ref[...] = columns
    rows_ref[...] = table[0:8]
    row_count = p_ref.shape[1]
    tenant_rows = jnp.broadcast_to(tenant, (8, count)).astype(BF16)
    down = lax.broadcasted_iota(jnp.int32, (row_count, count), 0).astype(F32)
    across = lax.broadcasted_iota(jnp.int32, (count, row_count), 1).astype(F32)
    for i in range(n_local):
        picked = (down == place[i : i + 1]).astype(BF16)
        p_ref[i] = picked
        pt_ref[i] = (across == columns[:, i : i + 1]).astype(BF16)
        tslot_ref[i] = mm_nt(tenant_rows, picked)


def build_meta(blocks, ids, adapters, pool_slots, n_local, local_halves, row_count):
    count = sum(block.shape[0] for block in blocks)
    return pl.pallas_call(
        functools.partial(meta_kernel, n_local, local_halves),
        out_shape=(
            jax.ShapeDtypeStruct((n_local, row_count, count), BF16),
            jax.ShapeDtypeStruct((n_local, count, row_count), BF16),
            jax.ShapeDtypeStruct((count, 128), F32),
            jax.ShapeDtypeStruct((8, count), F32),
            jax.ShapeDtypeStruct((n_local, 8, row_count), F32),
        ),
        in_specs=[smem()] * 3 + [vmem()] * len(blocks),
        out_specs=(vmem(),) * 5,
        cost_estimate=SMALL,
        compiler_params=params(min(38, LIMIT_EARLY * count // 512)),
        name="routing_tables",
    )(ids, adapters, pool_slots, *blocks)


class Slabs:
    def __init__(self, gate_ref, up_ref, resident, ring, sems):
        self.sources, self.resident, self.ring, self.sems = (gate_ref, up_ref), resident, ring, sems
        self.halves, self.depth, hidden = gate_ref.shape
        self.width = resident[0].shape[2]
        self.each = resident[0].shape[0]
        self.first = len(resident) * self.each
        self.capacity = 1 if ring is None else ring.shape[0]
        self.tiles = hidden // self.width
        self.count = 2 * self.halves * self.tiles

    def place(self, number):
        if number < self.first:
            return self.resident[number // self.each].at[number % self.each]
        return self.ring.at[(number - self.first) % self.capacity]

    def copies(self, number):
        place, rows = self.place(number), self.depth // 2
        slot = number if number < self.first else (number - self.first) % self.capacity
        half, tile, which = number // (2 * self.tiles), number // 2 % self.tiles, number % 2
        return [
            pltpu.make_async_copy(
                self.sources[which].at[half, pl.ds(i * rows, rows), pl.ds(tile * self.width, self.width)],
                place.at[pl.ds(i * rows, rows)],
                self.sems.at[slot, i],
            )
            for i in range(2)
        ]

    def start(self, number):
        for copy in self.copies(number):
            copy.start()

    def wait(self, number):
        for copy in self.copies(number):
            copy.wait()


def resident_shapes(gate):
    local_halves, width, hidden_count = gate.shape
    tile = min(N_TILE, hidden_count)
    count = 2 * local_halves * hidden_count // tile
    each = min(HELD_EACH, count)
    return [(each, width, tile)] * min(HELD_ARRAYS, count // each)


def down_slabs(down, n_ad):
    return pltpu.VMEM((down.shape[0], down.shape[1], down.shape[2] // n_ad), BF16)


def down_fetch(n_ad, step, ids_ref, down_ref, into_ref, sems):
    _, rows, span = into_ref.shape
    rows = rows // 2
    start = pl.multiple_of(lax.rem(ids_ref[1] + step, n_ad) * span, span)
    return [
        pltpu.make_async_copy(
            down_ref.at[half, pl.ds(i * rows, rows), pl.ds(start, span)],
            into_ref.at[half, pl.ds(i * rows, rows)],
            sems.at[half, i],
        )
        for half in range(down_ref.shape[0])
        for i in range(2)
    ]


def prefetch_kernel(ids_ref, gate_ref, up_ref, *refs):
    resident, mark_ref, sems = refs[:-2], refs[-2], refs[-1]
    slabs = Slabs(gate_ref, up_ref, resident, None, sems)
    for number in range(slabs.first):
        slabs.start(number)
    mark_ref[...] = jnp.zeros_like(mark_ref)
    for number in range(slabs.first):
        slabs.wait(number)


def prefetch(ids, gate, up, count):
    shapes = resident_shapes(gate)
    return pl.pallas_call(
        prefetch_kernel,
        out_shape=(*[pltpu.VMEM(shape, BF16) for shape in shapes], jax.ShapeDtypeStruct((8, 128), F32)),
        in_specs=[smem()] + [pl.BlockSpec(memory_space=pltpu.HBM)] * 2,
        out_specs=(vmem(),) * (len(shapes) + 1),
        scratch_shapes=[pltpu.SemaphoreType.DMA((len(shapes) * shapes[0][0], 2))],
        cost_estimate=SMALL,
        compiler_params=params(min(38, LIMIT_EARLY * count // 512)),
        name="weight_prefetch",
    )(ids, gate, up)


def expert_kernel(n_blocks, n_resident, n_ad, step, *refs):
    blocks, refs = refs[:n_blocks], refs[n_blocks:]
    ids_ref, adapter_ref, pool_slot_ref, p_ref, tslot_ref, rows_ref = refs[1:7]
    gate_ref, up_ref, down_ref, pool_ref = refs[7:11]
    resident, refs = refs[11 : 11 + n_resident], refs[11 + n_resident :]
    hidden, low_ref, next_ref, packed, factors, factor_sems, down_sems, ring, sems = refs
    slabs = Slabs(gate_ref, up_ref, resident, ring, sems)
    n_local = p_ref.shape[0]
    local_halves, depth, _ = gate_ref.shape
    halves_each = local_halves // n_local
    tenants, rank = adapter_ref.shape[0], pool_ref.shape[2]
    factor_copies = [
        pltpu.make_async_copy(
            pool_ref.at[pool_slot_ref[adapter_ref[number]]],
            factors.at[:, number * rank : (number + 1) * rank],
            factor_sems.at[number],
        )
        for number in range(tenants)
    ]
    for copy in factor_copies:
        copy.start()
    for number in range(slabs.first, min(slabs.count, slabs.first + slabs.capacity)):
        slabs.start(number)

    def ready(number):
        if number >= slabs.first:
            slabs.wait(number)

    def used(number):
        if slabs.first <= number < slabs.count - slabs.capacity:
            slabs.start(number + slabs.capacity)

    whole = jnp.concatenate([block[:, :depth] for block in blocks], axis=0)
    for i in range(n_local):
        packed[i] = mm(p_ref[i], whole).astype(BF16)
    for half in range(local_halves):
        rows = packed[half // halves_each]
        for tile in range(slabs.tiles):
            values = []
            for which in range(2):
                number = (half * slabs.tiles + tile) * 2 + which
                ready(number)
                values.append(mm(rows, slabs.place(number)[...]))
                used(number)
            span = slice(tile * slabs.width, (tile + 1) * slabs.width)
            hidden[half, :, span] = (jax.nn.silu(values[0]) * values[1]).astype(BF16)
    down_copies = down_fetch(n_ad, step, ids_ref, down_ref, next_ref, down_sems)
    for copy in down_copies:
        copy.start()
    for copy in factor_copies:
        copy.wait()
    for i in range(n_local):
        low = mm_nt(factors[i * halves_each], hidden[i * halves_each])
        for half in range(i * halves_each + 1, (i + 1) * halves_each):
            low = low + mm_nt(factors[half], hidden[half])
        owner = tslot_ref[i][0:1]
        total = jnp.zeros((rank, low.shape[1]), F32)
        for number in range(tenants):
            total = total + jnp.where(owner == number, low[number * rank : (number + 1) * rank], 0.0)
        weight = rows_ref[n_local + i : n_local + i + 1]
        low_ref[i * rank : (i + 1) * rank] = (mm(total.astype(BF16), p_ref[i]) * weight).astype(BF16)
    for copy in down_copies:
        copy.wait()


def expert_part(
    blocks, mark, ids, adapters, pool_slots, picked, tslot, table_rows, gate, up, down, pool, resident, n_ad, step
):
    local_halves, width, hidden_count = gate.shape
    n_local, row_count, count = picked.shape
    tenants, rank = adapters.shape[0], pool.shape[2]
    hbm = pl.BlockSpec(memory_space=pltpu.HBM)
    each, _, tile = resident[0].shape
    ring = max(1, min(RING, 2 * local_halves * hidden_count // tile - len(resident) * each))
    return pl.pallas_call(
        functools.partial(expert_kernel, len(blocks), len(resident), n_ad, step),
        out_shape=(
            pltpu.VMEM((local_halves, row_count, hidden_count), BF16),
            jax.ShapeDtypeStruct((n_local * rank, count), BF16),
            down_slabs(down, n_ad),
        ),
        in_specs=[vmem()] * (len(blocks) + 1) + [smem()] * 3 + [vmem()] * 3 + [hbm] * 4 + [vmem()] * len(resident),
        out_specs=(vmem(),) * 3,
        scratch_shapes=[
            pltpu.VMEM((n_local, row_count, width), BF16),
            pltpu.VMEM((local_halves, tenants * rank, hidden_count), BF16),
            pltpu.SemaphoreType.DMA((tenants,)),
            pltpu.SemaphoreType.DMA((local_halves, 2)),
            pltpu.VMEM((ring, width, tile), BF16),
            pltpu.SemaphoreType.DMA((ring, 2)),
        ],
        cost_estimate=SMALL,
        compiler_params=params(min(38, LIMIT_EARLY * count // 512)),
        name="experts",
    )(
        *blocks, mark, ids, adapters, pool_slots, picked, tslot, table_rows, gate, up, down, pool,
        *[pltpu.with_memory_space_constraint(x, pltpu.VMEM) for x in resident],
    )


def weighted_down(hidden_ref, weight_ref, pt_ref, cols_ref):
    n_local = pt_ref.shape[0]
    halves_each = hidden_ref.shape[0] // n_local
    total = None
    for i in range(n_local):
        part_sum = mm(hidden_ref[i * halves_each], weight_ref[i * halves_each])
        for half in range(i * halves_each + 1, (i + 1) * halves_each):
            part_sum = part_sum + mm(hidden_ref[half], weight_ref[half])
        laid = mm(pt_ref[i], part_sum.astype(BF16)) * cols_ref[:, n_local + i : n_local + i + 1]
        total = laid if total is None else total + laid
    return total


def down_first_kernel(n_ad, step, ids_ref, hidden_ref, weight_ref, pt_ref, cols_ref, down_ref, keep, send, next_ref, sems):
    copies = down_fetch(n_ad, step, ids_ref, down_ref, next_ref, sems)
    for copy in copies:
        copy.start()
    write_pairs(weighted_down(hidden_ref, weight_ref, pt_ref, cols_ref), (keep, send))
    for copy in copies:
        copy.wait()


def down_first(ids, hidden, weights, pt, cols, down, n_ad, step):
    count, span = pt.shape[1], weights.shape[2]
    return pl.pallas_call(
        functools.partial(down_first_kernel, n_ad, step),
        out_shape=(jax.ShapeDtypeStruct((count // 2, span), BF16),) * 2 + (down_slabs(down, n_ad),),
        in_specs=[smem()] + [vmem()] * 4 + [pl.BlockSpec(memory_space=pltpu.HBM)],
        out_specs=(vmem(),) * 3,
        scratch_shapes=[pltpu.SemaphoreType.DMA((down.shape[0], 2))],
        cost_estimate=SMALL,
        compiler_params=params(max(LIMIT, 12 * count * span // MIB)),
        name="down_first",
    )(ids, hidden, pltpu.with_memory_space_constraint(weights, pltpu.VMEM), pt, cols, down)


def down_rest_kernel(n_ad, steps, ids_ref, hidden_ref, weight_ref, pt_ref, cols_ref, down_ref, keep, send, base, *refs):
    held, sems = refs[:-1], refs[-1]
    copies = [
        down_fetch(n_ad, step, ids_ref, down_ref, into, sems.at[number])
        for number, (step, into) in enumerate(zip(steps[1:], held))
    ]
    for copy in [copy for group in copies for copy in group]:
        copy.start()
    span = weight_ref.shape[2]
    for number in range(len(steps)):
        if number:
            for copy in copies[number - 1]:
                copy.wait()
        total = weighted_down(hidden_ref, held[number - 1] if number else weight_ref, pt_ref, cols_ref)
        if number < len(steps) - 1:
            write_pairs(total, (keep, send), number * span)
        else:
            base[...] = total


def down_rest(ids, hidden, weights, pt, cols, down, n_ad, steps):
    count, span = pt.shape[1], weights.shape[2]
    return pl.pallas_call(
        functools.partial(down_rest_kernel, n_ad, steps),
        out_shape=(jax.ShapeDtypeStruct((count // 2, span * (len(steps) - 1)), BF16),) * 2
        + (jax.ShapeDtypeStruct((count, span), F32),),
        in_specs=[smem()] + [vmem()] * 4 + [pl.BlockSpec(memory_space=pltpu.HBM)],
        out_specs=(vmem(),) * 3,
        scratch_shapes=[pltpu.VMEM(weights.shape, BF16)] * (len(steps) - 1)
        + [pltpu.SemaphoreType.DMA((len(steps) - 1, down.shape[0], 2))],
        cost_estimate=SMALL,
        compiler_params=params(max(LIMIT, 12 * count * span // MIB) + (len(steps) - 1) * weights.size * 2 // MIB),
        name="down_rest",
    )(ids, hidden, pltpu.with_memory_space_constraint(weights, pltpu.VMEM), pt, cols, down)


def write_pairs(total, outs, at=0):
    keep, send = outs
    for b in range(total.shape[0] // 128):
        block = total[b * 128 : b * 128 + 128].astype(BF16)
        (send if b % 2 else keep)[b // 2 * 128 : b // 2 * 128 + 128, pl.ds(at, total.shape[1])] = block


def adapter_kernel(slot_column, local_halves, ids_ref, base_ref, cols_ref, factor_ref, low_ref, keep, send, wide):
    blocks = base_ref.shape[0] // 128
    height = low_ref.shape[0] // blocks
    wide[...] = jnp.zeros_like(wide)
    for m in range(blocks):
        row = pl.multiple_of(((ids_ref[0] ^ m) * local_halves // 2) * RANK, RANK)
        value = low_ref[m * height : (m + 1) * height].astype(F32)
        value = jnp.concatenate([value[:, (m ^ b) * 128 : (m ^ b) * 128 + 128] for b in range(blocks)], axis=1)
        wide[pl.ds(row, height)] += value
    low = wide[...].T.astype(BF16)
    zero = jnp.zeros_like(low)
    slot = cols_ref[:, slot_column : slot_column + 1]
    depth = EXPERT_COUNT * RANK
    slot_count = factor_ref.shape[0] // depth
    total = base_ref[...]
    for j in range(0, slot_count, 2):
        spread = jnp.concatenate(
            [jnp.where(slot == (ids_ref[0] * slot_count + j + i).astype(F32), low, zero) for i in range(2)], axis=1
        )
        total = total + mm(spread, factor_ref[j * depth : (j + 2) * depth])
    write_pairs(total, (keep, send))


def adapter_part(ids, base, cols, slot_column, local_halves, factors, low):
    count, span = base.shape
    return pl.pallas_call(
        functools.partial(adapter_kernel, slot_column, local_halves),
        out_shape=(jax.ShapeDtypeStruct((count // 2, span), BF16),) * 2,
        in_specs=[smem()] + [vmem()] * 4,
        out_specs=(vmem(),) * 2,
        scratch_shapes=[pltpu.VMEM((EXPERT_COUNT * RANK, count), F32)],
        cost_estimate=SMALL,
        compiler_params=params(max(LIMIT, 24 * count * span // MIB)),
        name="adapters",
    )(ids, base, cols, factors, low)


def split_kernel(keep_ref, came_ref, keep, send):
    for b in range(keep_ref.shape[0] // 128):
        total = keep_ref[b * 128 : b * 128 + 128].astype(F32) + came_ref[b * 128 : b * 128 + 128].astype(F32)
        (send if b % 2 else keep)[b // 2 * 128 : b // 2 * 128 + 128] = total.astype(BF16)


def split_sum(keep, came):
    return pl.pallas_call(
        split_kernel,
        out_shape=(jax.ShapeDtypeStruct((keep.shape[0] // 2, keep.shape[1]), BF16),) * 2,
        in_specs=[vmem()] * 2,
        out_specs=(vmem(),) * 2,
        cost_estimate=SMALL,
        compiler_params=params(LIMIT),
        name="sum_and_split",
    )(keep, came)


def cut_kernel(edges, keep_ref, came_ref, *outs):
    for first, last, out in zip(edges, edges[1:], outs):
        out[...] = (keep_ref[:, first:last].astype(F32) + came_ref[:, first:last].astype(F32)).astype(BF16)


def cut_sum(keep, came, edges):
    return pl.pallas_call(
        functools.partial(cut_kernel, edges),
        out_shape=tuple(
            jax.ShapeDtypeStruct((keep.shape[0], last - first), BF16) for first, last in zip(edges, edges[1:])
        ),
        in_specs=[vmem()] * 2,
        out_specs=(vmem(),) * (len(edges) - 1),
        cost_estimate=SMALL,
        compiler_params=params(LIMIT),
        name="sum_and_cut",
    )(keep, came)


def per_device(
    n_ep,
    n_ad,
    tokens,
    chosen_experts,
    router_gate_logits,
    token_tenant,
    adapter_of_tenant,
    adapter_pool_slot,
    gate_weight,
    up_weight,
    down_weight,
    adapter_input_factors,
    adapter_output_factors,
):
    gate_weight, up_weight, down_weight, adapter_input_factors = [
        pltpu.with_memory_space_constraint(x, pltpu.HBM)
        for x in (gate_weight, up_weight, down_weight, adapter_input_factors)
    ]
    width = tokens.shape[1]
    span = width // n_ad
    local_halves = gate_weight.shape[0]
    n_local = max(1, local_halves // 2)
    row_count = n_ep * CAP
    bits = n_ep.bit_length() - 1
    ids = jnp.stack([lax.axis_index("ep"), lax.axis_index("ad")]).astype(jnp.int32)

    def swap(x, mask):
        return lax.ppermute(x, "ep", [(i, i ^ mask) for i in range(n_ep)])

    def tie(x, y):
        return lax.optimization_barrier((x, y))

    def shift(x, step):
        return lax.ppermute(x, "ad", [(i, (i + step) % n_ad) for i in range(n_ad)])

    order = sorted(range(1, n_ad), key=lambda step: (step != n_ad // 2, step))
    own = with_facts(tokens, chosen_experts, router_gate_logits, token_tenant)
    *resident, mark = prefetch(ids, gate_weight, up_weight, n_ep * tokens.shape[0])
    blocks = {0: own}
    for bit in reversed(range(bits)):
        for mask in list(blocks):
            blocks[mask | 1 << bit] = swap(blocks[mask], 1 << bit)
        if bit == bits - 1:
            blocks[1 << bit], mark = tie(blocks[1 << bit], mark)
    blocks = [blocks[mask] for mask in range(n_ep)]
    picked, pt, cols, table_rows, tslot = build_meta(
        blocks, ids, adapter_of_tenant, adapter_pool_slot, n_local, local_halves, row_count
    )
    hidden, low, weights = expert_part(
        blocks, mark, ids, adapter_of_tenant, adapter_pool_slot, picked, tslot, table_rows, gate_weight, up_weight,
        down_weight, adapter_input_factors, resident, n_ad, order[0],
    )

    def onward(keep, came, first=1):
        for bit in range(first, bits):
            keep, send = split_sum(keep, came)
            came = swap(send, 1 << bit)
        return keep, came

    def other_of(low, bit):
        return lax.ppermute(low, "ad", [(i, i ^ 1 << bit) for i in range(n_ad)])

    def added(x, y):
        return (x.astype(F32) + y.astype(F32)).astype(BF16)

    far_steps = range(1, n_ad.bit_length() - 1)
    others = [other_of(low, bit) for bit in far_steps[:1]]
    keep, send, weights = down_first(ids, hidden, weights, pt, cols, down_weight, n_ad, order[1])
    others, keep, send, weights = lax.optimization_barrier((others, keep, send, weights))
    for bit in far_steps:
        low = added(low, others[0] if bit == 1 else other_of(low, bit))
    for bit in range(bits - 1):
        low = jnp.concatenate([low, swap(low, 1 << bit)], axis=0)
    crossed = swap(low, 1 << (bits - 1))
    keep, came = onward(keep, swap(send, 1), 1)
    keep, hidden = tie(keep, hidden)
    keep_rest, send_rest, base = down_rest(ids, hidden, weights, pt, cols, down_weight, n_ad, (*order[1:], 0))
    came, crossed, keep_rest, send_rest, base = lax.optimization_barrier((came, crossed, keep_rest, send_rest, base))
    low = jnp.concatenate([low, crossed], axis=0)
    low = added(low, other_of(low, 0))
    (sums,) = cut_sum(keep, came, (0, span))
    results = [shift(sums, order[0])]
    keep_rest, came_rest = onward(keep_rest, swap(send_rest, 1))
    slot_count = adapter_output_factors.shape[0]
    flat_factors = adapter_output_factors.reshape(slot_count * EXPERT_COUNT * RANK, span)
    keep, send = adapter_part(ids, base, cols, 2 * n_local, local_halves, flat_factors, low)
    came_rest, keep, send = lax.optimization_barrier((came_rest, keep, send))
    came = swap(send, 1)
    if bits > 1:
        keep, send = split_sum(keep, came)
        came_rest, keep, send = lax.optimization_barrier((came_rest, keep, send))
        came = swap(send, 2)
    keep, came = onward(keep, came, 2)
    parts = cut_sum(keep_rest, came_rest, [span * i for i in range(n_ad - 1)])
    results += [shift(x, step) for x, step in zip(parts, order[1:])]
    return sum(x.astype(F32) for x in [keep, came] + results).astype(BF16)


def solution(mesh):
    placed = (
        P(("rep", "ep"), None),
        P(("rep", "ep"), None),
        P(("rep", "ep"), None),
        P(("rep", "ep")),
        P("rep"),
        P(),
        P("ep", None, "ad"),
        P("ep", None, "ad"),
        P("ep", "ad", None),
        P(None, "ep", None, "ad"),
        P("ep", None, None, "ad"),
    )
    return jax.shard_map(
        functools.partial(per_device, mesh.shape["ep"], mesh.shape["ad"]),
        mesh=mesh,
        in_specs=placed,
        out_specs=P(("rep", "ep"), "ad"),
        check_vma=False,
    )
```

```python
import functools
import math

import jax
import jax.numpy as jnp
from jax import lax
from jax.experimental import pallas as pl
from jax.experimental.pallas import tpu as pltpu
from jax.sharding import PartitionSpec as P

EXPERT_COUNT = 8
TOP = 2
RANK = 16
CAP = 48
LIMIT = 16
LIMIT_EARLY = 8
N_TILE = 512
MIB = 1 << 20

F32 = jnp.float32
BF16 = jnp.bfloat16


def mm(a, b):
    return jnp.dot(a, b, preferred_element_type=F32)


def mm_nt(a, b):
    return lax.dot_general(a, b, (((1,), (1,)), ((), ())), preferred_element_type=F32)


SMALL = pl.CostEstimate(flops=1, bytes_accessed=1, transcendentals=0)


def params(mib):
    return pltpu.CompilerParams(vmem_limit_bytes=mib * MIB)


def vmem():
    return pl.BlockSpec(memory_space=pltpu.VMEM)


def smem():
    return pl.BlockSpec(memory_space=pltpu.SMEM)


def parts_kernel(tokens_ref, chosen_ref, logits_ref, tenant_ref, first_ref, second_ref, sems):
    rows, width = second_ref.shape
    copies = [
        pltpu.make_async_copy(tokens_ref.at[:, pl.ds(0, width)], first_ref.at[:, pl.ds(0, width)], sems.at[0]),
        pltpu.make_async_copy(tokens_ref.at[:, pl.ds(width, width)], second_ref, sems.at[1]),
    ]
    for copy in copies:
        copy.start()
    diagonal = lax.broadcasted_iota(jnp.int32, (rows, rows), 0) == lax.broadcasted_iota(jnp.int32, (rows, rows), 1)

    def column(row):
        return jnp.sum(jnp.where(diagonal, row, 0.0), axis=1, keepdims=True)

    chosen, logits = chosen_ref[...].astype(F32), logits_ref[...]
    columns = [column(chosen[0:1]), column(chosen[1:2]), column(tenant_ref[...].astype(F32))]
    rests = [column(logits[0:1]), column(logits[1:2])]
    for _ in range(3):
        pieces = [rest.astype(BF16).astype(F32) for rest in rests]
        columns += pieces
        rests = [rest - piece for rest, piece in zip(rests, pieces)]
    lane = lax.broadcasted_iota(jnp.int32, (rows, 128), 1)
    facts = jnp.zeros((rows, 128), F32)
    for number, value in enumerate(columns):
        facts = jnp.where(lane == number, value, facts)
    first_ref[:, width:] = facts.astype(BF16)
    for copy in copies:
        copy.wait()


def token_parts_of(tokens, chosen_experts, logits, tenant):
    rows, width = tokens.shape[0], tokens.shape[1] // 2
    return pl.pallas_call(
        parts_kernel,
        out_shape=(
            jax.ShapeDtypeStruct((rows, width + 128), BF16),
            jax.ShapeDtypeStruct((rows, width), BF16),
        ),
        in_specs=[pl.BlockSpec(memory_space=pltpu.HBM)] + [vmem()] * 3,
        out_specs=(vmem(),) * 2,
        scratch_shapes=[pltpu.SemaphoreType.DMA((2,))],
        cost_estimate=SMALL,
        compiler_params=params(LIMIT_EARLY),
        name="token_parts",
    )(pltpu.with_memory_space_constraint(tokens, pltpu.HBM), chosen_experts.T, logits.T, tenant.reshape(1, rows))


def meta_kernel(n_local, local_halves, ids_ref, adapter_ref, pool_slot_ref, *refs):
    blocks, (p_ref, pt_ref, cols_ref, rows_ref, tslot_ref) = refs[:-5], refs[-5:]
    at = blocks[0].shape[1] - 128
    facts = jnp.concatenate([block[:, at:] for block in blocks], axis=0).astype(F32).T
    count = facts.shape[1]
    first, second, tenant = facts[0:1], facts[1:2], facts[2:3]
    logit_first = (facts[3:4] + facts[5:6]) + facts[7:8]
    logit_second = (facts[4:5] + facts[6:7]) + facts[8:9]
    weight_first = jax.nn.sigmoid(logit_first - logit_second)
    weight_second = jax.nn.sigmoid(logit_second - logit_first)
    slot = jnp.zeros_like(tenant)
    for number in range(adapter_ref.shape[0]):
        slot = jnp.where(tenant == number, pool_slot_ref[adapter_ref[number]].astype(F32), slot)
    members, weights = [], []
    for i in range(n_local):
        expert = (ids_ref[0] * local_halves // 2 + i).astype(F32)
        hit_first, hit_second = first == expert, second == expert
        members.append(jnp.where(hit_first | hit_second, 1.0, 0.0))
        weights.append(jnp.where(hit_first, weight_first, 0.0) + jnp.where(hit_second, weight_second, 0.0))
    member = jnp.concatenate(members + [jnp.zeros((8 - n_local, count), F32)], axis=0)
    before = (
        lax.broadcasted_iota(jnp.int32, (count, count), 0) < lax.broadcasted_iota(jnp.int32, (count, count), 1)
    ).astype(BF16)
    place = jnp.where(member > 0, mm(member.astype(BF16), before), -1.0)
    table = jnp.concatenate(
        [place[0:n_local]] + weights + [slot] + [jnp.zeros((127 - 2 * n_local, count), F32)], axis=0
    )
    columns = table.T
    cols_ref[...] = columns
    rows_ref[...] = table[0:8]
    row_count = p_ref.shape[1]
    tenant_rows = jnp.broadcast_to(tenant, (8, count)).astype(BF16)
    down = lax.broadcasted_iota(jnp.int32, (row_count, count), 0).astype(F32)
    across = lax.broadcasted_iota(jnp.int32, (count, row_count), 1).astype(F32)
    for i in range(n_local):
        picked = (down == place[i : i + 1]).astype(BF16)
        p_ref[i] = picked
        pt_ref[i] = (across == columns[:, i : i + 1]).astype(BF16)
        tslot_ref[i] = mm_nt(tenant_rows, picked)


def build_meta(blocks, ids, adapters, pool_slots, n_local, local_halves, row_count):
    count = sum(block.shape[0] for block in blocks)
    return pl.pallas_call(
        functools.partial(meta_kernel, n_local, local_halves),
        out_shape=(
            jax.ShapeDtypeStruct((n_local, row_count, count), BF16),
            jax.ShapeDtypeStruct((n_local, count, row_count), BF16),
            jax.ShapeDtypeStruct((count, 128), F32),
            jax.ShapeDtypeStruct((8, count), F32),
            jax.ShapeDtypeStruct((n_local, 8, row_count), F32),
        ),
        in_specs=[smem()] * 3 + [vmem()] * len(blocks),
        out_specs=(vmem(),) * 5,
        cost_estimate=SMALL,
        compiler_params=params(max(LIMIT_EARLY, 12 * count * count // MIB)),
        name="routing_tables",
    )(ids, adapters, pool_slots, *blocks)


def slab_copies(gate_ref, up_ref, into_ref, sems, part, half):
    depth, width = into_ref.shape[1], into_ref.shape[2]
    copies = []
    for number in range(into_ref.shape[0]):
        source = (gate_ref, up_ref)[number % 2].at[half, pl.ds(part * depth, depth), pl.ds(number // 2 * width, width)]
        copies.append(pltpu.make_async_copy(source, into_ref.at[number], sems.at[half, number]))
    return copies


def prefetch_kernel(ids_ref, gate_ref, up_ref, *refs):
    slabs, mark_ref, sems = refs[:-2], refs[-2], refs[-1]
    copies = [copy for half, slab in enumerate(slabs) for copy in slab_copies(gate_ref, up_ref, slab, sems, 0, half)]
    for copy in copies:
        copy.start()
    mark_ref[...] = jnp.zeros_like(mark_ref)
    for copy in copies:
        copy.wait()


def prefetch(ids, gate, up, part_width):
    local_halves, _, hidden_count = gate.shape
    tile = min(N_TILE, hidden_count)
    each = 2 * hidden_count // tile
    return pl.pallas_call(
        prefetch_kernel,
        out_shape=(pltpu.VMEM((each, part_width, tile), BF16),) * local_halves + (jax.ShapeDtypeStruct((8, 128), F32),),
        in_specs=[smem()] + [pl.BlockSpec(memory_space=pltpu.HBM)] * 2,
        out_specs=(vmem(),) * (local_halves + 1),
        scratch_shapes=[pltpu.SemaphoreType.DMA((local_halves, each))],
        cost_estimate=SMALL,
        compiler_params=params(LIMIT_EARLY),
        name="weight_prefetch",
    )(ids, gate, up)


def pack(blocks, p_ref, packed):
    depth = packed.shape[2]
    whole = jnp.concatenate([block[:, :depth] for block in blocks], axis=0)
    for i in range(p_ref.shape[0]):
        packed[i] = mm(p_ref[i], whole).astype(BF16)


def down_slabs(down, n_ad):
    return pltpu.VMEM((down.shape[0], down.shape[1], down.shape[2] // n_ad), BF16)


def down_fetch(n_ad, step, ids_ref, down_ref, into_ref, sems):
    _, rows, span = into_ref.shape
    rows = rows // 2
    start = pl.multiple_of(lax.rem(ids_ref[1] + step, n_ad) * span, span)
    return [
        pltpu.make_async_copy(
            down_ref.at[half, pl.ds(i * rows, rows), pl.ds(start, span)],
            into_ref.at[half, pl.ds(i * rows, rows)],
            sems.at[half, i],
        )
        for half in range(down_ref.shape[0])
        for i in range(2)
    ]


def first_kernel(n_blocks, local_halves, *refs):
    blocks, refs = refs[:n_blocks], refs[n_blocks:]
    _, p_ref, gate_ref, up_ref, refs = *refs[:4], refs[4:]
    slabs, refs = refs[:local_halves], refs[local_halves:]
    ahead, (gate_out, up_out, mark_out, packed, sems) = refs[:-5], refs[-5:]
    mark_out[...] = jnp.zeros_like(mark_out)
    pack(blocks, p_ref, packed)
    slabs = list(ahead) + list(slabs[len(ahead) :])
    copies = [slab_copies(gate_ref, up_ref, slab, sems, 1, half) for half, slab in enumerate(ahead)]
    halves_each = local_halves // p_ref.shape[0]
    for half in range(local_halves):
        rows = packed[half // halves_each]
        tiles, _, width = slabs[half].shape
        for tile in range(tiles // 2):
            span = slice(tile * width, (tile + 1) * width)
            gate_out[half, :, span] = mm(rows, slabs[half][2 * tile])
            up_out[half, :, span] = mm(rows, slabs[half][2 * tile + 1])
            if half < len(ahead):
                copies[half][2 * tile].start()
                copies[half][2 * tile + 1].start()
    for copy in [copy for half in copies for copy in half]:
        copy.wait()


def first_part(blocks, mark, picked, gate, up, slabs):
    local_halves, _, hidden_count = gate.shape
    n_local, row_count, _ = picked.shape
    each, part_width, _ = slabs[0].shape
    hbm = pl.BlockSpec(memory_space=pltpu.HBM)
    sums = pltpu.VMEM((local_halves, row_count, hidden_count), F32)
    n_ahead = max(1, local_halves - 1)
    return pl.pallas_call(
        functools.partial(first_kernel, len(blocks), local_halves),
        out_shape=(pltpu.VMEM(slabs[0].shape, BF16),) * n_ahead
        + (sums, sums, jax.ShapeDtypeStruct((8, 128), F32)),
        in_specs=[vmem()] * (len(blocks) + 2) + [hbm, hbm] + [vmem()] * local_halves,
        out_specs=(vmem(),) * (n_ahead + 3),
        scratch_shapes=[
            pltpu.VMEM((n_local, row_count, part_width), BF16),
            pltpu.SemaphoreType.DMA((n_ahead, each)),
        ],
        input_output_aliases={len(blocks) + 4 + half: half for half in range(n_ahead)},
        cost_estimate=SMALL,
        compiler_params=params(max(LIMIT_EARLY, 10 * n_local * row_count * part_width // MIB)),
        name="gate_up_first",
    )(*blocks, mark, picked, gate, up, *[pltpu.with_memory_space_constraint(x, pltpu.VMEM) for x in slabs])


def second_kernel(n_blocks, n_ahead, n_ad, step, *refs):
    blocks, refs = refs[:n_blocks], refs[n_blocks:]
    p_ref, gate_ref, up_ref, refs = *refs[1:4], refs[4:]
    ahead, gate_in, up_in, refs = refs[:n_ahead], refs[n_ahead], refs[n_ahead + 1], refs[n_ahead + 2 :]
    ids_ref, adapter_ref, pool_slot_ref, pool_ref, tslot_ref, rows_ref, down_ref, refs = *refs[:7], refs[7:]
    hidden_ref, low_ref, next_ref, packed, factors, factor_sems, down_sems, late, sems = refs
    n_local = p_ref.shape[0]
    local_halves, _, hidden_count = gate_ref.shape
    halves_each = local_halves // n_local
    slabs = list(ahead) + [late] * (local_halves - n_ahead)
    copies = {
        half: slab_copies(gate_ref, up_ref, slabs[half], sems, 1, half) for half in range(n_ahead, local_halves)
    }
    tenants, rank = adapter_ref.shape[0], pool_ref.shape[2]
    factor_copies = [
        pltpu.make_async_copy(
            pool_ref.at[pool_slot_ref[adapter_ref[number]]],
            factors.at[:, number * rank : (number + 1) * rank],
            factor_sems.at[number],
        )
        for number in range(tenants)
    ]
    down_copies = down_fetch(n_ad, step, ids_ref, down_ref, next_ref, down_sems)
    for copy in copies.get(n_ahead, []) + factor_copies + down_copies:
        copy.start()
    pack(blocks, p_ref, packed)
    for half in range(local_halves):
        rows = packed[half // halves_each]
        tiles, _, width = slabs[half].shape
        for tile in range(tiles // 2):
            span = slice(tile * width, (tile + 1) * width)
            values = []
            for number in (2 * tile, 2 * tile + 1):
                if half in copies:
                    copies[half][number].wait()
                values.append(mm(rows, slabs[half][number]))
                if half in copies and half + 1 in copies:
                    copies[half + 1][number].start()
            gate = values[0] + gate_in[half, :, span]
            up = values[1] + up_in[half, :, span]
            hidden_ref[half, :, span] = (jax.nn.silu(gate) * up).astype(BF16)
    for copy in factor_copies:
        copy.wait()
    for i in range(n_local):
        low = mm_nt(factors[i * halves_each], hidden_ref[i * halves_each])
        for half in range(i * halves_each + 1, (i + 1) * halves_each):
            low = low + mm_nt(factors[half], hidden_ref[half])
        owner = tslot_ref[i][0:1]
        total = jnp.zeros((rank, low.shape[1]), F32)
        for number in range(tenants):
            total = total + jnp.where(owner == number, low[number * rank : (number + 1) * rank], 0.0)
        weight = rows_ref[n_local + i : n_local + i + 1]
        low_ref[i * rank : (i + 1) * rank] = (mm(total.astype(BF16), p_ref[i]) * weight).astype(BF16)
    for copy in down_copies:
        copy.wait()


def second_part(
    blocks, mark, picked, gate, up, ahead, sums, ids, adapters, pool_slots, pool, tslot, table_rows, down, n_ad, step
):
    local_halves, _, hidden_count = gate.shape
    n_local, row_count, count = picked.shape
    each, part_width, tile = ahead[0].shape
    tenants, rank = adapters.shape[0], pool.shape[2]
    hbm = pl.BlockSpec(memory_space=pltpu.HBM)
    held = [pltpu.with_memory_space_constraint(x, pltpu.VMEM) for x in (*ahead, *sums)]
    late_bytes = 2 * each * part_width * tile
    return pl.pallas_call(
        functools.partial(second_kernel, len(blocks), len(ahead), n_ad, step),
        out_shape=(
            pltpu.VMEM((local_halves, row_count, hidden_count), BF16),
            jax.ShapeDtypeStruct((n_local * rank, count), BF16),
            down_slabs(down, n_ad),
        ),
        in_specs=[vmem()] * (len(blocks) + 2) + [hbm, hbm] + [vmem()] * len(held) + [smem()] * 3 + [hbm, vmem(), vmem(), hbm],
        out_specs=(vmem(),) * 3,
        scratch_shapes=[
            pltpu.VMEM((n_local, row_count, part_width), BF16),
            pltpu.VMEM((local_halves, tenants * rank, hidden_count), BF16),
            pltpu.SemaphoreType.DMA((tenants,)),
            pltpu.SemaphoreType.DMA((local_halves, 2)),
            pltpu.VMEM((each, part_width, tile), BF16),
            pltpu.SemaphoreType.DMA((local_halves, each)),
        ],
        cost_estimate=SMALL,
        compiler_params=params(
            max(LIMIT_EARLY, 10 * n_local * row_count * part_width // MIB) + late_bytes // MIB + 1
        ),
        name="gate_up_second",
    )(*blocks, mark, picked, gate, up, *held, ids, adapters, pool_slots, pool, tslot, table_rows, down)


def weighted_down(hidden_ref, weight_ref, pt_ref, cols_ref):
    n_local = pt_ref.shape[0]
    halves_each = hidden_ref.shape[0] // n_local
    total = None
    for i in range(n_local):
        part_sum = mm(hidden_ref[i * halves_each], weight_ref[i * halves_each])
        for half in range(i * halves_each + 1, (i + 1) * halves_each):
            part_sum = part_sum + mm(hidden_ref[half], weight_ref[half])
        laid = mm(pt_ref[i], part_sum.astype(BF16)) * cols_ref[:, n_local + i : n_local + i + 1]
        total = laid if total is None else total + laid
    return total


def down_first_kernel(n_ad, step, ids_ref, hidden_ref, weight_ref, pt_ref, cols_ref, down_ref, keep, send, next_ref, sems):
    copies = down_fetch(n_ad, step, ids_ref, down_ref, next_ref, sems)
    for copy in copies:
        copy.start()
    write_pairs(weighted_down(hidden_ref, weight_ref, pt_ref, cols_ref), (keep, send))
    for copy in copies:
        copy.wait()


def down_first(ids, hidden, weights, pt, cols, down, n_ad, step):
    count, span = pt.shape[1], weights.shape[2]
    return pl.pallas_call(
        functools.partial(down_first_kernel, n_ad, step),
        out_shape=(jax.ShapeDtypeStruct((count // 2, span), BF16),) * 2 + (down_slabs(down, n_ad),),
        in_specs=[smem()] + [vmem()] * 4 + [pl.BlockSpec(memory_space=pltpu.HBM)],
        out_specs=(vmem(),) * 3,
        scratch_shapes=[pltpu.SemaphoreType.DMA((down.shape[0], 2))],
        cost_estimate=SMALL,
        compiler_params=params(max(LIMIT, 12 * count * span // MIB)),
        name="down_first",
    )(ids, hidden, pltpu.with_memory_space_constraint(weights, pltpu.VMEM), pt, cols, down)


def down_rest_kernel(n_ad, steps, ids_ref, hidden_ref, weight_ref, pt_ref, cols_ref, down_ref, keep, send, base, *refs):
    held, sems = refs[:-1], refs[-1]
    copies = [
        down_fetch(n_ad, step, ids_ref, down_ref, into, sems.at[number])
        for number, (step, into) in enumerate(zip(steps[1:], held))
    ]
    for copy in [copy for group in copies for copy in group]:
        copy.start()
    span = weight_ref.shape[2]
    for number in range(len(steps)):
        if number:
            for copy in copies[number - 1]:
                copy.wait()
        total = weighted_down(hidden_ref, held[number - 1] if number else weight_ref, pt_ref, cols_ref)
        if number < len(steps) - 1:
            write_pairs(total, (keep, send), number * span)
        else:
            base[...] = total


def down_rest(ids, hidden, weights, pt, cols, down, n_ad, steps):
    count, span = pt.shape[1], weights.shape[2]
    return pl.pallas_call(
        functools.partial(down_rest_kernel, n_ad, steps),
        out_shape=(jax.ShapeDtypeStruct((count // 2, span * (len(steps) - 1)), BF16),) * 2
        + (jax.ShapeDtypeStruct((count, span), F32),),
        in_specs=[smem()] + [vmem()] * 4 + [pl.BlockSpec(memory_space=pltpu.HBM)],
        out_specs=(vmem(),) * 3,
        scratch_shapes=[pltpu.VMEM(weights.shape, BF16)] * (len(steps) - 1)
        + [pltpu.SemaphoreType.DMA((len(steps) - 1, down.shape[0], 2))],
        cost_estimate=SMALL,
        compiler_params=params(max(LIMIT, 12 * count * span // MIB) + (len(steps) - 1) * weights.size * 2 // MIB),
        name="down_rest",
    )(ids, hidden, pltpu.with_memory_space_constraint(weights, pltpu.VMEM), pt, cols, down)


def write_pairs(total, outs, at=0):
    keep, send = outs
    for b in range(total.shape[0] // 128):
        block = total[b * 128 : b * 128 + 128].astype(BF16)
        (send if b % 2 else keep)[b // 2 * 128 : b // 2 * 128 + 128, pl.ds(at, total.shape[1])] = block


def adapter_kernel(slot_column, local_halves, ids_ref, base_ref, cols_ref, factor_ref, low_ref, keep, send, wide):
    blocks = base_ref.shape[0] // 128
    height = low_ref.shape[0] // blocks
    wide[...] = jnp.zeros_like(wide)
    for m in range(blocks):
        row = pl.multiple_of(((ids_ref[0] ^ m) * local_halves // 2) * RANK, RANK)
        value = low_ref[m * height : (m + 1) * height].astype(F32)
        value = jnp.concatenate([value[:, (m ^ b) * 128 : (m ^ b) * 128 + 128] for b in range(blocks)], axis=1)
        wide[pl.ds(row, height)] += value
    low = wide[...].T.astype(BF16)
    zero = jnp.zeros_like(low)
    slot = cols_ref[:, slot_column : slot_column + 1]
    depth = EXPERT_COUNT * RANK
    slot_count = factor_ref.shape[0] // depth
    total = base_ref[...]
    for j in range(0, slot_count, 2):
        spread = jnp.concatenate(
            [jnp.where(slot == (ids_ref[0] * slot_count + j + i).astype(F32), low, zero) for i in range(2)], axis=1
        )
        total = total + mm(spread, factor_ref[j * depth : (j + 2) * depth])
    write_pairs(total, (keep, send))


def adapter_part(ids, base, cols, slot_column, local_halves, factors, low):
    count, span = base.shape
    return pl.pallas_call(
        functools.partial(adapter_kernel, slot_column, local_halves),
        out_shape=(jax.ShapeDtypeStruct((count // 2, span), BF16),) * 2,
        in_specs=[smem()] + [vmem()] * 4,
        out_specs=(vmem(),) * 2,
        scratch_shapes=[pltpu.VMEM((EXPERT_COUNT * RANK, count), F32)],
        cost_estimate=SMALL,
        compiler_params=params(max(LIMIT, 24 * count * span // MIB)),
        name="adapters",
    )(ids, base, cols, factors, low)


def split_kernel(keep_ref, came_ref, keep, send):
    for b in range(keep_ref.shape[0] // 128):
        total = keep_ref[b * 128 : b * 128 + 128].astype(F32) + came_ref[b * 128 : b * 128 + 128].astype(F32)
        (send if b % 2 else keep)[b // 2 * 128 : b // 2 * 128 + 128] = total.astype(BF16)


def split_sum(keep, came):
    return pl.pallas_call(
        split_kernel,
        out_shape=(jax.ShapeDtypeStruct((keep.shape[0] // 2, keep.shape[1]), BF16),) * 2,
        in_specs=[vmem()] * 2,
        out_specs=(vmem(),) * 2,
        cost_estimate=SMALL,
        compiler_params=params(LIMIT),
        name="sum_and_split",
    )(keep, came)


def cut_kernel(edges, keep_ref, came_ref, *outs):
    for first, last, out in zip(edges, edges[1:], outs):
        out[...] = (keep_ref[:, first:last].astype(F32) + came_ref[:, first:last].astype(F32)).astype(BF16)


def cut_sum(keep, came, edges):
    return pl.pallas_call(
        functools.partial(cut_kernel, edges),
        out_shape=tuple(
            jax.ShapeDtypeStruct((keep.shape[0], last - first), BF16) for first, last in zip(edges, edges[1:])
        ),
        in_specs=[vmem()] * 2,
        out_specs=(vmem(),) * (len(edges) - 1),
        cost_estimate=SMALL,
        compiler_params=params(LIMIT),
        name="sum_and_cut",
    )(keep, came)


def per_device(
    n_ep,
    n_ad,
    tokens,
    chosen_experts,
    router_gate_logits,
    token_tenant,
    adapter_of_tenant,
    adapter_pool_slot,
    gate_weight,
    up_weight,
    down_weight,
    adapter_input_factors,
    adapter_output_factors,
):
    gate_weight, up_weight, down_weight, adapter_input_factors = [
        pltpu.with_memory_space_constraint(x, pltpu.HBM)
        for x in (gate_weight, up_weight, down_weight, adapter_input_factors)
    ]
    width = tokens.shape[1]
    span = width // n_ad
    local_halves = gate_weight.shape[0]
    n_local = max(1, local_halves // 2)
    row_count = n_ep * CAP
    bits = n_ep.bit_length() - 1
    ids = jnp.stack([lax.axis_index("ep"), lax.axis_index("ad")]).astype(jnp.int32)

    def swap(x, mask):
        return lax.ppermute(x, "ep", [(i, i ^ mask) for i in range(n_ep)])

    def tie(x, y):
        return lax.optimization_barrier((x, y))

    def shift(x, step):
        return lax.ppermute(x, "ad", [(i, (i + step) % n_ad) for i in range(n_ad)])

    order = sorted(range(1, n_ad), key=lambda step: (step != n_ad // 2, step))
    token_part = token_parts_of(tokens, chosen_experts, router_gate_logits, token_tenant)
    *slabs, mark = prefetch(ids, gate_weight, up_weight, width // 2)
    high = 1 << (bits - 1)
    crossing = [swap(own, high) for own in token_part]

    def spread(part, crossed):
        blocks = {0: token_part[part], high: crossed}
        for bit in reversed(range(bits - 1)):
            for mask in list(blocks):
                blocks[mask | 1 << bit] = swap(blocks[mask], 1 << bit)
        return [blocks[mask] for mask in range(n_ep)]

    crossing[0], mark = tie(crossing[0], mark)
    blocks = spread(0, crossing[0])
    picked, pt, cols, table_rows, tslot = build_meta(
        blocks, ids, adapter_of_tenant, adapter_pool_slot, n_local, local_halves, row_count
    )
    *ahead, gate_sum, up_sum, mark = first_part(blocks, mark, picked, gate_weight, up_weight, slabs)
    crossing[1], mark = tie(crossing[1], mark)
    hidden, low, weights = second_part(
        spread(1, crossing[1]), mark, picked, gate_weight, up_weight, ahead, (gate_sum, up_sum), ids,
        adapter_of_tenant, adapter_pool_slot, adapter_input_factors, tslot, table_rows, down_weight, n_ad, order[0],
    )

    def onward(keep, came, first=1):
        for bit in range(first, bits):
            keep, send = split_sum(keep, came)
            came = swap(send, 1 << bit)
        return keep, came

    def other_of(low, bit):
        return lax.ppermute(low, "ad", [(i, i ^ 1 << bit) for i in range(n_ad)])

    def added(x, y):
        return (x.astype(F32) + y.astype(F32)).astype(BF16)

    far_steps = range(1, n_ad.bit_length() - 1)
    others = [other_of(low, bit) for bit in far_steps[:1]]
    keep, send, weights = down_first(ids, hidden, weights, pt, cols, down_weight, n_ad, order[1])
    others, keep, send, weights = lax.optimization_barrier((others, keep, send, weights))
    for bit in far_steps:
        low = added(low, others[0] if bit == 1 else other_of(low, bit))
    for bit in range(bits - 1):
        low = jnp.concatenate([low, swap(low, 1 << bit)], axis=0)
    crossed = swap(low, 1 << (bits - 1))
    keep, came = onward(keep, swap(send, 1), 1)
    keep, hidden = tie(keep, hidden)
    keep_rest, send_rest, base = down_rest(ids, hidden, weights, pt, cols, down_weight, n_ad, (*order[1:], 0))
    came, crossed, keep_rest, send_rest, base = lax.optimization_barrier((came, crossed, keep_rest, send_rest, base))
    low = jnp.concatenate([low, crossed], axis=0)
    low = added(low, other_of(low, 0))
    (sums,) = cut_sum(keep, came, (0, span))
    results = [shift(sums, order[0])]
    keep_rest, came_rest = onward(keep_rest, swap(send_rest, 1))
    slot_count = adapter_output_factors.shape[0]
    flat_factors = adapter_output_factors.reshape(slot_count * EXPERT_COUNT * RANK, span)
    keep, send = adapter_part(ids, base, cols, 2 * n_local, local_halves, flat_factors, low)
    came_rest, results, keep, send = lax.optimization_barrier((came_rest, results, keep, send))
    came = swap(send, 1)
    if bits > 1:
        keep, send = split_sum(keep, came)
        came_rest, keep, send = lax.optimization_barrier((came_rest, keep, send))
        came = swap(send, 2)
    keep, came = onward(keep, came, 2)
    parts = cut_sum(keep_rest, came_rest, [span * i for i in range(n_ad - 1)])
    results += [shift(x, step) for x, step in zip(parts, order[1:])]
    return sum(x.astype(F32) for x in [keep, came] + results).astype(BF16)


def solution(mesh):
    placed = (
        P(("rep", "ep"), None),
        P(("rep", "ep"), None),
        P(("rep", "ep"), None),
        P(("rep", "ep")),
        P("rep"),
        P(),
        P("ep", None, "ad"),
        P("ep", None, "ad"),
        P("ep", "ad", None),
        P(None, "ep", None, "ad"),
        P("ep", None, None, "ad"),
    )
    return jax.shard_map(
        functools.partial(per_device, mesh.shape["ep"], mesh.shape["ad"]),
        mesh=mesh,
        in_specs=placed,
        out_specs=P(("rep", "ep"), "ad"),
        check_vma=False,
    )
```

```python
import functools
import math

import jax
import jax.numpy as jnp
from jax import lax
from jax.experimental import pallas as pl
from jax.experimental.pallas import tpu as pltpu
from jax.sharding import PartitionSpec as P

EXPERT_COUNT = 8
TOP = 2
RANK = 16
CAP = 48
LIMIT = 16
LIMIT_EARLY = 8
N_TILE = 512
MIB = 1 << 20

F32 = jnp.float32
BF16 = jnp.bfloat16


def mm(a, b):
    return jnp.dot(a, b, preferred_element_type=F32)


def mm_nt(a, b):
    return lax.dot_general(a, b, (((1,), (1,)), ((), ())), preferred_element_type=F32)


SMALL = pl.CostEstimate(flops=1, bytes_accessed=1, transcendentals=0)


def silu(x):
    half = 0.5 * x
    return half + half * jnp.tanh(half)


def params(mib):
    return pltpu.CompilerParams(vmem_limit_bytes=mib * MIB)


def vmem():
    return pl.BlockSpec(memory_space=pltpu.VMEM)


def smem():
    return pl.BlockSpec(memory_space=pltpu.SMEM)


def parts_kernel(tokens_ref, chosen_in, logits_in, tenant_in, first_ref, second_ref, chosen_ref, logits_ref, tenant_ref, sems):
    rows, width = second_ref.shape
    copies = [
        pltpu.make_async_copy(tokens_ref.at[:, pl.ds(0, width)], first_ref.at[:, pl.ds(0, width)], sems.at[0]),
        pltpu.make_async_copy(tokens_ref.at[:, pl.ds(width, width)], second_ref, sems.at[1]),
    ]
    small = [
        pltpu.make_async_copy(source, into, sems.at[2 + number])
        for number, (source, into) in enumerate(
            [(chosen_in, chosen_ref), (logits_in, logits_ref), (tenant_in, tenant_ref)]
        )
    ]
    for copy in small + copies:
        copy.start()
    for copy in small:
        copy.wait()
    diagonal = lax.broadcasted_iota(jnp.int32, (rows, rows), 0) == lax.broadcasted_iota(jnp.int32, (rows, rows), 1)

    def column(row):
        return jnp.sum(jnp.where(diagonal, row, 0.0), axis=1, keepdims=True)

    chosen, logits = chosen_ref[...].astype(F32), logits_ref[...]
    columns = [column(chosen[0:1]), column(chosen[1:2]), column(tenant_ref[...].astype(F32))]
    rests = [column(logits[0:1]), column(logits[1:2])]
    for _ in range(3):
        pieces = [rest.astype(BF16).astype(F32) for rest in rests]
        columns += pieces
        rests = [rest - piece for rest, piece in zip(rests, pieces)]
    lane = lax.broadcasted_iota(jnp.int32, (rows, 128), 1)
    facts = jnp.zeros((rows, 128), F32)
    for number, value in enumerate(columns):
        facts = jnp.where(lane == number, value, facts)
    first_ref[:, width:] = facts.astype(BF16)
    for copy in copies:
        copy.wait()


def token_parts_of(tokens, chosen_experts, logits, tenant):
    rows, width = tokens.shape[0], tokens.shape[1] // 2
    return pl.pallas_call(
        parts_kernel,
        out_shape=(
            jax.ShapeDtypeStruct((rows, width + 128), BF16),
            jax.ShapeDtypeStruct((rows, width), BF16),
        ),
        in_specs=[pl.BlockSpec(memory_space=pltpu.HBM)] * 4,
        out_specs=(vmem(),) * 2,
        scratch_shapes=[
            pltpu.VMEM((2, rows), jnp.int32),
            pltpu.VMEM((2, rows), F32),
            pltpu.VMEM((1, rows), jnp.int32),
            pltpu.SemaphoreType.DMA((5,)),
        ],
        cost_estimate=SMALL,
        compiler_params=params(LIMIT_EARLY),
        name="token_parts",
    )(
        *[
            pltpu.with_memory_space_constraint(x, pltpu.HBM)
            for x in (tokens, chosen_experts.T, logits.T, tenant.reshape(1, rows))
        ]
    )


def meta_kernel(n_local, local_halves, ids_ref, adapter_ref, pool_slot_ref, *refs):
    blocks, (p_ref, pt_ref, cols_ref, rows_ref, tslot_ref) = refs[:-5], refs[-5:]
    at = blocks[0].shape[1] - 128
    facts = jnp.concatenate([block[:, at:] for block in blocks], axis=0).astype(F32).T
    count = facts.shape[1]
    first, second, tenant = facts[0:1], facts[1:2], facts[2:3]
    logit_first = (facts[3:4] + facts[5:6]) + facts[7:8]
    logit_second = (facts[4:5] + facts[6:7]) + facts[8:9]
    weight_first = jax.nn.sigmoid(logit_first - logit_second)
    weight_second = jax.nn.sigmoid(logit_second - logit_first)
    slot = jnp.zeros_like(tenant)
    for number in range(adapter_ref.shape[0]):
        slot = jnp.where(tenant == number, pool_slot_ref[adapter_ref[number]].astype(F32), slot)
    members, weights = [], []
    for i in range(n_local):
        expert = (ids_ref[0] * local_halves // 2 + i).astype(F32)
        hit_first, hit_second = first == expert, second == expert
        members.append(jnp.where(hit_first | hit_second, 1.0, 0.0))
        weights.append(jnp.where(hit_first, weight_first, 0.0) + jnp.where(hit_second, weight_second, 0.0))
    member = jnp.concatenate(members + [jnp.zeros((8 - n_local, count), F32)], axis=0)
    before = (
        lax.broadcasted_iota(jnp.int32, (count, count), 0) < lax.broadcasted_iota(jnp.int32, (count, count), 1)
    ).astype(BF16)
    place = jnp.where(member > 0, mm(member.astype(BF16), before), -1.0)
    table = jnp.concatenate(
        [place[0:n_local]] + weights + [slot] + [jnp.zeros((127 - 2 * n_local, count), F32)], axis=0
    )
    columns = table.T
    cols_ref[...] = columns
    rows_ref[...] = table[0:8]
    row_count = p_ref.shape[1]
    tenant_rows = jnp.broadcast_to(tenant, (8, count)).astype(BF16)
    down = lax.broadcasted_iota(jnp.int32, (row_count, count), 0).astype(F32)
    across = lax.broadcasted_iota(jnp.int32, (count, row_count), 1).astype(F32)
    for i in range(n_local):
        picked = (down == place[i : i + 1]).astype(BF16)
        p_ref[i] = picked
        pt_ref[i] = (across == columns[:, i : i + 1]).astype(BF16)
        tslot_ref[i] = mm_nt(tenant_rows, picked)


def build_meta(blocks, ids, adapters, pool_slots, n_local, local_halves, row_count):
    count = sum(block.shape[0] for block in blocks)
    return pl.pallas_call(
        functools.partial(meta_kernel, n_local, local_halves),
        out_shape=(
            jax.ShapeDtypeStruct((n_local, row_count, count), BF16),
            jax.ShapeDtypeStruct((n_local, count, row_count), BF16),
            jax.ShapeDtypeStruct((count, 128), F32),
            jax.ShapeDtypeStruct((8, count), F32),
            jax.ShapeDtypeStruct((n_local, 8, row_count), F32),
        ),
        in_specs=[smem()] * 3 + [vmem()] * len(blocks),
        out_specs=(vmem(),) * 5,
        cost_estimate=SMALL,
        compiler_params=params(max(LIMIT_EARLY, 12 * count * count // MIB)),
        name="routing_tables",
    )(ids, adapters, pool_slots, *blocks)


def slab_copies(gate_ref, up_ref, into_ref, sems, part, half):
    depth, width = into_ref.shape[1], into_ref.shape[2]
    copies = []
    for number in range(into_ref.shape[0]):
        source = (gate_ref, up_ref)[number % 2].at[half, pl.ds(part * depth, depth), pl.ds(number // 2 * width, width)]
        copies.append(pltpu.make_async_copy(source, into_ref.at[number], sems.at[half, number]))
    return copies


def prefetch_kernel(ids_ref, adapter_ref, pool_slot_ref, gate_ref, up_ref, pool_ref, *refs):
    slabs, (factors, mark_ref, sems, factor_sems) = refs[:-4], refs[-4:]
    copies = [copy for half, slab in enumerate(slabs) for copy in slab_copies(gate_ref, up_ref, slab, sems, 0, half)]
    rank = pool_ref.shape[2]
    for number in range(adapter_ref.shape[0]):
        source = pool_ref.at[pool_slot_ref[adapter_ref[number]]]
        into = factors.at[:, number * rank : (number + 1) * rank]
        copies.append(pltpu.make_async_copy(source, into, factor_sems.at[number]))
    for copy in copies:
        copy.start()
    mark_ref[...] = jnp.zeros_like(mark_ref)
    for copy in copies:
        copy.wait()


def prefetch(ids, adapters, pool_slots, gate, up, pool, part_width):
    local_halves, _, hidden_count = gate.shape
    tile = min(N_TILE, hidden_count)
    each = 2 * hidden_count // tile
    tenants, rank = adapters.shape[0], pool.shape[2]
    return pl.pallas_call(
        prefetch_kernel,
        out_shape=(pltpu.VMEM((each, part_width, tile), BF16),) * local_halves
        + (pltpu.VMEM((local_halves, tenants * rank, hidden_count), BF16), jax.ShapeDtypeStruct((8, 128), F32)),
        in_specs=[smem()] * 3 + [pl.BlockSpec(memory_space=pltpu.HBM)] * 3,
        out_specs=(vmem(),) * (local_halves + 2),
        scratch_shapes=[pltpu.SemaphoreType.DMA((local_halves, each)), pltpu.SemaphoreType.DMA((tenants,))],
        cost_estimate=SMALL,
        compiler_params=params(LIMIT_EARLY),
        name="weight_prefetch",
    )(ids, adapters, pool_slots, gate, up, pool)


def pack(blocks, p_ref, packed):
    depth = packed.shape[2]
    whole = jnp.concatenate([block[:, :depth] for block in blocks], axis=0)
    for i in range(p_ref.shape[0]):
        packed[i] = mm(p_ref[i], whole).astype(BF16)


def down_slabs(down, n_ad, halves=None):
    return pltpu.VMEM((halves or down.shape[0], down.shape[1], down.shape[2] // n_ad), BF16)


def down_fetch(n_ad, step, ids_ref, down_ref, into_ref, sems, pieces=2, first=0):
    halves, rows, span = into_ref.shape
    rows = rows // pieces
    start = pl.multiple_of(lax.rem(ids_ref[1] + step, n_ad) * span, span)
    return [
        pltpu.make_async_copy(
            down_ref.at[first + half, pl.ds(i * rows, rows), pl.ds(start, span)],
            into_ref.at[half, pl.ds(i * rows, rows)],
            sems.at[half, i],
        )
        for half in range(halves)
        for i in range(pieces)
    ]


def first_kernel(n_blocks, local_halves, *refs):
    blocks, refs = refs[:n_blocks], refs[n_blocks:]
    _, p_ref, gate_ref, up_ref, refs = *refs[:4], refs[4:]
    slabs, refs = refs[:local_halves], refs[local_halves:]
    ahead, (gate_out, up_out, mark_out, packed, sems) = refs[:-5], refs[-5:]
    mark_out[...] = jnp.zeros_like(mark_out)
    pack(blocks, p_ref, packed)
    slabs = list(ahead) + list(slabs[len(ahead) :])
    copies = [slab_copies(gate_ref, up_ref, slab, sems, 1, half) for half, slab in enumerate(ahead)]
    halves_each = local_halves // p_ref.shape[0]
    for half in range(local_halves):
        rows = packed[half // halves_each]
        tiles, _, width = slabs[half].shape
        for tile in range(tiles // 2):
            span = slice(tile * width, (tile + 1) * width)
            gate_out[half, :, span] = mm(rows, slabs[half][2 * tile])
            up_out[half, :, span] = mm(rows, slabs[half][2 * tile + 1])
            if half < len(ahead):
                copies[half][2 * tile].start()
                copies[half][2 * tile + 1].start()
    for copy in [copy for half in copies for copy in half]:
        copy.wait()


def first_part(blocks, mark, picked, gate, up, slabs):
    local_halves, _, hidden_count = gate.shape
    n_local, row_count, _ = picked.shape
    each, part_width, _ = slabs[0].shape
    hbm = pl.BlockSpec(memory_space=pltpu.HBM)
    sums = pltpu.VMEM((local_halves, row_count, hidden_count), F32)
    n_ahead = max(1, local_halves - 2)
    return pl.pallas_call(
        functools.partial(first_kernel, len(blocks), local_halves),
        out_shape=(pltpu.VMEM(slabs[0].shape, BF16),) * n_ahead
        + (sums, sums, jax.ShapeDtypeStruct((8, 128), F32)),
        in_specs=[vmem()] * (len(blocks) + 2) + [hbm, hbm] + [vmem()] * local_halves,
        out_specs=(vmem(),) * (n_ahead + 3),
        scratch_shapes=[
            pltpu.VMEM((n_local, row_count, part_width), BF16),
            pltpu.SemaphoreType.DMA((n_ahead, each)),
        ],
        input_output_aliases={len(blocks) + 4 + half: half for half in range(n_ahead)},
        cost_estimate=SMALL,
        compiler_params=params(max(LIMIT_EARLY, 10 * n_local * row_count * part_width // MIB)),
        name="gate_up_first",
    )(*blocks, mark, picked, gate, up, *[pltpu.with_memory_space_constraint(x, pltpu.VMEM) for x in slabs])


def second_kernel(n_blocks, n_ahead, n_ad, steps, *refs):
    blocks, refs = refs[:n_blocks], refs[n_blocks:]
    p_ref, gate_ref, up_ref, refs = *refs[1:4], refs[4:]
    ahead, gate_in, up_in, refs = refs[:n_ahead], refs[n_ahead], refs[n_ahead + 1], refs[n_ahead + 2 :]
    ids_ref, factors, tslot_ref, rows_ref, down_ref, refs = *refs[:5], refs[5:]
    hidden_ref, low_ref, refs = refs[0], refs[1], refs[2:]
    nexts, (packed, down_sems, late, sems) = refs[:-4], refs[-4:]
    n_local = p_ref.shape[0]
    local_halves, _, hidden_count = gate_ref.shape
    halves_each = local_halves // n_local
    slabs = list(ahead) + [late] * (local_halves - n_ahead)
    copies = {
        half: slab_copies(gate_ref, up_ref, slabs[half], sems, 1, half) for half in range(n_ahead, local_halves)
    }
    rank = RANK
    tenants = factors.shape[1] // rank
    down_copies = []
    for number, step in enumerate(steps):
        down_copies += down_fetch(n_ad, step, ids_ref, down_ref, nexts[number], down_sems.at[number], 1)
    for copy in copies.get(n_ahead, []) + down_copies:
        copy.start()
    pack(blocks, p_ref, packed)
    for half in range(local_halves):
        rows = packed[half // halves_each]
        tiles, _, width = slabs[half].shape
        for tile in range(tiles // 2):
            span = slice(tile * width, (tile + 1) * width)
            values = []
            for number in (2 * tile, 2 * tile + 1):
                if half in copies:
                    copies[half][number].wait()
                values.append(mm(rows, slabs[half][number]))
                if half in copies and half + 1 in copies:
                    copies[half + 1][number].start()
            gate = values[0] + gate_in[half, :, span]
            up = values[1] + up_in[half, :, span]
            hidden_ref[half, :, span] = (silu(gate) * up).astype(BF16)
    for i in range(n_local):
        low = mm_nt(factors[i * halves_each], hidden_ref[i * halves_each])
        for half in range(i * halves_each + 1, (i + 1) * halves_each):
            low = low + mm_nt(factors[half], hidden_ref[half])
        owner = tslot_ref[i][0:1]
        total = jnp.zeros((rank, low.shape[1]), F32)
        for number in range(tenants):
            total = total + jnp.where(owner == number, low[number * rank : (number + 1) * rank], 0.0)
        weight = rows_ref[n_local + i : n_local + i + 1]
        low_ref[i * rank : (i + 1) * rank] = (mm(total.astype(BF16), p_ref[i]) * weight).astype(BF16)
    for copy in down_copies:
        copy.wait()


def second_part(
    blocks, mark, picked, gate, up, ahead, sums, ids, factors, tslot, table_rows, down, n_ad, steps
):
    local_halves, _, hidden_count = gate.shape
    n_local, row_count, count = picked.shape
    each, part_width, tile = ahead[0].shape
    rank = RANK
    hbm = pl.BlockSpec(memory_space=pltpu.HBM)
    held = [pltpu.with_memory_space_constraint(x, pltpu.VMEM) for x in (*ahead, *sums)]
    factors = pltpu.with_memory_space_constraint(factors, pltpu.VMEM)
    late_bytes = 2 * each * part_width * tile
    return pl.pallas_call(
        functools.partial(second_kernel, len(blocks), len(ahead), n_ad, steps),
        out_shape=(
            pltpu.VMEM((local_halves, row_count, hidden_count), BF16),
            jax.ShapeDtypeStruct((n_local * rank, count), BF16),
            *[down_slabs(down, n_ad, None if i == 0 else max(1, local_halves // 2)) for i in range(len(steps))],
        ),
        in_specs=[vmem()] * (len(blocks) + 2) + [hbm, hbm] + [vmem()] * len(held) + [smem()] + [vmem()] * 3 + [hbm],
        out_specs=(vmem(),) * (2 + len(steps)),
        scratch_shapes=[
            pltpu.VMEM((n_local, row_count, part_width), BF16),
            pltpu.SemaphoreType.DMA((len(steps), local_halves, 2)),
            pltpu.VMEM((each, part_width, tile), BF16),
            pltpu.SemaphoreType.DMA((local_halves, each)),
        ],
        cost_estimate=SMALL,
        compiler_params=params(
            max(LIMIT_EARLY, 10 * n_local * row_count * part_width // MIB) + late_bytes // MIB + 1
        ),
        name="gate_up_second",
    )(*blocks, mark, picked, gate, up, *held, ids, factors, tslot, table_rows, down)


def weighted_down(hidden_ref, weights, pt_ref, cols_ref):
    slabs = [ref.at[half] for ref in weights for half in range(ref.shape[0])]
    n_local = pt_ref.shape[0]
    halves_each = hidden_ref.shape[0] // n_local
    total = None
    for i in range(n_local):
        part_sum = mm(hidden_ref[i * halves_each], slabs[i * halves_each][...])
        for half in range(i * halves_each + 1, (i + 1) * halves_each):
            part_sum = part_sum + mm(hidden_ref[half], slabs[half][...])
        laid = mm(pt_ref[i], part_sum.astype(BF16)) * cols_ref[:, n_local + i : n_local + i + 1]
        total = laid if total is None else total + laid
    return total


def down_first_kernel(n_ad, step, ids_ref, hidden_ref, weight_ref, pt_ref, cols_ref, down_ref, keep, send, *refs):
    copies = []
    if refs:
        into, sems = refs
        copies = down_fetch(n_ad, step, ids_ref, down_ref, into, sems, 2, down_ref.shape[0] - into.shape[0])
    for copy in copies:
        copy.start()
    write_pairs(weighted_down(hidden_ref, [weight_ref], pt_ref, cols_ref), (keep, send))
    for copy in copies:
        copy.wait()


def down_first(ids, hidden, weights, pt, cols, down, n_ad, step, left):
    count, span = pt.shape[1], weights.shape[2]
    return pl.pallas_call(
        functools.partial(down_first_kernel, n_ad, step),
        out_shape=(jax.ShapeDtypeStruct((count // 2, span), BF16),) * 2
        + ((down_slabs(down, n_ad, left),) if left else ()),
        in_specs=[smem()] + [vmem()] * 4 + [pl.BlockSpec(memory_space=pltpu.HBM)],
        out_specs=(vmem(),) * (3 if left else 2),
        scratch_shapes=[pltpu.SemaphoreType.DMA((left, 2))] if left else [],
        cost_estimate=SMALL,
        compiler_params=params(max(LIMIT, 12 * count * span // MIB)),
        name="down_first",
    )(ids, hidden, pltpu.with_memory_space_constraint(weights, pltpu.VMEM), pt, cols, down)


def down_rest_kernel(n_weights, n_ad, steps, ids_ref, hidden_ref, pt_ref, cols_ref, down_ref, *refs):
    weights, (keep, send, base), refs = refs[:n_weights], refs[n_weights : n_weights + 3], refs[n_weights + 3 :]
    held, sems = refs[:-1], refs[-1]
    copies = [
        down_fetch(n_ad, step, ids_ref, down_ref, into, sems.at[number])
        for number, (step, into) in enumerate(zip(steps[1:], held))
    ]
    for copy in [copy for group in copies for copy in group]:
        copy.start()
    span = base.shape[1]
    for number in range(len(steps)):
        if number:
            for copy in copies[number - 1]:
                copy.wait()
        total = weighted_down(hidden_ref, [held[number - 1]] if number else weights, pt_ref, cols_ref)
        if number < len(steps) - 1:
            write_pairs(total, (keep, send), number * span)
        else:
            base[...] = total


def down_rest(ids, hidden, weights, pt, cols, down, n_ad, steps):
    count, span = pt.shape[1], down.shape[2] // n_ad
    chunk = (*down.shape[:2], span)
    return pl.pallas_call(
        functools.partial(down_rest_kernel, len(weights), n_ad, steps),
        out_shape=(jax.ShapeDtypeStruct((count // 2, span * (len(steps) - 1)), BF16),) * 2
        + (jax.ShapeDtypeStruct((count, span), F32),),
        in_specs=[smem()] + [vmem()] * 3 + [pl.BlockSpec(memory_space=pltpu.HBM)] + [vmem()] * len(weights),
        out_specs=(vmem(),) * 3,
        scratch_shapes=[pltpu.VMEM(chunk, BF16)] * (len(steps) - 1)
        + [pltpu.SemaphoreType.DMA((len(steps) - 1, down.shape[0], 2))],
        cost_estimate=SMALL,
        compiler_params=params(max(LIMIT, 12 * count * span // MIB) + (len(steps) - 1) * math.prod(chunk) * 2 // MIB),
        name="down_rest",
    )(ids, hidden, pt, cols, down, *[pltpu.with_memory_space_constraint(x, pltpu.VMEM) for x in weights])


def write_pairs(total, outs, at=0):
    keep, send = outs
    for b in range(total.shape[0] // 128):
        block = total[b * 128 : b * 128 + 128].astype(BF16)
        (send if b % 2 else keep)[b // 2 * 128 : b // 2 * 128 + 128, pl.ds(at, total.shape[1])] = block


def adapter_kernel(slot_column, local_halves, ids_ref, base_ref, cols_ref, factor_ref, low_ref, keep, send, wide):
    blocks = base_ref.shape[0] // 128
    height = low_ref.shape[0] // blocks
    wide[...] = jnp.zeros_like(wide)
    for m in range(blocks):
        row = pl.multiple_of(((ids_ref[0] ^ m) * local_halves // 2) * RANK, RANK)
        value = low_ref[m * height : (m + 1) * height].astype(F32)
        value = jnp.concatenate([value[:, (m ^ b) * 128 : (m ^ b) * 128 + 128] for b in range(blocks)], axis=1)
        wide[pl.ds(row, height)] += value
    low = wide[...].T.astype(BF16)
    zero = jnp.zeros_like(low)
    slot = cols_ref[:, slot_column : slot_column + 1]
    depth = EXPERT_COUNT * RANK
    slot_count = factor_ref.shape[0] // depth
    total = base_ref[...]
    for j in range(0, slot_count, 2):
        spread = jnp.concatenate(
            [jnp.where(slot == (ids_ref[0] * slot_count + j + i).astype(F32), low, zero) for i in range(2)], axis=1
        )
        total = total + mm(spread, factor_ref[j * depth : (j + 2) * depth])
    write_pairs(total, (keep, send))


def adapter_part(ids, base, cols, slot_column, local_halves, factors, low):
    count, span = base.shape
    return pl.pallas_call(
        functools.partial(adapter_kernel, slot_column, local_halves),
        out_shape=(jax.ShapeDtypeStruct((count // 2, span), BF16),) * 2,
        in_specs=[smem()] + [vmem()] * 4,
        out_specs=(vmem(),) * 2,
        scratch_shapes=[pltpu.VMEM((EXPERT_COUNT * RANK, count), F32)],
        cost_estimate=SMALL,
        compiler_params=params(max(LIMIT, 24 * count * span // MIB)),
        name="adapters",
    )(ids, base, cols, factors, low)


def split_kernel(keep_ref, came_ref, keep, send):
    for b in range(keep_ref.shape[0] // 128):
        total = keep_ref[b * 128 : b * 128 + 128].astype(F32) + came_ref[b * 128 : b * 128 + 128].astype(F32)
        (send if b % 2 else keep)[b // 2 * 128 : b // 2 * 128 + 128] = total.astype(BF16)


def split_sum(keep, came):
    return pl.pallas_call(
        split_kernel,
        out_shape=(jax.ShapeDtypeStruct((keep.shape[0] // 2, keep.shape[1]), BF16),) * 2,
        in_specs=[vmem()] * 2,
        out_specs=(vmem(),) * 2,
        cost_estimate=SMALL,
        compiler_params=params(LIMIT),
        name="sum_and_split",
    )(keep, came)


def cut_kernel(edges, keep_ref, came_ref, *outs):
    for first, last, out in zip(edges, edges[1:], outs):
        out[...] = (keep_ref[:, first:last].astype(F32) + came_ref[:, first:last].astype(F32)).astype(BF16)


def cut_sum(keep, came, edges):
    return pl.pallas_call(
        functools.partial(cut_kernel, edges),
        out_shape=tuple(
            jax.ShapeDtypeStruct((keep.shape[0], last - first), BF16) for first, last in zip(edges, edges[1:])
        ),
        in_specs=[vmem()] * 2,
        out_specs=(vmem(),) * (len(edges) - 1),
        cost_estimate=SMALL,
        compiler_params=params(LIMIT),
        name="sum_and_cut",
    )(keep, came)


def per_device(
    n_ep,
    n_ad,
    tokens,
    chosen_experts,
    router_gate_logits,
    token_tenant,
    adapter_of_tenant,
    adapter_pool_slot,
    gate_weight,
    up_weight,
    down_weight,
    adapter_input_factors,
    adapter_output_factors,
):
    gate_weight, up_weight, down_weight, adapter_input_factors = [
        pltpu.with_memory_space_constraint(x, pltpu.HBM)
        for x in (gate_weight, up_weight, down_weight, adapter_input_factors)
    ]
    width = tokens.shape[1]
    span = width // n_ad
    local_halves = gate_weight.shape[0]
    n_local = max(1, local_halves // 2)
    row_count = n_ep * CAP
    bits = n_ep.bit_length() - 1
    ids = jnp.stack([lax.axis_index("ep"), lax.axis_index("ad")]).astype(jnp.int32)

    def swap(x, mask):
        return lax.ppermute(x, "ep", [(i, i ^ mask) for i in range(n_ep)])

    def tie(x, y):
        return lax.optimization_barrier((x, y))

    def shift(x, step):
        return lax.ppermute(x, "ad", [(i, (i + step) % n_ad) for i in range(n_ad)])

    order = sorted(range(1, n_ad), key=lambda step: (step != n_ad // 2, step))
    token_part = token_parts_of(tokens, chosen_experts, router_gate_logits, token_tenant)
    *slabs, factors, mark = prefetch(
        ids, adapter_of_tenant, adapter_pool_slot, gate_weight, up_weight, adapter_input_factors, width // 2
    )
    high = 1 << (bits - 1)
    crossing = [swap(own, high) for own in token_part]

    def spread(part, crossed):
        blocks = {0: token_part[part], high: crossed}
        for bit in reversed(range(bits - 1)):
            for mask in list(blocks):
                blocks[mask | 1 << bit] = swap(blocks[mask], 1 << bit)
        return [blocks[mask] for mask in range(n_ep)]

    crossing[0], mark = tie(crossing[0], mark)
    blocks = spread(0, crossing[0])
    picked, pt, cols, table_rows, tslot = build_meta(
        blocks, ids, adapter_of_tenant, adapter_pool_slot, n_local, local_halves, row_count
    )
    *ahead, gate_sum, up_sum, mark = first_part(blocks, mark, picked, gate_weight, up_weight, slabs)
    crossing[1], mark = tie(crossing[1], mark)
    hidden, low, weights, *following = second_part(
        spread(1, crossing[1]), mark, picked, gate_weight, up_weight, ahead, (gate_sum, up_sum), ids, factors,
        tslot, table_rows, down_weight, n_ad, order[:2],
    )

    def onward(keep, came, first=1):
        for bit in range(first, bits):
            keep, send = split_sum(keep, came)
            came = swap(send, 1 << bit)
        return keep, came

    def other_of(low, bit):
        return lax.ppermute(low, "ad", [(i, i ^ 1 << bit) for i in range(n_ad)])

    def added(x, y):
        return (x.astype(F32) + y.astype(F32)).astype(BF16)

    far_steps = range(1, n_ad.bit_length() - 1)
    others = [other_of(low, bit) for bit in far_steps[:1]]
    left = local_halves - following[0].shape[0]
    keep, send, *later = down_first(ids, hidden, weights, pt, cols, down_weight, n_ad, order[1], left)
    others, keep, send, later = lax.optimization_barrier((others, keep, send, later))
    for bit in far_steps:
        low = added(low, others[0] if bit == 1 else other_of(low, bit))
    for bit in range(bits - 1):
        low = jnp.concatenate([low, swap(low, 1 << bit)], axis=0)
    crossed = swap(low, 1 << (bits - 1))
    keep, came = onward(keep, swap(send, 1), 1)
    keep, hidden = tie(keep, hidden)
    keep_rest, send_rest, base = down_rest(ids, hidden, following + later, pt, cols, down_weight, n_ad, (*order[1:], 0))
    came, crossed, keep_rest, send_rest, base = lax.optimization_barrier((came, crossed, keep_rest, send_rest, base))
    low = jnp.concatenate([low, crossed], axis=0)
    low = added(low, other_of(low, 0))
    (sums,) = cut_sum(keep, came, (0, span))
    results = [shift(sums, order[0])]
    keep_rest, came_rest = onward(keep_rest, swap(send_rest, 1))
    slot_count = adapter_output_factors.shape[0]
    flat_factors = adapter_output_factors.reshape(slot_count * EXPERT_COUNT * RANK, span)
    keep, send = adapter_part(ids, base, cols, 2 * n_local, local_halves, flat_factors, low)
    came_rest, results, keep, send = lax.optimization_barrier((came_rest, results, keep, send))
    came = swap(send, 1)
    if bits > 1:
        keep, send = split_sum(keep, came)
        came_rest, keep, send = lax.optimization_barrier((came_rest, keep, send))
        came = swap(send, 2)
    keep, came = onward(keep, came, 2)
    parts = cut_sum(keep_rest, came_rest, [span * i for i in range(n_ad - 1)])
    results += [shift(x, step) for x, step in zip(parts, order[1:])]
    return sum(x.astype(F32) for x in [keep, came] + results).astype(BF16)


def solution(mesh):
    placed = (
        P(("rep", "ep"), None),
        P(("rep", "ep"), None),
        P(("rep", "ep"), None),
        P(("rep", "ep")),
        P("rep"),
        P(),
        P("ep", None, "ad"),
        P("ep", None, "ad"),
        P("ep", "ad", None),
        P(None, "ep", None, "ad"),
        P("ep", None, None, "ad"),
    )
    return jax.shard_map(
        functools.partial(per_device, mesh.shape["ep"], mesh.shape["ad"]),
        mesh=mesh,
        in_specs=placed,
        out_specs=P(("rep", "ep"), "ad"),
        check_vma=False,
    )
```

```python
import functools
import math

import jax
import jax.numpy as jnp
from jax import lax
from jax.experimental import pallas as pl
from jax.experimental.pallas import tpu as pltpu
from jax.sharding import PartitionSpec as P

EXPERT_COUNT = 8
TOP = 2
RANK = 16
CAP = 48
LIMIT = 16
LIMIT_EARLY = 8
N_TILE = 512
MIB = 1 << 20

F32 = jnp.float32
BF16 = jnp.bfloat16


def mm(a, b):
    return jnp.dot(a, b, preferred_element_type=F32)


def mm_nt(a, b):
    return lax.dot_general(a, b, (((1,), (1,)), ((), ())), preferred_element_type=F32)


SMALL = pl.CostEstimate(flops=1, bytes_accessed=1, transcendentals=0)


def silu(x):
    half = 0.5 * x
    return half + half * jnp.tanh(half)


def params(mib):
    return pltpu.CompilerParams(vmem_limit_bytes=mib * MIB)


def vmem():
    return pl.BlockSpec(memory_space=pltpu.VMEM)


def smem():
    return pl.BlockSpec(memory_space=pltpu.SMEM)


def parts_kernel(tokens_ref, chosen_in, logits_in, tenant_in, first_ref, second_ref, chosen_ref, logits_ref, tenant_ref, sems):
    rows, width = second_ref.shape
    copies = [
        pltpu.make_async_copy(tokens_ref.at[:, pl.ds(0, width)], first_ref.at[:, pl.ds(0, width)], sems.at[0]),
        pltpu.make_async_copy(tokens_ref.at[:, pl.ds(width, width)], second_ref, sems.at[1]),
    ]
    small = [
        pltpu.make_async_copy(source, into, sems.at[2 + number])
        for number, (source, into) in enumerate(
            [(chosen_in, chosen_ref), (logits_in, logits_ref), (tenant_in, tenant_ref)]
        )
    ]
    for copy in small + copies:
        copy.start()
    for copy in small:
        copy.wait()
    diagonal = lax.broadcasted_iota(jnp.int32, (rows, rows), 0) == lax.broadcasted_iota(jnp.int32, (rows, rows), 1)

    def column(row):
        return jnp.sum(jnp.where(diagonal, row, 0.0), axis=1, keepdims=True)

    chosen, logits = chosen_ref[...].astype(F32), logits_ref[...]
    columns = [column(chosen[0:1]), column(chosen[1:2]), column(tenant_ref[...].astype(F32))]
    rests = [column(logits[0:1]), column(logits[1:2])]
    for _ in range(3):
        pieces = [rest.astype(BF16).astype(F32) for rest in rests]
        columns += pieces
        rests = [rest - piece for rest, piece in zip(rests, pieces)]
    lane = lax.broadcasted_iota(jnp.int32, (rows, 128), 1)
    facts = jnp.zeros((rows, 128), F32)
    for number, value in enumerate(columns):
        facts = jnp.where(lane == number, value, facts)
    first_ref[:, width:] = facts.astype(BF16)
    for copy in copies:
        copy.wait()


def token_parts_of(tokens, chosen_experts, logits, tenant):
    rows, width = tokens.shape[0], tokens.shape[1] // 2
    return pl.pallas_call(
        parts_kernel,
        out_shape=(
            jax.ShapeDtypeStruct((rows, width + 128), BF16),
            jax.ShapeDtypeStruct((rows, width), BF16),
        ),
        in_specs=[pl.BlockSpec(memory_space=pltpu.HBM)] * 4,
        out_specs=(vmem(),) * 2,
        scratch_shapes=[
            pltpu.VMEM((2, rows), jnp.int32),
            pltpu.VMEM((2, rows), F32),
            pltpu.VMEM((1, rows), jnp.int32),
            pltpu.SemaphoreType.DMA((5,)),
        ],
        cost_estimate=SMALL,
        compiler_params=params(LIMIT_EARLY),
        name="token_parts",
    )(
        *[
            pltpu.with_memory_space_constraint(x, pltpu.HBM)
            for x in (tokens, chosen_experts.T, logits.T, tenant.reshape(1, rows))
        ]
    )


def meta_kernel(n_local, local_halves, ids_ref, adapter_ref, pool_slot_ref, *refs):
    blocks, (p_ref, pt_ref, cols_ref, rows_ref, tslot_ref) = refs[:-5], refs[-5:]
    at = blocks[0].shape[1] - 128
    facts = jnp.concatenate([block[:, at:] for block in blocks], axis=0).astype(F32).T
    count = facts.shape[1]
    first, second, tenant = facts[0:1], facts[1:2], facts[2:3]
    logit_first = (facts[3:4] + facts[5:6]) + facts[7:8]
    logit_second = (facts[4:5] + facts[6:7]) + facts[8:9]
    weight_first = jax.nn.sigmoid(logit_first - logit_second)
    weight_second = jax.nn.sigmoid(logit_second - logit_first)
    slot = jnp.zeros_like(tenant)
    for number in range(adapter_ref.shape[0]):
        slot = jnp.where(tenant == number, pool_slot_ref[adapter_ref[number]].astype(F32), slot)
    members, weights = [], []
    for i in range(n_local):
        expert = (ids_ref[0] * local_halves // 2 + i).astype(F32)
        hit_first, hit_second = first == expert, second == expert
        members.append(jnp.where(hit_first | hit_second, 1.0, 0.0))
        weights.append(jnp.where(hit_first, weight_first, 0.0) + jnp.where(hit_second, weight_second, 0.0))
    member = jnp.concatenate(members + [jnp.zeros((8 - n_local, count), F32)], axis=0)
    before = (
        lax.broadcasted_iota(jnp.int32, (count, count), 0) < lax.broadcasted_iota(jnp.int32, (count, count), 1)
    ).astype(BF16)
    place = jnp.where(member > 0, mm(member.astype(BF16), before), -1.0)
    table = jnp.concatenate(
        [place[0:n_local]] + weights + [slot] + [jnp.zeros((127 - 2 * n_local, count), F32)], axis=0
    )
    columns = table.T
    cols_ref[...] = columns
    rows_ref[...] = table[0:8]
    row_count = p_ref.shape[1]
    tenant_rows = jnp.broadcast_to(tenant, (8, count)).astype(BF16)
    down = lax.broadcasted_iota(jnp.int32, (row_count, count), 0).astype(F32)
    across = lax.broadcasted_iota(jnp.int32, (count, row_count), 1).astype(F32)
    for i in range(n_local):
        picked = (down == place[i : i + 1]).astype(BF16)
        p_ref[i] = picked
        pt_ref[i] = (across == columns[:, i : i + 1]).astype(BF16)
        tslot_ref[i] = mm_nt(tenant_rows, picked)


def build_meta(blocks, ids, adapters, pool_slots, n_local, local_halves, row_count):
    count = sum(block.shape[0] for block in blocks)
    return pl.pallas_call(
        functools.partial(meta_kernel, n_local, local_halves),
        out_shape=(
            jax.ShapeDtypeStruct((n_local, row_count, count), BF16),
            jax.ShapeDtypeStruct((n_local, count, row_count), BF16),
            jax.ShapeDtypeStruct((count, 128), F32),
            jax.ShapeDtypeStruct((8, count), F32),
            jax.ShapeDtypeStruct((n_local, 8, row_count), F32),
        ),
        in_specs=[smem()] * 3 + [vmem()] * len(blocks),
        out_specs=(vmem(),) * 5,
        cost_estimate=SMALL,
        compiler_params=params(max(LIMIT_EARLY, 12 * count * count // MIB)),
        name="routing_tables",
    )(ids, adapters, pool_slots, *blocks)


def slab_copies(gate_ref, up_ref, into_ref, sems, part, half):
    depth, width = into_ref.shape[1], into_ref.shape[2]
    copies = []
    for number in range(into_ref.shape[0]):
        source = (gate_ref, up_ref)[number % 2].at[half, pl.ds(part * depth, depth), pl.ds(number // 2 * width, width)]
        copies.append(pltpu.make_async_copy(source, into_ref.at[number], sems.at[half, number]))
    return copies


def prefetch_kernel(ids_ref, adapter_ref, pool_slot_ref, gate_ref, up_ref, pool_ref, *refs):
    slabs, (factors, mark_ref, sems, factor_sems) = refs[:-4], refs[-4:]
    copies = [copy for half, slab in enumerate(slabs) for copy in slab_copies(gate_ref, up_ref, slab, sems, 0, half)]
    rank = pool_ref.shape[2]
    for number in range(adapter_ref.shape[0]):
        source = pool_ref.at[pool_slot_ref[adapter_ref[number]]]
        into = factors.at[:, number * rank : (number + 1) * rank]
        copies.append(pltpu.make_async_copy(source, into, factor_sems.at[number]))
    for copy in copies:
        copy.start()
    mark_ref[...] = jnp.zeros_like(mark_ref)
    for copy in copies:
        copy.wait()


def prefetch(ids, adapters, pool_slots, gate, up, pool, part_width):
    local_halves, _, hidden_count = gate.shape
    tile = min(N_TILE, hidden_count)
    each = 2 * hidden_count // tile
    tenants, rank = adapters.shape[0], pool.shape[2]
    return pl.pallas_call(
        prefetch_kernel,
        out_shape=(pltpu.VMEM((each, part_width, tile), BF16),) * local_halves
        + (pltpu.VMEM((local_halves, tenants * rank, hidden_count), BF16), jax.ShapeDtypeStruct((8, 128), F32)),
        in_specs=[smem()] * 3 + [pl.BlockSpec(memory_space=pltpu.HBM)] * 3,
        out_specs=(vmem(),) * (local_halves + 2),
        scratch_shapes=[pltpu.SemaphoreType.DMA((local_halves, each)), pltpu.SemaphoreType.DMA((tenants,))],
        cost_estimate=SMALL,
        compiler_params=params(LIMIT_EARLY),
        name="weight_prefetch",
    )(ids, adapters, pool_slots, gate, up, pool)


def pack(blocks, p_ref, packed):
    depth = packed.shape[2]
    whole = jnp.concatenate([block[:, :depth] for block in blocks], axis=0)
    for i in range(p_ref.shape[0]):
        packed[i] = mm(p_ref[i], whole).astype(BF16)


def down_slabs(down, n_ad, halves=None):
    return pltpu.VMEM((halves or down.shape[0], down.shape[1], down.shape[2] // n_ad), BF16)


def down_fetch(n_ad, step, ids_ref, down_ref, into_ref, sems, pieces=2, first=0):
    halves, rows, span = into_ref.shape
    rows = rows // pieces
    start = pl.multiple_of(lax.rem(ids_ref[1] + step, n_ad) * span, span)
    return [
        pltpu.make_async_copy(
            down_ref.at[first + half, pl.ds(i * rows, rows), pl.ds(start, span)],
            into_ref.at[half, pl.ds(i * rows, rows)],
            sems.at[half, i],
        )
        for half in range(halves)
        for i in range(pieces)
    ]


def first_kernel(n_blocks, local_halves, *refs):
    blocks, refs = refs[:n_blocks], refs[n_blocks:]
    _, p_ref, gate_ref, up_ref, refs = *refs[:4], refs[4:]
    slabs, refs = refs[:local_halves], refs[local_halves:]
    ahead, (gate_out, up_out, mark_out, packed, sems) = refs[:-5], refs[-5:]
    mark_out[...] = jnp.zeros_like(mark_out)
    pack(blocks, p_ref, packed)
    slabs = list(ahead) + list(slabs[len(ahead) :])
    copies = [slab_copies(gate_ref, up_ref, slab, sems, 1, half) for half, slab in enumerate(ahead)]
    halves_each = local_halves // p_ref.shape[0]
    for half in range(local_halves):
        rows = packed[half // halves_each]
        tiles, _, width = slabs[half].shape
        for tile in range(tiles // 2):
            span = slice(tile * width, (tile + 1) * width)
            gate_out[half, :, span] = mm(rows, slabs[half][2 * tile])
            up_out[half, :, span] = mm(rows, slabs[half][2 * tile + 1])
            if half < len(ahead):
                copies[half][2 * tile].start()
                copies[half][2 * tile + 1].start()
    for copy in [copy for half in copies for copy in half]:
        copy.wait()


def first_part(blocks, mark, picked, gate, up, slabs):
    local_halves, _, hidden_count = gate.shape
    n_local, row_count, _ = picked.shape
    each, part_width, _ = slabs[0].shape
    hbm = pl.BlockSpec(memory_space=pltpu.HBM)
    sums = pltpu.VMEM((local_halves, row_count, hidden_count), F32)
    n_ahead = max(1, local_halves - 2)
    return pl.pallas_call(
        functools.partial(first_kernel, len(blocks), local_halves),
        out_shape=(pltpu.VMEM(slabs[0].shape, BF16),) * n_ahead
        + (sums, sums, jax.ShapeDtypeStruct((8, 128), F32)),
        in_specs=[vmem()] * (len(blocks) + 2) + [hbm, hbm] + [vmem()] * local_halves,
        out_specs=(vmem(),) * (n_ahead + 3),
        scratch_shapes=[
            pltpu.VMEM((n_local, row_count, part_width), BF16),
            pltpu.SemaphoreType.DMA((n_ahead, each)),
        ],
        input_output_aliases={len(blocks) + 4 + half: half for half in range(n_ahead)},
        cost_estimate=SMALL,
        compiler_params=params(max(LIMIT_EARLY, 10 * n_local * row_count * part_width // MIB)),
        name="gate_up_first",
    )(*blocks, mark, picked, gate, up, *[pltpu.with_memory_space_constraint(x, pltpu.VMEM) for x in slabs])


def second_kernel(n_blocks, n_ahead, n_ad, steps, *refs):
    blocks, refs = refs[:n_blocks], refs[n_blocks:]
    p_ref, gate_ref, up_ref, refs = *refs[1:4], refs[4:]
    ahead, gate_in, up_in, refs = refs[:n_ahead], refs[n_ahead], refs[n_ahead + 1], refs[n_ahead + 2 :]
    ids_ref, factors, tslot_ref, rows_ref, down_ref, refs = *refs[:5], refs[5:]
    hidden_ref, low_ref, refs = refs[0], refs[1], refs[2:]
    nexts, (packed, down_sems, late, sems) = refs[:-4], refs[-4:]
    n_local = p_ref.shape[0]
    local_halves, _, hidden_count = gate_ref.shape
    halves_each = local_halves // n_local
    slabs = list(ahead) + [late] * (local_halves - n_ahead)
    copies = {
        half: slab_copies(gate_ref, up_ref, slabs[half], sems, 1, half) for half in range(n_ahead, local_halves)
    }
    rank = RANK
    tenants = factors.shape[1] // rank
    down_copies = [
        down_fetch(n_ad, step, ids_ref, down_ref, nexts[number], down_sems.at[number]) for number, step in enumerate(steps)
    ]
    for copy in copies.get(n_ahead, []):
        copy.start()
    pack(blocks, p_ref, packed)
    for half in range(local_halves):
        rows = packed[half // halves_each]
        tiles, _, width = slabs[half].shape
        for tile in range(tiles // 2):
            span = slice(tile * width, (tile + 1) * width)
            values = []
            for number in (2 * tile, 2 * tile + 1):
                if half in copies:
                    copies[half][number].wait()
                values.append(mm(rows, slabs[half][number]))
                if half in copies and half + 1 in copies:
                    copies[half + 1][number].start()
            gate = values[0] + gate_in[half, :, span]
            up = values[1] + up_in[half, :, span]
            hidden_ref[half, :, span] = (silu(gate) * up).astype(BF16)
        for number, group in enumerate(down_copies):
            if half == min(local_halves - 1, number * n_ahead):
                for copy in group:
                    copy.start()
    for i in range(n_local):
        low = mm_nt(factors[i * halves_each], hidden_ref[i * halves_each])
        for half in range(i * halves_each + 1, (i + 1) * halves_each):
            low = low + mm_nt(factors[half], hidden_ref[half])
        owner = tslot_ref[i][0:1]
        total = jnp.zeros((rank, low.shape[1]), F32)
        for number in range(tenants):
            total = total + jnp.where(owner == number, low[number * rank : (number + 1) * rank], 0.0)
        weight = rows_ref[n_local + i : n_local + i + 1]
        low_ref[i * rank : (i + 1) * rank] = (mm(total.astype(BF16), p_ref[i]) * weight).astype(BF16)
    for copy in [copy for group in down_copies for copy in group]:
        copy.wait()


def second_part(
    blocks, mark, picked, gate, up, ahead, sums, ids, factors, tslot, table_rows, down, n_ad, steps
):
    local_halves, _, hidden_count = gate.shape
    n_local, row_count, count = picked.shape
    each, part_width, tile = ahead[0].shape
    rank = RANK
    hbm = pl.BlockSpec(memory_space=pltpu.HBM)
    held = [pltpu.with_memory_space_constraint(x, pltpu.VMEM) for x in (*ahead, *sums)]
    factors = pltpu.with_memory_space_constraint(factors, pltpu.VMEM)
    late_bytes = 2 * each * part_width * tile
    return pl.pallas_call(
        functools.partial(second_kernel, len(blocks), len(ahead), n_ad, steps),
        out_shape=(
            pltpu.VMEM((local_halves, row_count, hidden_count), BF16),
            jax.ShapeDtypeStruct((n_local * rank, count), BF16),
            *[down_slabs(down, n_ad, None if i == 0 else max(1, local_halves // 2)) for i in range(len(steps))],
        ),
        in_specs=[vmem()] * (len(blocks) + 2) + [hbm, hbm] + [vmem()] * len(held) + [smem()] + [vmem()] * 3 + [hbm],
        out_specs=(vmem(),) * (2 + len(steps)),
        scratch_shapes=[
            pltpu.VMEM((n_local, row_count, part_width), BF16),
            pltpu.SemaphoreType.DMA((len(steps), local_halves, 2)),
            pltpu.VMEM((each, part_width, tile), BF16),
            pltpu.SemaphoreType.DMA((local_halves, each)),
        ],
        cost_estimate=SMALL,
        compiler_params=params(
            max(LIMIT_EARLY, 10 * n_local * row_count * part_width // MIB) + late_bytes // MIB + 1
        ),
        name="gate_up_second",
    )(*blocks, mark, picked, gate, up, *held, ids, factors, tslot, table_rows, down)


def weighted_down(hidden_ref, weights, pt_ref, cols_ref):
    slabs = [ref.at[half] for ref in weights for half in range(ref.shape[0])]
    n_local = pt_ref.shape[0]
    halves_each = hidden_ref.shape[0] // n_local
    total = None
    for i in range(n_local):
        part_sum = mm(hidden_ref[i * halves_each], slabs[i * halves_each][...])
        for half in range(i * halves_each + 1, (i + 1) * halves_each):
            part_sum = part_sum + mm(hidden_ref[half], slabs[half][...])
        laid = mm(pt_ref[i], part_sum.astype(BF16)) * cols_ref[:, n_local + i : n_local + i + 1]
        total = laid if total is None else total + laid
    return total


def down_first_kernel(n_ad, step, ids_ref, hidden_ref, weight_ref, pt_ref, cols_ref, down_ref, keep, send, *refs):
    copies = []
    if refs:
        into, sems = refs
        copies = down_fetch(n_ad, step, ids_ref, down_ref, into, sems, 2, down_ref.shape[0] - into.shape[0])
    for copy in copies:
        copy.start()
    write_pairs(weighted_down(hidden_ref, [weight_ref], pt_ref, cols_ref), (keep, send))
    for copy in copies:
        copy.wait()


def down_first(ids, hidden, weights, pt, cols, down, n_ad, step, left):
    count, span = pt.shape[1], weights.shape[2]
    return pl.pallas_call(
        functools.partial(down_first_kernel, n_ad, step),
        out_shape=(jax.ShapeDtypeStruct((count // 2, span), BF16),) * 2
        + ((down_slabs(down, n_ad, left),) if left else ()),
        in_specs=[smem()] + [vmem()] * 4 + [pl.BlockSpec(memory_space=pltpu.HBM)],
        out_specs=(vmem(),) * (3 if left else 2),
        scratch_shapes=[pltpu.SemaphoreType.DMA((left, 2))] if left else [],
        cost_estimate=SMALL,
        compiler_params=params(max(LIMIT, 12 * count * span // MIB)),
        name="down_first",
    )(ids, hidden, pltpu.with_memory_space_constraint(weights, pltpu.VMEM), pt, cols, down)


def down_rest_kernel(n_weights, n_ad, steps, ids_ref, hidden_ref, pt_ref, cols_ref, down_ref, *refs):
    weights, (keep, send, base), refs = refs[:n_weights], refs[n_weights : n_weights + 3], refs[n_weights + 3 :]
    held, sems = refs[:-1], refs[-1]
    copies = [
        down_fetch(n_ad, step, ids_ref, down_ref, into, sems.at[number])
        for number, (step, into) in enumerate(zip(steps[1:], held))
    ]
    for copy in [copy for group in copies for copy in group]:
        copy.start()
    span = base.shape[1]
    for number in range(len(steps)):
        if number:
            for copy in copies[number - 1]:
                copy.wait()
        total = weighted_down(hidden_ref, [held[number - 1]] if number else weights, pt_ref, cols_ref)
        if number < len(steps) - 1:
            write_pairs(total, (keep, send), number * span)
        else:
            base[...] = total


def down_rest(ids, hidden, weights, pt, cols, down, n_ad, steps):
    count, span = pt.shape[1], down.shape[2] // n_ad
    chunk = (*down.shape[:2], span)
    return pl.pallas_call(
        functools.partial(down_rest_kernel, len(weights), n_ad, steps),
        out_shape=(jax.ShapeDtypeStruct((count // 2, span * (len(steps) - 1)), BF16),) * 2
        + (jax.ShapeDtypeStruct((count, span), F32),),
        in_specs=[smem()] + [vmem()] * 3 + [pl.BlockSpec(memory_space=pltpu.HBM)] + [vmem()] * len(weights),
        out_specs=(vmem(),) * 3,
        scratch_shapes=[pltpu.VMEM(chunk, BF16)] * (len(steps) - 1)
        + [pltpu.SemaphoreType.DMA((len(steps) - 1, down.shape[0], 2))],
        cost_estimate=SMALL,
        compiler_params=params(max(LIMIT, 12 * count * span // MIB) + (len(steps) - 1) * math.prod(chunk) * 2 // MIB),
        name="down_rest",
    )(ids, hidden, pt, cols, down, *[pltpu.with_memory_space_constraint(x, pltpu.VMEM) for x in weights])


def write_pairs(total, outs, at=0):
    keep, send = outs
    for b in range(total.shape[0] // 128):
        block = total[b * 128 : b * 128 + 128].astype(BF16)
        (send if b % 2 else keep)[b // 2 * 128 : b // 2 * 128 + 128, pl.ds(at, total.shape[1])] = block


def adapter_kernel(slot_column, local_halves, ids_ref, base_ref, cols_ref, factor_ref, low_ref, keep, send, wide):
    blocks = base_ref.shape[0] // 128
    height = low_ref.shape[0] // blocks
    wide[...] = jnp.zeros_like(wide)
    for m in range(blocks):
        row = pl.multiple_of(((ids_ref[0] ^ m) * local_halves // 2) * RANK, RANK)
        value = low_ref[m * height : (m + 1) * height].astype(F32)
        value = jnp.concatenate([value[:, (m ^ b) * 128 : (m ^ b) * 128 + 128] for b in range(blocks)], axis=1)
        wide[pl.ds(row, height)] += value
    low = wide[...].T.astype(BF16)
    zero = jnp.zeros_like(low)
    slot = cols_ref[:, slot_column : slot_column + 1]
    depth = EXPERT_COUNT * RANK
    slot_count = factor_ref.shape[0] // depth
    total = base_ref[...]
    for j in range(0, slot_count, 2):
        spread = jnp.concatenate(
            [jnp.where(slot == (ids_ref[0] * slot_count + j + i).astype(F32), low, zero) for i in range(2)], axis=1
        )
        total = total + mm(spread, factor_ref[j * depth : (j + 2) * depth])
    write_pairs(total, (keep, send))


def adapter_part(ids, base, cols, slot_column, local_halves, factors, low):
    count, span = base.shape
    return pl.pallas_call(
        functools.partial(adapter_kernel, slot_column, local_halves),
        out_shape=(jax.ShapeDtypeStruct((count // 2, span), BF16),) * 2,
        in_specs=[smem()] + [vmem()] * 4,
        out_specs=(vmem(),) * 2,
        scratch_shapes=[pltpu.VMEM((EXPERT_COUNT * RANK, count), F32)],
        cost_estimate=SMALL,
        compiler_params=params(max(LIMIT, 24 * count * span // MIB)),
        name="adapters",
    )(ids, base, cols, factors, low)


def split_kernel(keep_ref, came_ref, keep, send):
    for b in range(keep_ref.shape[0] // 128):
        total = keep_ref[b * 128 : b * 128 + 128].astype(F32) + came_ref[b * 128 : b * 128 + 128].astype(F32)
        (send if b % 2 else keep)[b // 2 * 128 : b // 2 * 128 + 128] = total.astype(BF16)


def split_sum(keep, came):
    return pl.pallas_call(
        split_kernel,
        out_shape=(jax.ShapeDtypeStruct((keep.shape[0] // 2, keep.shape[1]), BF16),) * 2,
        in_specs=[vmem()] * 2,
        out_specs=(vmem(),) * 2,
        cost_estimate=SMALL,
        compiler_params=params(LIMIT),
        name="sum_and_split",
    )(keep, came)


def cut_kernel(edges, keep_ref, came_ref, *outs):
    for first, last, out in zip(edges, edges[1:], outs):
        out[...] = (keep_ref[:, first:last].astype(F32) + came_ref[:, first:last].astype(F32)).astype(BF16)


def cut_sum(keep, came, edges):
    return pl.pallas_call(
        functools.partial(cut_kernel, edges),
        out_shape=tuple(
            jax.ShapeDtypeStruct((keep.shape[0], last - first), BF16) for first, last in zip(edges, edges[1:])
        ),
        in_specs=[vmem()] * 2,
        out_specs=(vmem(),) * (len(edges) - 1),
        cost_estimate=SMALL,
        compiler_params=params(LIMIT),
        name="sum_and_cut",
    )(keep, came)


def per_device(
    n_ep,
    n_ad,
    tokens,
    chosen_experts,
    router_gate_logits,
    token_tenant,
    adapter_of_tenant,
    adapter_pool_slot,
    gate_weight,
    up_weight,
    down_weight,
    adapter_input_factors,
    adapter_output_factors,
):
    gate_weight, up_weight, down_weight, adapter_input_factors = [
        pltpu.with_memory_space_constraint(x, pltpu.HBM)
        for x in (gate_weight, up_weight, down_weight, adapter_input_factors)
    ]
    width = tokens.shape[1]
    span = width // n_ad
    local_halves = gate_weight.shape[0]
    n_local = max(1, local_halves // 2)
    row_count = n_ep * CAP
    bits = n_ep.bit_length() - 1
    ids = jnp.stack([lax.axis_index("ep"), lax.axis_index("ad")]).astype(jnp.int32)

    def swap(x, mask):
        return lax.ppermute(x, "ep", [(i, i ^ mask) for i in range(n_ep)])

    def tie(x, y):
        return lax.optimization_barrier((x, y))

    def shift(x, step):
        return lax.ppermute(x, "ad", [(i, (i + step) % n_ad) for i in range(n_ad)])

    order = sorted(range(1, n_ad), key=lambda step: (step != n_ad // 2, step))
    token_part = token_parts_of(tokens, chosen_experts, router_gate_logits, token_tenant)
    *slabs, factors, mark = prefetch(
        ids, adapter_of_tenant, adapter_pool_slot, gate_weight, up_weight, adapter_input_factors, width // 2
    )
    high = 1 << (bits - 1)
    crossing = [swap(own, high) for own in token_part]

    def spread(part, crossed):
        blocks = {0: token_part[part], high: crossed}
        for bit in reversed(range(bits - 1)):
            for mask in list(blocks):
                blocks[mask | 1 << bit] = swap(blocks[mask], 1 << bit)
        return [blocks[mask] for mask in range(n_ep)]

    crossing[0], mark = tie(crossing[0], mark)
    blocks = spread(0, crossing[0])
    picked, pt, cols, table_rows, tslot = build_meta(
        blocks, ids, adapter_of_tenant, adapter_pool_slot, n_local, local_halves, row_count
    )
    *ahead, gate_sum, up_sum, mark = first_part(blocks, mark, picked, gate_weight, up_weight, slabs)
    crossing[1], mark = tie(crossing[1], mark)
    hidden, low, weights, *following = second_part(
        spread(1, crossing[1]), mark, picked, gate_weight, up_weight, ahead, (gate_sum, up_sum), ids, factors,
        tslot, table_rows, down_weight, n_ad, order[:2],
    )

    def onward(keep, came, first=1):
        for bit in range(first, bits):
            keep, send = split_sum(keep, came)
            came = swap(send, 1 << bit)
        return keep, came

    def other_of(low, bit):
        return lax.ppermute(low, "ad", [(i, i ^ 1 << bit) for i in range(n_ad)])

    def added(x, y):
        return (x.astype(F32) + y.astype(F32)).astype(BF16)

    far_steps = range(1, n_ad.bit_length() - 1)
    others = [other_of(low, bit) for bit in far_steps[:1]]
    left = local_halves - following[0].shape[0]
    keep, send, *later = down_first(ids, hidden, weights, pt, cols, down_weight, n_ad, order[1], left)
    others, keep, send, later = lax.optimization_barrier((others, keep, send, later))
    for bit in far_steps:
        low = added(low, others[0] if bit == 1 else other_of(low, bit))
    for bit in range(bits - 1):
        low = jnp.concatenate([low, swap(low, 1 << bit)], axis=0)
    crossed = swap(low, 1 << (bits - 1))
    keep, came = onward(keep, swap(send, 1), 1)
    keep, hidden = tie(keep, hidden)
    keep_rest, send_rest, base = down_rest(ids, hidden, following + later, pt, cols, down_weight, n_ad, (*order[1:], 0))
    came, crossed, keep_rest, send_rest, base = lax.optimization_barrier((came, crossed, keep_rest, send_rest, base))
    low = jnp.concatenate([low, crossed], axis=0)
    low = added(low, other_of(low, 0))
    (sums,) = cut_sum(keep, came, (0, span))
    results = [shift(sums, order[0])]
    keep_rest, came_rest = onward(keep_rest, swap(send_rest, 1))
    slot_count = adapter_output_factors.shape[0]
    flat_factors = adapter_output_factors.reshape(slot_count * EXPERT_COUNT * RANK, span)
    keep, send = adapter_part(ids, base, cols, 2 * n_local, local_halves, flat_factors, low)
    came_rest, results, keep, send = lax.optimization_barrier((came_rest, results, keep, send))
    came = swap(send, 1)
    if bits > 1:
        keep, send = split_sum(keep, came)
        came_rest, keep, send = lax.optimization_barrier((came_rest, keep, send))
        came = swap(send, 2)
    keep, came = onward(keep, came, 2)
    parts = cut_sum(keep_rest, came_rest, [span * i for i in range(n_ad - 1)])
    results += [shift(x, step) for x, step in zip(parts, order[1:])]
    return sum(x.astype(F32) for x in [keep, came] + results).astype(BF16)


def solution(mesh):
    placed = (
        P(("rep", "ep"), None),
        P(("rep", "ep"), None),
        P(("rep", "ep"), None),
        P(("rep", "ep")),
        P("rep"),
        P(),
        P("ep", None, "ad"),
        P("ep", None, "ad"),
        P("ep", "ad", None),
        P(None, "ep", None, "ad"),
        P("ep", None, None, "ad"),
    )
    return jax.shard_map(
        functools.partial(per_device, mesh.shape["ep"], mesh.shape["ad"]),
        mesh=mesh,
        in_specs=placed,
        out_specs=P(("rep", "ep"), "ad"),
        check_vma=False,
    )
```

```python
import functools
import math

import jax
import jax.numpy as jnp
from jax import lax
from jax.experimental import pallas as pl
from jax.experimental.pallas import tpu as pltpu
from jax.sharding import PartitionSpec as P

EXPERT_COUNT = 8
TOP = 2
RANK = 16
CAP = 48
LIMIT = 16
LIMIT_EARLY = 8
N_TILE = 512
MIB = 1 << 20

F32 = jnp.float32
BF16 = jnp.bfloat16


def mm(a, b):
    return jnp.dot(a, b, preferred_element_type=F32)


def mm_nt(a, b):
    return lax.dot_general(a, b, (((1,), (1,)), ((), ())), preferred_element_type=F32)


SMALL = pl.CostEstimate(flops=1, bytes_accessed=1, transcendentals=0)


def silu(x):
    half = 0.5 * x
    return half + half * jnp.tanh(half)


def params(mib):
    return pltpu.CompilerParams(vmem_limit_bytes=mib * MIB)


def vmem():
    return pl.BlockSpec(memory_space=pltpu.VMEM)


def smem():
    return pl.BlockSpec(memory_space=pltpu.SMEM)


def parts_kernel(tokens_ref, chosen_in, logits_in, tenant_in, first_ref, second_ref, chosen_ref, logits_ref, tenant_ref, sems):
    rows, width = second_ref.shape
    copies = [
        pltpu.make_async_copy(tokens_ref.at[:, pl.ds(0, width)], first_ref.at[:, pl.ds(0, width)], sems.at[0]),
        pltpu.make_async_copy(tokens_ref.at[:, pl.ds(width, width)], second_ref, sems.at[1]),
    ]
    small = [
        pltpu.make_async_copy(source, into, sems.at[2 + number])
        for number, (source, into) in enumerate(
            [(chosen_in, chosen_ref), (logits_in, logits_ref), (tenant_in, tenant_ref)]
        )
    ]
    for copy in small + copies:
        copy.start()
    for copy in small:
        copy.wait()
    diagonal = lax.broadcasted_iota(jnp.int32, (rows, rows), 0) == lax.broadcasted_iota(jnp.int32, (rows, rows), 1)

    def column(row):
        return jnp.sum(jnp.where(diagonal, row, 0.0), axis=1, keepdims=True)

    chosen, logits = chosen_ref[...].astype(F32), logits_ref[...]
    columns = [column(chosen[0:1]), column(chosen[1:2]), column(tenant_ref[...].astype(F32))]
    rests = [column(logits[0:1]), column(logits[1:2])]
    for _ in range(3):
        pieces = [rest.astype(BF16).astype(F32) for rest in rests]
        columns += pieces
        rests = [rest - piece for rest, piece in zip(rests, pieces)]
    lane = lax.broadcasted_iota(jnp.int32, (rows, 128), 1)
    facts = jnp.zeros((rows, 128), F32)
    for number, value in enumerate(columns):
        facts = jnp.where(lane == number, value, facts)
    first_ref[:, width:] = facts.astype(BF16)
    for copy in copies:
        copy.wait()


def token_parts_of(tokens, chosen_experts, logits, tenant):
    rows, width = tokens.shape[0], tokens.shape[1] // 2
    return pl.pallas_call(
        parts_kernel,
        out_shape=(
            jax.ShapeDtypeStruct((rows, width + 128), BF16),
            jax.ShapeDtypeStruct((rows, width), BF16),
        ),
        in_specs=[pl.BlockSpec(memory_space=pltpu.HBM)] * 4,
        out_specs=(vmem(),) * 2,
        scratch_shapes=[
            pltpu.VMEM((2, rows), jnp.int32),
            pltpu.VMEM((2, rows), F32),
            pltpu.VMEM((1, rows), jnp.int32),
            pltpu.SemaphoreType.DMA((5,)),
        ],
        cost_estimate=SMALL,
        compiler_params=params(LIMIT_EARLY),
        name="token_parts",
    )(
        *[
            pltpu.with_memory_space_constraint(x, pltpu.HBM)
            for x in (tokens, chosen_experts.T, logits.T, tenant.reshape(1, rows))
        ]
    )


def meta_kernel(n_local, local_halves, ids_ref, adapter_ref, pool_slot_ref, *refs):
    blocks, (p_ref, pt_ref, cols_ref, rows_ref, tslot_ref) = refs[:-5], refs[-5:]
    at = blocks[0].shape[1] - 128
    facts = jnp.concatenate([block[:, at:] for block in blocks], axis=0).astype(F32).T
    count = facts.shape[1]
    first, second, tenant = facts[0:1], facts[1:2], facts[2:3]
    logit_first = (facts[3:4] + facts[5:6]) + facts[7:8]
    logit_second = (facts[4:5] + facts[6:7]) + facts[8:9]
    weight_first = jax.nn.sigmoid(logit_first - logit_second)
    weight_second = jax.nn.sigmoid(logit_second - logit_first)
    slot = jnp.zeros_like(tenant)
    for number in range(adapter_ref.shape[0]):
        slot = jnp.where(tenant == number, pool_slot_ref[adapter_ref[number]].astype(F32), slot)
    members, weights = [], []
    for i in range(n_local):
        expert = (ids_ref[0] * local_halves // 2 + i).astype(F32)
        hit_first, hit_second = first == expert, second == expert
        members.append(jnp.where(hit_first | hit_second, 1.0, 0.0))
        weights.append(jnp.where(hit_first, weight_first, 0.0) + jnp.where(hit_second, weight_second, 0.0))
    member = jnp.concatenate(members + [jnp.zeros((8 - n_local, count), F32)], axis=0)
    before = (
        lax.broadcasted_iota(jnp.int32, (count, count), 0) < lax.broadcasted_iota(jnp.int32, (count, count), 1)
    ).astype(BF16)
    place = jnp.where(member > 0, mm(member.astype(BF16), before), -1.0)
    table = jnp.concatenate(
        [place[0:n_local]] + weights + [slot] + [jnp.zeros((127 - 2 * n_local, count), F32)], axis=0
    )
    columns = table.T
    cols_ref[...] = columns
    rows_ref[...] = table[0:8]
    row_count = p_ref.shape[1]
    tenant_rows = jnp.broadcast_to(tenant, (8, count)).astype(BF16)
    down = lax.broadcasted_iota(jnp.int32, (row_count, count), 0).astype(F32)
    across = lax.broadcasted_iota(jnp.int32, (count, row_count), 1).astype(F32)
    for i in range(n_local):
        picked = (down == place[i : i + 1]).astype(BF16)
        p_ref[i] = picked
        pt_ref[i] = (across == columns[:, i : i + 1]).astype(BF16)
        tslot_ref[i] = mm_nt(tenant_rows, picked)


def build_meta(blocks, ids, adapters, pool_slots, n_local, local_halves, row_count):
    count = sum(block.shape[0] for block in blocks)
    return pl.pallas_call(
        functools.partial(meta_kernel, n_local, local_halves),
        out_shape=(
            jax.ShapeDtypeStruct((n_local, row_count, count), BF16),
            jax.ShapeDtypeStruct((n_local, count, row_count), BF16),
            jax.ShapeDtypeStruct((count, 128), F32),
            jax.ShapeDtypeStruct((8, count), F32),
            jax.ShapeDtypeStruct((n_local, 8, row_count), F32),
        ),
        in_specs=[smem()] * 3 + [vmem()] * len(blocks),
        out_specs=(vmem(),) * 5,
        cost_estimate=SMALL,
        compiler_params=params(max(LIMIT_EARLY, 12 * count * count // MIB)),
        name="routing_tables",
    )(ids, adapters, pool_slots, *blocks)


def slab_copies(gate_ref, up_ref, into_ref, sems, part, half):
    depth, width = into_ref.shape[1], into_ref.shape[2]
    copies = []
    for number in range(into_ref.shape[0]):
        source = (gate_ref, up_ref)[number % 2].at[half, pl.ds(part * depth, depth), pl.ds(number // 2 * width, width)]
        copies.append(pltpu.make_async_copy(source, into_ref.at[number], sems.at[half, number]))
    return copies


def prefetch_kernel(ids_ref, adapter_ref, pool_slot_ref, gate_ref, up_ref, pool_ref, *refs):
    slabs, (factors, mark_ref, sems, factor_sems) = refs[:-4], refs[-4:]
    copies = [copy for half, slab in enumerate(slabs) for copy in slab_copies(gate_ref, up_ref, slab, sems, 0, half)]
    rank = pool_ref.shape[2]
    for number in range(adapter_ref.shape[0]):
        source = pool_ref.at[pool_slot_ref[adapter_ref[number]]]
        into = factors.at[:, number * rank : (number + 1) * rank]
        copies.append(pltpu.make_async_copy(source, into, factor_sems.at[number]))
    for copy in copies:
        copy.start()
    mark_ref[...] = jnp.zeros_like(mark_ref)
    for copy in copies:
        copy.wait()


def prefetch(ids, adapters, pool_slots, gate, up, pool, part_width):
    local_halves, _, hidden_count = gate.shape
    tile = min(N_TILE, hidden_count)
    each = 2 * hidden_count // tile
    tenants, rank = adapters.shape[0], pool.shape[2]
    return pl.pallas_call(
        prefetch_kernel,
        out_shape=(pltpu.VMEM((each, part_width, tile), BF16),) * local_halves
        + (pltpu.VMEM((local_halves, tenants * rank, hidden_count), BF16), jax.ShapeDtypeStruct((8, 128), F32)),
        in_specs=[smem()] * 3 + [pl.BlockSpec(memory_space=pltpu.HBM)] * 3,
        out_specs=(vmem(),) * (local_halves + 2),
        scratch_shapes=[pltpu.SemaphoreType.DMA((local_halves, each)), pltpu.SemaphoreType.DMA((tenants,))],
        cost_estimate=SMALL,
        compiler_params=params(LIMIT_EARLY),
        name="weight_prefetch",
    )(ids, adapters, pool_slots, gate, up, pool)


def pack(blocks, p_ref, packed):
    depth = packed.shape[2]
    whole = jnp.concatenate([block[:, :depth] for block in blocks], axis=0)
    for i in range(p_ref.shape[0]):
        packed[i] = mm(p_ref[i], whole).astype(BF16)


def down_slabs(down, n_ad, halves=None):
    return pltpu.VMEM((halves or down.shape[0], down.shape[1], down.shape[2] // n_ad), BF16)


def down_fetch(n_ad, step, ids_ref, down_ref, into_ref, sems, pieces=2, first=0):
    halves, rows, span = into_ref.shape
    rows = rows // pieces
    start = pl.multiple_of(lax.rem(ids_ref[1] + step, n_ad) * span, span)
    return [
        pltpu.make_async_copy(
            down_ref.at[first + half, pl.ds(i * rows, rows), pl.ds(start, span)],
            into_ref.at[half, pl.ds(i * rows, rows)],
            sems.at[half, i],
        )
        for half in range(halves)
        for i in range(pieces)
    ]


def first_kernel(n_blocks, local_halves, *refs):
    blocks, refs = refs[:n_blocks], refs[n_blocks:]
    _, p_ref, gate_ref, up_ref, refs = *refs[:4], refs[4:]
    slabs, refs = refs[:local_halves], refs[local_halves:]
    ahead, (gate_out, up_out, mark_out, packed, sems) = refs[:-5], refs[-5:]
    mark_out[...] = jnp.zeros_like(mark_out)
    pack(blocks, p_ref, packed)
    slabs = list(ahead) + list(slabs[len(ahead) :])
    copies = [slab_copies(gate_ref, up_ref, slab, sems, 1, half) for half, slab in enumerate(ahead)]
    halves_each = local_halves // p_ref.shape[0]
    for half in range(local_halves):
        rows = packed[half // halves_each]
        tiles, _, width = slabs[half].shape
        for tile in range(tiles // 2):
            span = slice(tile * width, (tile + 1) * width)
            gate_out[half, :, span] = mm(rows, slabs[half][2 * tile])
            up_out[half, :, span] = mm(rows, slabs[half][2 * tile + 1])
            if half < len(ahead):
                copies[half][2 * tile].start()
                copies[half][2 * tile + 1].start()
    for copy in [copy for half in copies for copy in half]:
        copy.wait()


def first_part(blocks, mark, picked, gate, up, slabs):
    local_halves, _, hidden_count = gate.shape
    n_local, row_count, _ = picked.shape
    each, part_width, _ = slabs[0].shape
    hbm = pl.BlockSpec(memory_space=pltpu.HBM)
    sums = pltpu.VMEM((local_halves, row_count, hidden_count), F32)
    n_ahead = max(1, local_halves - 2)
    return pl.pallas_call(
        functools.partial(first_kernel, len(blocks), local_halves),
        out_shape=(pltpu.VMEM(slabs[0].shape, BF16),) * n_ahead
        + (sums, sums, jax.ShapeDtypeStruct((8, 128), F32)),
        in_specs=[vmem()] * (len(blocks) + 2) + [hbm, hbm] + [vmem()] * local_halves,
        out_specs=(vmem(),) * (n_ahead + 3),
        scratch_shapes=[
            pltpu.VMEM((n_local, row_count, part_width), BF16),
            pltpu.SemaphoreType.DMA((n_ahead, each)),
        ],
        input_output_aliases={len(blocks) + 4 + half: half for half in range(n_ahead)},
        cost_estimate=SMALL,
        compiler_params=params(max(LIMIT_EARLY, 10 * n_local * row_count * part_width // MIB)),
        name="gate_up_first",
    )(*blocks, mark, picked, gate, up, *[pltpu.with_memory_space_constraint(x, pltpu.VMEM) for x in slabs])


def second_kernel(n_blocks, n_ahead, n_ad, steps, *refs):
    blocks, refs = refs[:n_blocks], refs[n_blocks:]
    p_ref, gate_ref, up_ref, refs = *refs[1:4], refs[4:]
    ahead, gate_in, up_in, refs = refs[:n_ahead], refs[n_ahead], refs[n_ahead + 1], refs[n_ahead + 2 :]
    ids_ref, factors, tslot_ref, rows_ref, down_ref, refs = *refs[:5], refs[5:]
    hidden_ref, low_ref, refs = refs[0], refs[1], refs[2:]
    nexts, (packed, down_sems, late, sems) = refs[:-4], refs[-4:]
    n_local = p_ref.shape[0]
    local_halves, _, hidden_count = gate_ref.shape
    halves_each = local_halves // n_local
    slabs = list(ahead) + [late] * (local_halves - n_ahead)
    copies = {
        half: slab_copies(gate_ref, up_ref, slabs[half], sems, 1, half) for half in range(n_ahead, local_halves)
    }
    rank = RANK
    tenants = factors.shape[1] // rank
    down_copies = []
    for number, step in enumerate(steps):
        down_copies += down_fetch(n_ad, step, ids_ref, down_ref, nexts[number], down_sems.at[number], 1)
    for copy in copies.get(n_ahead, []) + down_copies:
        copy.start()
    pack(blocks, p_ref, packed)
    for half in range(local_halves):
        rows = packed[half // halves_each]
        tiles, _, width = slabs[half].shape
        for tile in range(tiles // 2):
            span = slice(tile * width, (tile + 1) * width)
            values = []
            for number in (2 * tile, 2 * tile + 1):
                if half in copies:
                    copies[half][number].wait()
                values.append(mm(rows, slabs[half][number]))
                if half in copies and half + 1 in copies:
                    copies[half + 1][number].start()
            gate = values[0] + gate_in[half, :, span]
            up = values[1] + up_in[half, :, span]
            hidden_ref[half, :, span] = (silu(gate) * up).astype(BF16)
    for i in range(n_local):
        low = mm_nt(factors[i * halves_each], hidden_ref[i * halves_each])
        for half in range(i * halves_each + 1, (i + 1) * halves_each):
            low = low + mm_nt(factors[half], hidden_ref[half])
        owner = tslot_ref[i][0:1]
        total = jnp.zeros((rank, low.shape[1]), F32)
        for number in range(tenants):
            total = total + jnp.where(owner == number, low[number * rank : (number + 1) * rank], 0.0)
        weight = rows_ref[n_local + i : n_local + i + 1]
        low_ref[i * rank : (i + 1) * rank] = (mm(total.astype(BF16), p_ref[i]) * weight).astype(BF16)
    for copy in down_copies:
        copy.wait()


def second_part(
    blocks, mark, picked, gate, up, ahead, sums, ids, factors, tslot, table_rows, down, n_ad, steps
):
    local_halves, _, hidden_count = gate.shape
    n_local, row_count, count = picked.shape
    each, part_width, tile = ahead[0].shape
    rank = RANK
    hbm = pl.BlockSpec(memory_space=pltpu.HBM)
    held = [pltpu.with_memory_space_constraint(x, pltpu.VMEM) for x in (*ahead, *sums)]
    factors = pltpu.with_memory_space_constraint(factors, pltpu.VMEM)
    late_bytes = 2 * each * part_width * tile
    return pl.pallas_call(
        functools.partial(second_kernel, len(blocks), len(ahead), n_ad, steps),
        out_shape=(
            pltpu.VMEM((local_halves, row_count, hidden_count), BF16),
            jax.ShapeDtypeStruct((n_local * rank, count), BF16),
            *[down_slabs(down, n_ad, None if i == 0 else max(1, local_halves // 2)) for i in range(len(steps))],
        ),
        in_specs=[vmem()] * (len(blocks) + 2) + [hbm, hbm] + [vmem()] * len(held) + [smem()] + [vmem()] * 3 + [hbm],
        out_specs=(vmem(),) * (2 + len(steps)),
        scratch_shapes=[
            pltpu.VMEM((n_local, row_count, part_width), BF16),
            pltpu.SemaphoreType.DMA((len(steps), local_halves, 2)),
            pltpu.VMEM((each, part_width, tile), BF16),
            pltpu.SemaphoreType.DMA((local_halves, each)),
        ],
        cost_estimate=SMALL,
        compiler_params=params(
            max(LIMIT_EARLY, 10 * n_local * row_count * part_width // MIB) + late_bytes // MIB + 1
        ),
        name="gate_up_second",
    )(*blocks, mark, picked, gate, up, *held, ids, factors, tslot, table_rows, down)


def weighted_down(hidden_ref, weights, pt_ref, cols_ref):
    slabs = [ref.at[half] for ref in weights for half in range(ref.shape[0])]
    n_local = pt_ref.shape[0]
    halves_each = hidden_ref.shape[0] // n_local
    total = None
    for i in range(n_local):
        part_sum = mm(hidden_ref[i * halves_each], slabs[i * halves_each][...])
        for half in range(i * halves_each + 1, (i + 1) * halves_each):
            part_sum = part_sum + mm(hidden_ref[half], slabs[half][...])
        laid = mm(pt_ref[i], part_sum.astype(BF16)) * cols_ref[:, n_local + i : n_local + i + 1]
        total = laid if total is None else total + laid
    return total


def down_first_kernel(n_ad, step, ids_ref, hidden_ref, weight_ref, pt_ref, cols_ref, down_ref, keep, send, *refs):
    copies = []
    if refs:
        into, sems = refs
        copies = down_fetch(n_ad, step, ids_ref, down_ref, into, sems, 2, down_ref.shape[0] - into.shape[0])
    for copy in copies:
        copy.start()
    write_pairs(weighted_down(hidden_ref, [weight_ref], pt_ref, cols_ref), (keep, send))
    for copy in copies:
        copy.wait()


def down_first(ids, hidden, weights, pt, cols, down, n_ad, step, left):
    count, span = pt.shape[1], weights.shape[2]
    return pl.pallas_call(
        functools.partial(down_first_kernel, n_ad, step),
        out_shape=(jax.ShapeDtypeStruct((count // 2, span), BF16),) * 2
        + ((down_slabs(down, n_ad, left),) if left else ()),
        in_specs=[smem()] + [vmem()] * 4 + [pl.BlockSpec(memory_space=pltpu.HBM)],
        out_specs=(vmem(),) * (3 if left else 2),
        scratch_shapes=[pltpu.SemaphoreType.DMA((left, 2))] if left else [],
        cost_estimate=SMALL,
        compiler_params=params(max(LIMIT, 12 * count * span // MIB)),
        name="down_first",
    )(ids, hidden, pltpu.with_memory_space_constraint(weights, pltpu.VMEM), pt, cols, down)


def down_rest_kernel(n_weights, n_ad, steps, ids_ref, hidden_ref, pt_ref, cols_ref, down_ref, *refs):
    weights, (keep, send, base), refs = refs[:n_weights], refs[n_weights : n_weights + 3], refs[n_weights + 3 :]
    held, sems = refs[:-1], refs[-1]
    copies = [
        down_fetch(n_ad, step, ids_ref, down_ref, into, sems.at[number])
        for number, (step, into) in enumerate(zip(steps[1:], held))
    ]
    for copy in [copy for group in copies for copy in group]:
        copy.start()
    span = base.shape[1]
    for number in range(len(steps)):
        if number:
            for copy in copies[number - 1]:
                copy.wait()
        total = weighted_down(hidden_ref, [held[number - 1]] if number else weights, pt_ref, cols_ref)
        if number < len(steps) - 1:
            write_pairs(total, (keep, send), number * span)
        else:
            base[...] = total


def down_rest(ids, hidden, weights, pt, cols, down, n_ad, steps):
    count, span = pt.shape[1], down.shape[2] // n_ad
    chunk = (*down.shape[:2], span)
    return pl.pallas_call(
        functools.partial(down_rest_kernel, len(weights), n_ad, steps),
        out_shape=(jax.ShapeDtypeStruct((count // 2, span * (len(steps) - 1)), BF16),) * 2
        + (jax.ShapeDtypeStruct((count, span), F32),),
        in_specs=[smem()] + [vmem()] * 3 + [pl.BlockSpec(memory_space=pltpu.HBM)] + [vmem()] * len(weights),
        out_specs=(vmem(),) * 3,
        scratch_shapes=[pltpu.VMEM(chunk, BF16)] * (len(steps) - 1)
        + [pltpu.SemaphoreType.DMA((len(steps) - 1, down.shape[0], 2))],
        cost_estimate=SMALL,
        compiler_params=params(max(LIMIT, 12 * count * span // MIB) + (len(steps) - 1) * math.prod(chunk) * 2 // MIB),
        name="down_rest",
    )(ids, hidden, pt, cols, down, *[pltpu.with_memory_space_constraint(x, pltpu.VMEM) for x in weights])


def write_pairs(total, outs, at=0):
    keep, send = outs
    for b in range(total.shape[0] // 128):
        block = total[b * 128 : b * 128 + 128].astype(BF16)
        (send if b % 2 else keep)[b // 2 * 128 : b // 2 * 128 + 128, pl.ds(at, total.shape[1])] = block


def adapter_kernel(slot_column, local_halves, ids_ref, base_ref, cols_ref, factor_ref, low_ref, keep, send, wide):
    blocks = base_ref.shape[0] // 128
    height = low_ref.shape[0] // blocks
    wide[...] = jnp.zeros_like(wide)
    for m in range(blocks):
        row = pl.multiple_of(((ids_ref[0] ^ m) * local_halves // 2) * RANK, RANK)
        value = low_ref[m * height : (m + 1) * height].astype(F32)
        value = jnp.concatenate([value[:, (m ^ b) * 128 : (m ^ b) * 128 + 128] for b in range(blocks)], axis=1)
        wide[pl.ds(row, height)] += value
    low = wide[...].T.astype(BF16)
    zero = jnp.zeros_like(low)
    slot = cols_ref[:, slot_column : slot_column + 1]
    depth = EXPERT_COUNT * RANK
    slot_count = factor_ref.shape[0] // depth
    total = base_ref[...]
    for j in range(0, slot_count, 2):
        spread = jnp.concatenate(
            [jnp.where(slot == (ids_ref[0] * slot_count + j + i).astype(F32), low, zero) for i in range(2)], axis=1
        )
        total = total + mm(spread, factor_ref[j * depth : (j + 2) * depth])
    write_pairs(total, (keep, send))


def adapter_part(ids, base, cols, slot_column, local_halves, factors, low):
    count, span = base.shape
    return pl.pallas_call(
        functools.partial(adapter_kernel, slot_column, local_halves),
        out_shape=(jax.ShapeDtypeStruct((count // 2, span), BF16),) * 2,
        in_specs=[smem()] + [vmem()] * 4,
        out_specs=(vmem(),) * 2,
        scratch_shapes=[pltpu.VMEM((EXPERT_COUNT * RANK, count), F32)],
        cost_estimate=SMALL,
        compiler_params=params(max(LIMIT, 24 * count * span // MIB)),
        name="adapters",
    )(ids, base, cols, factors, low)


def split_kernel(keep_ref, came_ref, keep, send):
    for b in range(keep_ref.shape[0] // 128):
        total = keep_ref[b * 128 : b * 128 + 128].astype(F32) + came_ref[b * 128 : b * 128 + 128].astype(F32)
        (send if b % 2 else keep)[b // 2 * 128 : b // 2 * 128 + 128] = total.astype(BF16)


def split_sum(keep, came):
    return pl.pallas_call(
        split_kernel,
        out_shape=(jax.ShapeDtypeStruct((keep.shape[0] // 2, keep.shape[1]), BF16),) * 2,
        in_specs=[vmem()] * 2,
        out_specs=(vmem(),) * 2,
        cost_estimate=SMALL,
        compiler_params=params(LIMIT),
        name="sum_and_split",
    )(keep, came)


def cut_kernel(edges, keep_ref, came_ref, *outs):
    for first, last, out in zip(edges, edges[1:], outs):
        out[...] = (keep_ref[:, first:last].astype(F32) + came_ref[:, first:last].astype(F32)).astype(BF16)


def cut_sum(keep, came, edges):
    return pl.pallas_call(
        functools.partial(cut_kernel, edges),
        out_shape=tuple(
            jax.ShapeDtypeStruct((keep.shape[0], last - first), BF16) for first, last in zip(edges, edges[1:])
        ),
        in_specs=[vmem()] * 2,
        out_specs=(vmem(),) * (len(edges) - 1),
        cost_estimate=SMALL,
        compiler_params=params(LIMIT),
        name="sum_and_cut",
    )(keep, came)


def per_device(
    n_ep,
    n_ad,
    tokens,
    chosen_experts,
    router_gate_logits,
    token_tenant,
    adapter_of_tenant,
    adapter_pool_slot,
    gate_weight,
    up_weight,
    down_weight,
    adapter_input_factors,
    adapter_output_factors,
):
    gate_weight, up_weight, down_weight, adapter_input_factors = [
        pltpu.with_memory_space_constraint(x, pltpu.HBM)
        for x in (gate_weight, up_weight, down_weight, adapter_input_factors)
    ]
    width = tokens.shape[1]
    span = width // n_ad
    local_halves = gate_weight.shape[0]
    n_local = max(1, local_halves // 2)
    row_count = n_ep * CAP
    bits = n_ep.bit_length() - 1
    ids = jnp.stack([lax.axis_index("ep"), lax.axis_index("ad")]).astype(jnp.int32)

    def swap(x, mask):
        return lax.ppermute(x, "ep", [(i, i ^ mask) for i in range(n_ep)])

    def tie(x, y):
        return lax.optimization_barrier((x, y))

    def shift(x, step):
        return lax.ppermute(x, "ad", [(i, (i + step) % n_ad) for i in range(n_ad)])

    order = list(range(1, n_ad))
    token_part = token_parts_of(tokens, chosen_experts, router_gate_logits, token_tenant)
    *slabs, factors, mark = prefetch(
        ids, adapter_of_tenant, adapter_pool_slot, gate_weight, up_weight, adapter_input_factors, width // 2
    )
    high = 1 << (bits - 1)
    crossing = [swap(own, high) for own in token_part]

    def spread(part, crossed):
        blocks = {0: token_part[part], high: crossed}
        for bit in reversed(range(bits - 1)):
            for mask in list(blocks):
                blocks[mask | 1 << bit] = swap(blocks[mask], 1 << bit)
        return [blocks[mask] for mask in range(n_ep)]

    crossing[0], mark = tie(crossing[0], mark)
    blocks = spread(0, crossing[0])
    picked, pt, cols, table_rows, tslot = build_meta(
        blocks, ids, adapter_of_tenant, adapter_pool_slot, n_local, local_halves, row_count
    )
    *ahead, gate_sum, up_sum, mark = first_part(blocks, mark, picked, gate_weight, up_weight, slabs)
    crossing[1], mark = tie(crossing[1], mark)
    hidden, low, weights, *following = second_part(
        spread(1, crossing[1]), mark, picked, gate_weight, up_weight, ahead, (gate_sum, up_sum), ids, factors,
        tslot, table_rows, down_weight, n_ad, order[:2],
    )

    def onward(keep, came, first=1):
        for bit in range(first, bits):
            keep, send = split_sum(keep, came)
            came = swap(send, 1 << bit)
        return keep, came

    def other_of(low, bit):
        return lax.ppermute(low, "ad", [(i, i ^ 1 << bit) for i in range(n_ad)])

    def added(x, y):
        return (x.astype(F32) + y.astype(F32)).astype(BF16)

    far_steps = range(1, n_ad.bit_length() - 1)
    others = [other_of(low, bit) for bit in far_steps[:1]]
    left = local_halves - following[0].shape[0]
    keep, send, *later = down_first(ids, hidden, weights, pt, cols, down_weight, n_ad, order[1], left)
    others, keep, send, later = lax.optimization_barrier((others, keep, send, later))
    for bit in far_steps:
        low = added(low, others[0] if bit == 1 else other_of(low, bit))
    for bit in range(bits - 1):
        low = jnp.concatenate([low, swap(low, 1 << bit)], axis=0)
    crossed = swap(low, 1 << (bits - 1))
    keep, came = onward(keep, swap(send, 1), 1)
    keep, hidden = tie(keep, hidden)
    keep_rest, send_rest, base = down_rest(ids, hidden, following + later, pt, cols, down_weight, n_ad, (*order[1:], 0))
    came, crossed, keep_rest, send_rest, base = lax.optimization_barrier((came, crossed, keep_rest, send_rest, base))
    low = jnp.concatenate([low, crossed], axis=0)
    low = added(low, other_of(low, 0))
    (sums,) = cut_sum(keep, came, (0, span))
    results = [shift(sums, order[0])]
    keep_rest, came_rest = onward(keep_rest, swap(send_rest, 1))
    slot_count = adapter_output_factors.shape[0]
    flat_factors = adapter_output_factors.reshape(slot_count * EXPERT_COUNT * RANK, span)
    keep, send = adapter_part(ids, base, cols, 2 * n_local, local_halves, flat_factors, low)
    came_rest, results, keep, send = lax.optimization_barrier((came_rest, results, keep, send))
    came = swap(send, 1)
    if bits > 1:
        keep, send = split_sum(keep, came)
        came_rest, keep, send = lax.optimization_barrier((came_rest, keep, send))
        came = swap(send, 2)
    keep, came = onward(keep, came, 2)
    parts = cut_sum(keep_rest, came_rest, [span * i for i in range(n_ad - 1)])
    results += [shift(x, step) for x, step in zip(parts, order[1:])]
    return sum(x.astype(F32) for x in [keep, came] + results).astype(BF16)


def solution(mesh):
    placed = (
        P(("rep", "ep"), None),
        P(("rep", "ep"), None),
        P(("rep", "ep"), None),
        P(("rep", "ep")),
        P("rep"),
        P(),
        P("ep", None, "ad"),
        P("ep", None, "ad"),
        P("ep", "ad", None),
        P(None, "ep", None, "ad"),
        P("ep", None, None, "ad"),
    )
    return jax.shard_map(
        functools.partial(per_device, mesh.shape["ep"], mesh.shape["ad"]),
        mesh=mesh,
        in_specs=placed,
        out_specs=P(("rep", "ep"), "ad"),
        check_vma=False,
    )
```

```python
import functools
import math

import jax
import jax.numpy as jnp
from jax import lax
from jax.experimental import pallas as pl
from jax.experimental.pallas import tpu as pltpu
from jax.sharding import PartitionSpec as P

EXPERT_COUNT = 8
TOP = 2
RANK = 16
CAP = 48
LIMIT = 16
LIMIT_EARLY = 8
N_TILE = 512
MIB = 1 << 20

F32 = jnp.float32
BF16 = jnp.bfloat16


def mm(a, b):
    return jnp.dot(a, b, preferred_element_type=F32)


def mm_nt(a, b):
    return lax.dot_general(a, b, (((1,), (1,)), ((), ())), preferred_element_type=F32)


SMALL = pl.CostEstimate(flops=1, bytes_accessed=1, transcendentals=0)


def silu(x):
    half = 0.5 * x
    return half + half * jnp.tanh(half)


def params(mib):
    return pltpu.CompilerParams(vmem_limit_bytes=mib * MIB)


def vmem():
    return pl.BlockSpec(memory_space=pltpu.VMEM)


def smem():
    return pl.BlockSpec(memory_space=pltpu.SMEM)


def parts_kernel(tokens_ref, chosen_in, logits_in, tenant_in, first_ref, second_ref, chosen_ref, logits_ref, tenant_ref, sems):
    rows, width = second_ref.shape
    copies = [
        pltpu.make_async_copy(tokens_ref.at[:, pl.ds(0, width)], first_ref.at[:, pl.ds(0, width)], sems.at[0]),
        pltpu.make_async_copy(tokens_ref.at[:, pl.ds(width, width)], second_ref, sems.at[1]),
    ]
    small = [
        pltpu.make_async_copy(source, into, sems.at[2 + number])
        for number, (source, into) in enumerate(
            [(chosen_in, chosen_ref), (logits_in, logits_ref), (tenant_in, tenant_ref)]
        )
    ]
    for copy in small + copies:
        copy.start()
    for copy in small:
        copy.wait()
    diagonal = lax.broadcasted_iota(jnp.int32, (rows, rows), 0) == lax.broadcasted_iota(jnp.int32, (rows, rows), 1)

    def column(row):
        return jnp.sum(jnp.where(diagonal, row, 0.0), axis=1, keepdims=True)

    chosen, logits = chosen_ref[...].astype(F32), logits_ref[...]
    columns = [column(chosen[0:1]), column(chosen[1:2]), column(tenant_ref[...].astype(F32))]
    rests = [column(logits[0:1]), column(logits[1:2])]
    for _ in range(3):
        pieces = [rest.astype(BF16).astype(F32) for rest in rests]
        columns += pieces
        rests = [rest - piece for rest, piece in zip(rests, pieces)]
    lane = lax.broadcasted_iota(jnp.int32, (rows, 128), 1)
    facts = jnp.zeros((rows, 128), F32)
    for number, value in enumerate(columns):
        facts = jnp.where(lane == number, value, facts)
    first_ref[:, width:] = facts.astype(BF16)
    for copy in copies:
        copy.wait()


def token_parts_of(tokens, chosen_experts, logits, tenant):
    rows, width = tokens.shape[0], tokens.shape[1] // 2
    return pl.pallas_call(
        parts_kernel,
        out_shape=(
            jax.ShapeDtypeStruct((rows, width + 128), BF16),
            jax.ShapeDtypeStruct((rows, width), BF16),
        ),
        in_specs=[pl.BlockSpec(memory_space=pltpu.HBM)] * 4,
        out_specs=(vmem(),) * 2,
        scratch_shapes=[
            pltpu.VMEM((2, rows), jnp.int32),
            pltpu.VMEM((2, rows), F32),
            pltpu.VMEM((1, rows), jnp.int32),
            pltpu.SemaphoreType.DMA((5,)),
        ],
        cost_estimate=SMALL,
        compiler_params=params(LIMIT_EARLY),
        name="token_parts",
    )(
        *[
            pltpu.with_memory_space_constraint(x, pltpu.HBM)
            for x in (tokens, chosen_experts.T, logits.T, tenant.reshape(1, rows))
        ]
    )


def meta_kernel(n_local, local_halves, ids_ref, adapter_ref, pool_slot_ref, *refs):
    blocks, (p_ref, pt_ref, cols_ref, rows_ref, tslot_ref) = refs[:-5], refs[-5:]
    at = blocks[0].shape[1] - 128
    facts = jnp.concatenate([block[:, at:] for block in blocks], axis=0).astype(F32).T
    count = facts.shape[1]
    first, second, tenant = facts[0:1], facts[1:2], facts[2:3]
    logit_first = (facts[3:4] + facts[5:6]) + facts[7:8]
    logit_second = (facts[4:5] + facts[6:7]) + facts[8:9]
    weight_first = jax.nn.sigmoid(logit_first - logit_second)
    weight_second = jax.nn.sigmoid(logit_second - logit_first)
    slot = jnp.zeros_like(tenant)
    for number in range(adapter_ref.shape[0]):
        slot = jnp.where(tenant == number, pool_slot_ref[adapter_ref[number]].astype(F32), slot)
    members, weights = [], []
    for i in range(n_local):
        expert = (ids_ref[0] * local_halves // 2 + i).astype(F32)
        hit_first, hit_second = first == expert, second == expert
        members.append(jnp.where(hit_first | hit_second, 1.0, 0.0))
        weights.append(jnp.where(hit_first, weight_first, 0.0) + jnp.where(hit_second, weight_second, 0.0))
    member = jnp.concatenate(members + [jnp.zeros((8 - n_local, count), F32)], axis=0)
    before = (
        lax.broadcasted_iota(jnp.int32, (count, count), 0) < lax.broadcasted_iota(jnp.int32, (count, count), 1)
    ).astype(BF16)
    place = jnp.where(member > 0, mm(member.astype(BF16), before), -1.0)
    table = jnp.concatenate(
        [place[0:n_local]] + weights + [slot] + [jnp.zeros((127 - 2 * n_local, count), F32)], axis=0
    )
    columns = table.T
    cols_ref[...] = columns
    rows_ref[...] = table[0:8]
    row_count = p_ref.shape[1]
    tenant_rows = jnp.broadcast_to(tenant, (8, count)).astype(BF16)
    down = lax.broadcasted_iota(jnp.int32, (row_count, count), 0).astype(F32)
    across = lax.broadcasted_iota(jnp.int32, (count, row_count), 1).astype(F32)
    for i in range(n_local):
        picked = (down == place[i : i + 1]).astype(BF16)
        p_ref[i] = picked
        pt_ref[i] = (across == columns[:, i : i + 1]).astype(BF16)
        tslot_ref[i] = mm_nt(tenant_rows, picked)


def build_meta(blocks, ids, adapters, pool_slots, n_local, local_halves, row_count):
    count = sum(block.shape[0] for block in blocks)
    return pl.pallas_call(
        functools.partial(meta_kernel, n_local, local_halves),
        out_shape=(
            jax.ShapeDtypeStruct((n_local, row_count, count), BF16),
            jax.ShapeDtypeStruct((n_local, count, row_count), BF16),
            jax.ShapeDtypeStruct((count, 128), F32),
            jax.ShapeDtypeStruct((8, count), F32),
            jax.ShapeDtypeStruct((n_local, 8, row_count), F32),
        ),
        in_specs=[smem()] * 3 + [vmem()] * len(blocks),
        out_specs=(vmem(),) * 5,
        cost_estimate=SMALL,
        compiler_params=params(max(LIMIT_EARLY, 12 * count * count // MIB)),
        name="routing_tables",
    )(ids, adapters, pool_slots, *blocks)


def slab_copies(gate_ref, up_ref, into_ref, sems, part, half):
    depth, width = into_ref.shape[1], into_ref.shape[2]
    copies = []
    for number in range(into_ref.shape[0]):
        source = (gate_ref, up_ref)[number % 2].at[half, pl.ds(part * depth, depth), pl.ds(number // 2 * width, width)]
        copies.append(pltpu.make_async_copy(source, into_ref.at[number], sems.at[half, number]))
    return copies


def prefetch_kernel(ids_ref, gate_ref, up_ref, *refs):
    slabs, (mark_ref, sems) = refs[:-2], refs[-2:]
    copies = [copy for half, slab in enumerate(slabs) for copy in slab_copies(gate_ref, up_ref, slab, sems, 0, half)]
    for copy in copies:
        copy.start()
    mark_ref[...] = jnp.zeros_like(mark_ref)
    for copy in copies:
        copy.wait()


def prefetch(ids, gate, up, part_width):
    local_halves, _, hidden_count = gate.shape
    tile = min(N_TILE, hidden_count)
    each = 2 * hidden_count // tile
    return pl.pallas_call(
        prefetch_kernel,
        out_shape=(pltpu.VMEM((each, part_width, tile), BF16),) * local_halves + (jax.ShapeDtypeStruct((8, 128), F32),),
        in_specs=[smem()] + [pl.BlockSpec(memory_space=pltpu.HBM)] * 2,
        out_specs=(vmem(),) * (local_halves + 1),
        scratch_shapes=[pltpu.SemaphoreType.DMA((local_halves, each))],
        cost_estimate=SMALL,
        compiler_params=params(LIMIT_EARLY),
        name="weight_prefetch",
    )(ids, gate, up)


def pack(blocks, p_ref, packed):
    depth = packed.shape[2]
    whole = jnp.concatenate([block[:, :depth] for block in blocks], axis=0)
    for i in range(p_ref.shape[0]):
        packed[i] = mm(p_ref[i], whole).astype(BF16)


def down_slabs(down, n_ad, halves=None):
    return pltpu.VMEM((halves or down.shape[0], down.shape[1], down.shape[2] // n_ad), BF16)


def down_fetch(n_ad, step, ids_ref, down_ref, into_ref, sems, pieces=2, first=0):
    halves, rows, span = into_ref.shape
    rows = rows // pieces
    start = pl.multiple_of(lax.rem(ids_ref[1] + step, n_ad) * span, span)
    return [
        pltpu.make_async_copy(
            down_ref.at[first + half, pl.ds(i * rows, rows), pl.ds(start, span)],
            into_ref.at[half, pl.ds(i * rows, rows)],
            sems.at[half, i],
        )
        for half in range(halves)
        for i in range(pieces)
    ]


def first_kernel(n_blocks, local_halves, *refs):
    blocks, refs = refs[:n_blocks], refs[n_blocks:]
    _, p_ref, gate_ref, up_ref, adapter_ref, pool_slot_ref, pool_ref, refs = *refs[:7], refs[7:]
    slabs, refs = refs[:local_halves], refs[local_halves:]
    ahead, (gate_out, up_out, factors, mark_out, packed, sems, factor_sems) = refs[:-7], refs[-7:]
    mark_out[...] = jnp.zeros_like(mark_out)
    factor_copies = []
    rank = pool_ref.shape[2]
    for number in range(adapter_ref.shape[0]):
        source = pool_ref.at[pool_slot_ref[adapter_ref[number]]]
        into = factors.at[:, number * rank : (number + 1) * rank]
        factor_copies.append(pltpu.make_async_copy(source, into, factor_sems.at[number]))
    for copy in factor_copies:
        copy.start()
    pack(blocks, p_ref, packed)
    slabs = list(ahead) + list(slabs[len(ahead) :])
    copies = [slab_copies(gate_ref, up_ref, slab, sems, 1, half) for half, slab in enumerate(ahead)]
    halves_each = local_halves // p_ref.shape[0]
    for half in range(local_halves):
        rows = packed[half // halves_each]
        tiles, _, width = slabs[half].shape
        for tile in range(tiles // 2):
            span = slice(tile * width, (tile + 1) * width)
            gate_out[half, :, span] = mm(rows, slabs[half][2 * tile])
            up_out[half, :, span] = mm(rows, slabs[half][2 * tile + 1])
            if half < len(ahead):
                copies[half][2 * tile].start()
                copies[half][2 * tile + 1].start()
    for copy in [copy for half in copies for copy in half] + factor_copies:
        copy.wait()


def first_part(blocks, mark, picked, gate, up, adapters, pool_slots, pool, slabs):
    local_halves, _, hidden_count = gate.shape
    n_local, row_count, _ = picked.shape
    each, part_width, _ = slabs[0].shape
    tenants, rank = adapters.shape[0], pool.shape[2]
    hbm = pl.BlockSpec(memory_space=pltpu.HBM)
    sums = pltpu.VMEM((local_halves, row_count, hidden_count), F32)
    n_ahead = max(1, local_halves - 2)
    return pl.pallas_call(
        functools.partial(first_kernel, len(blocks), local_halves),
        out_shape=(pltpu.VMEM(slabs[0].shape, BF16),) * n_ahead
        + (sums, sums, pltpu.VMEM((local_halves, tenants * rank, hidden_count), BF16), jax.ShapeDtypeStruct((8, 128), F32)),
        in_specs=[vmem()] * (len(blocks) + 2) + [hbm, hbm, smem(), smem(), hbm] + [vmem()] * local_halves,
        out_specs=(vmem(),) * (n_ahead + 4),
        scratch_shapes=[
            pltpu.VMEM((n_local, row_count, part_width), BF16),
            pltpu.SemaphoreType.DMA((n_ahead, each)),
            pltpu.SemaphoreType.DMA((tenants,)),
        ],
        input_output_aliases={len(blocks) + 7 + half: half for half in range(n_ahead)},
        cost_estimate=SMALL,
        compiler_params=params(max(LIMIT_EARLY, 10 * n_local * row_count * part_width // MIB)),
        name="gate_up_first",
    )(*blocks, mark, picked, gate, up, adapters, pool_slots, pool, *[pltpu.with_memory_space_constraint(x, pltpu.VMEM) for x in slabs])


def second_kernel(n_blocks, n_ahead, n_ad, steps, *refs):
    blocks, refs = refs[:n_blocks], refs[n_blocks:]
    p_ref, gate_ref, up_ref, refs = *refs[1:4], refs[4:]
    ahead, gate_in, up_in, refs = refs[:n_ahead], refs[n_ahead], refs[n_ahead + 1], refs[n_ahead + 2 :]
    ids_ref, factors, tslot_ref, rows_ref, down_ref, refs = *refs[:5], refs[5:]
    hidden_ref, low_ref, refs = refs[0], refs[1], refs[2:]
    nexts, (packed, down_sems, late, sems) = refs[:-4], refs[-4:]
    n_local = p_ref.shape[0]
    local_halves, _, hidden_count = gate_ref.shape
    halves_each = local_halves // n_local
    slabs = list(ahead) + [late] * (local_halves - n_ahead)
    copies = {
        half: slab_copies(gate_ref, up_ref, slabs[half], sems, 1, half) for half in range(n_ahead, local_halves)
    }
    rank = RANK
    tenants = factors.shape[1] // rank
    down_copies = []
    for number, step in enumerate(steps):
        down_copies += down_fetch(n_ad, step, ids_ref, down_ref, nexts[number], down_sems.at[number], 1)
    for copy in copies.get(n_ahead, []) + down_copies:
        copy.start()
    pack(blocks, p_ref, packed)
    for half in range(local_halves):
        rows = packed[half // halves_each]
        tiles, _, width = slabs[half].shape
        for tile in range(tiles // 2):
            span = slice(tile * width, (tile + 1) * width)
            values = []
            for number in (2 * tile, 2 * tile + 1):
                if half in copies:
                    copies[half][number].wait()
                values.append(mm(rows, slabs[half][number]))
                if half in copies and half + 1 in copies:
                    copies[half + 1][number].start()
            gate = values[0] + gate_in[half, :, span]
            up = values[1] + up_in[half, :, span]
            hidden_ref[half, :, span] = (silu(gate) * up).astype(BF16)
    for i in range(n_local):
        low = mm_nt(factors[i * halves_each], hidden_ref[i * halves_each])
        for half in range(i * halves_each + 1, (i + 1) * halves_each):
            low = low + mm_nt(factors[half], hidden_ref[half])
        owner = tslot_ref[i][0:1]
        total = jnp.zeros((rank, low.shape[1]), F32)
        for number in range(tenants):
            total = total + jnp.where(owner == number, low[number * rank : (number + 1) * rank], 0.0)
        weight = rows_ref[n_local + i : n_local + i + 1]
        low_ref[i * rank : (i + 1) * rank] = (mm(total.astype(BF16), p_ref[i]) * weight).astype(BF16)
    for copy in down_copies:
        copy.wait()


def second_part(
    blocks, mark, picked, gate, up, ahead, sums, ids, factors, tslot, table_rows, down, n_ad, steps
):
    local_halves, _, hidden_count = gate.shape
    n_local, row_count, count = picked.shape
    each, part_width, tile = ahead[0].shape
    rank = RANK
    hbm = pl.BlockSpec(memory_space=pltpu.HBM)
    held = [pltpu.with_memory_space_constraint(x, pltpu.VMEM) for x in (*ahead, *sums)]
    factors = pltpu.with_memory_space_constraint(factors, pltpu.VMEM)
    late_bytes = 2 * each * part_width * tile
    return pl.pallas_call(
        functools.partial(second_kernel, len(blocks), len(ahead), n_ad, steps),
        out_shape=(
            pltpu.VMEM((local_halves, row_count, hidden_count), BF16),
            jax.ShapeDtypeStruct((n_local * rank, count), BF16),
            *[down_slabs(down, n_ad, None if i == 0 else max(1, local_halves // 2)) for i in range(len(steps))],
        ),
        in_specs=[vmem()] * (len(blocks) + 2) + [hbm, hbm] + [vmem()] * len(held) + [smem()] + [vmem()] * 3 + [hbm],
        out_specs=(vmem(),) * (2 + len(steps)),
        scratch_shapes=[
            pltpu.VMEM((n_local, row_count, part_width), BF16),
            pltpu.SemaphoreType.DMA((len(steps), local_halves, 2)),
            pltpu.VMEM((each, part_width, tile), BF16),
            pltpu.SemaphoreType.DMA((local_halves, each)),
        ],
        cost_estimate=SMALL,
        compiler_params=params(
            max(LIMIT_EARLY, 10 * n_local * row_count * part_width // MIB) + late_bytes // MIB + 1
        ),
        name="gate_up_second",
    )(*blocks, mark, picked, gate, up, *held, ids, factors, tslot, table_rows, down)


def weighted_down(hidden_ref, weights, pt_ref, cols_ref):
    slabs = [ref.at[half] for ref in weights for half in range(ref.shape[0])]
    n_local = pt_ref.shape[0]
    halves_each = hidden_ref.shape[0] // n_local
    total = None
    for i in range(n_local):
        part_sum = mm(hidden_ref[i * halves_each], slabs[i * halves_each][...])
        for half in range(i * halves_each + 1, (i + 1) * halves_each):
            part_sum = part_sum + mm(hidden_ref[half], slabs[half][...])
        laid = mm(pt_ref[i], part_sum.astype(BF16)) * cols_ref[:, n_local + i : n_local + i + 1]
        total = laid if total is None else total + laid
    return total


def down_first_kernel(n_ad, step, ids_ref, hidden_ref, weight_ref, pt_ref, cols_ref, down_ref, keep, send, *refs):
    copies = []
    if refs:
        into, sems = refs
        copies = down_fetch(n_ad, step, ids_ref, down_ref, into, sems, 2, down_ref.shape[0] - into.shape[0])
    for copy in copies:
        copy.start()
    write_pairs(weighted_down(hidden_ref, [weight_ref], pt_ref, cols_ref), (keep, send))
    for copy in copies:
        copy.wait()


def down_first(ids, hidden, weights, pt, cols, down, n_ad, step, left):
    count, span = pt.shape[1], weights.shape[2]
    return pl.pallas_call(
        functools.partial(down_first_kernel, n_ad, step),
        out_shape=(jax.ShapeDtypeStruct((count // 2, span), BF16),) * 2
        + ((down_slabs(down, n_ad, left),) if left else ()),
        in_specs=[smem()] + [vmem()] * 4 + [pl.BlockSpec(memory_space=pltpu.HBM)],
        out_specs=(vmem(),) * (3 if left else 2),
        scratch_shapes=[pltpu.SemaphoreType.DMA((left, 2))] if left else [],
        cost_estimate=SMALL,
        compiler_params=params(max(LIMIT, 12 * count * span // MIB)),
        name="down_first",
    )(ids, hidden, pltpu.with_memory_space_constraint(weights, pltpu.VMEM), pt, cols, down)


def down_rest_kernel(n_weights, n_ad, steps, ids_ref, hidden_ref, pt_ref, cols_ref, down_ref, *refs):
    weights, (keep, send, base), refs = refs[:n_weights], refs[n_weights : n_weights + 3], refs[n_weights + 3 :]
    held, sems = refs[:-1], refs[-1]
    copies = [
        down_fetch(n_ad, step, ids_ref, down_ref, into, sems.at[number])
        for number, (step, into) in enumerate(zip(steps[1:], held))
    ]
    for copy in [copy for group in copies for copy in group]:
        copy.start()
    span = base.shape[1]
    for number in range(len(steps)):
        if number:
            for copy in copies[number - 1]:
                copy.wait()
        total = weighted_down(hidden_ref, [held[number - 1]] if number else weights, pt_ref, cols_ref)
        if number < len(steps) - 1:
            write_pairs(total, (keep, send), number * span)
        else:
            base[...] = total


def down_rest(ids, hidden, weights, pt, cols, down, n_ad, steps):
    count, span = pt.shape[1], down.shape[2] // n_ad
    chunk = (*down.shape[:2], span)
    return pl.pallas_call(
        functools.partial(down_rest_kernel, len(weights), n_ad, steps),
        out_shape=(jax.ShapeDtypeStruct((count // 2, span * (len(steps) - 1)), BF16),) * 2
        + (jax.ShapeDtypeStruct((count, span), F32),),
        in_specs=[smem()] + [vmem()] * 3 + [pl.BlockSpec(memory_space=pltpu.HBM)] + [vmem()] * len(weights),
        out_specs=(vmem(),) * 3,
        scratch_shapes=[pltpu.VMEM(chunk, BF16)] * (len(steps) - 1)
        + [pltpu.SemaphoreType.DMA((len(steps) - 1, down.shape[0], 2))],
        cost_estimate=SMALL,
        compiler_params=params(max(LIMIT, 12 * count * span // MIB) + (len(steps) - 1) * math.prod(chunk) * 2 // MIB),
        name="down_rest",
    )(ids, hidden, pt, cols, down, *[pltpu.with_memory_space_constraint(x, pltpu.VMEM) for x in weights])


def write_pairs(total, outs, at=0):
    keep, send = outs
    for b in range(total.shape[0] // 128):
        block = total[b * 128 : b * 128 + 128].astype(BF16)
        (send if b % 2 else keep)[b // 2 * 128 : b // 2 * 128 + 128, pl.ds(at, total.shape[1])] = block


def adapter_kernel(slot_column, local_halves, ids_ref, base_ref, cols_ref, factor_ref, low_ref, keep, send, wide):
    blocks = base_ref.shape[0] // 128
    height = low_ref.shape[0] // blocks
    wide[...] = jnp.zeros_like(wide)
    for m in range(blocks):
        row = pl.multiple_of(((ids_ref[0] ^ m) * local_halves // 2) * RANK, RANK)
        value = low_ref[m * height : (m + 1) * height].astype(F32)
        value = jnp.concatenate([value[:, (m ^ b) * 128 : (m ^ b) * 128 + 128] for b in range(blocks)], axis=1)
        wide[pl.ds(row, height)] += value
    low = wide[...].T.astype(BF16)
    zero = jnp.zeros_like(low)
    slot = cols_ref[:, slot_column : slot_column + 1]
    depth = EXPERT_COUNT * RANK
    slot_count = factor_ref.shape[0] // depth
    total = base_ref[...]
    for j in range(0, slot_count, 2):
        spread = jnp.concatenate(
            [jnp.where(slot == (ids_ref[0] * slot_count + j + i).astype(F32), low, zero) for i in range(2)], axis=1
        )
        total = total + mm(spread, factor_ref[j * depth : (j + 2) * depth])
    write_pairs(total, (keep, send))


def adapter_part(ids, base, cols, slot_column, local_halves, factors, low):
    count, span = base.shape
    return pl.pallas_call(
        functools.partial(adapter_kernel, slot_column, local_halves),
        out_shape=(jax.ShapeDtypeStruct((count // 2, span), BF16),) * 2,
        in_specs=[smem()] + [vmem()] * 4,
        out_specs=(vmem(),) * 2,
        scratch_shapes=[pltpu.VMEM((EXPERT_COUNT * RANK, count), F32)],
        cost_estimate=SMALL,
        compiler_params=params(max(LIMIT, 24 * count * span // MIB)),
        name="adapters",
    )(ids, base, cols, factors, low)


def split_kernel(keep_ref, came_ref, keep, send):
    for b in range(keep_ref.shape[0] // 128):
        total = keep_ref[b * 128 : b * 128 + 128].astype(F32) + came_ref[b * 128 : b * 128 + 128].astype(F32)
        (send if b % 2 else keep)[b // 2 * 128 : b // 2 * 128 + 128] = total.astype(BF16)


def split_sum(keep, came):
    return pl.pallas_call(
        split_kernel,
        out_shape=(jax.ShapeDtypeStruct((keep.shape[0] // 2, keep.shape[1]), BF16),) * 2,
        in_specs=[vmem()] * 2,
        out_specs=(vmem(),) * 2,
        cost_estimate=SMALL,
        compiler_params=params(LIMIT),
        name="sum_and_split",
    )(keep, came)


def cut_kernel(edges, keep_ref, came_ref, *outs):
    for first, last, out in zip(edges, edges[1:], outs):
        out[...] = (keep_ref[:, first:last].astype(F32) + came_ref[:, first:last].astype(F32)).astype(BF16)


def cut_sum(keep, came, edges):
    return pl.pallas_call(
        functools.partial(cut_kernel, edges),
        out_shape=tuple(
            jax.ShapeDtypeStruct((keep.shape[0], last - first), BF16) for first, last in zip(edges, edges[1:])
        ),
        in_specs=[vmem()] * 2,
        out_specs=(vmem(),) * (len(edges) - 1),
        cost_estimate=SMALL,
        compiler_params=params(LIMIT),
        name="sum_and_cut",
    )(keep, came)


def per_device(
    n_ep,
    n_ad,
    tokens,
    chosen_experts,
    router_gate_logits,
    token_tenant,
    adapter_of_tenant,
    adapter_pool_slot,
    gate_weight,
    up_weight,
    down_weight,
    adapter_input_factors,
    adapter_output_factors,
):
    gate_weight, up_weight, down_weight, adapter_input_factors = [
        pltpu.with_memory_space_constraint(x, pltpu.HBM)
        for x in (gate_weight, up_weight, down_weight, adapter_input_factors)
    ]
    width = tokens.shape[1]
    span = width // n_ad
    local_halves = gate_weight.shape[0]
    n_local = max(1, local_halves // 2)
    row_count = n_ep * CAP
    bits = n_ep.bit_length() - 1
    ids = jnp.stack([lax.axis_index("ep"), lax.axis_index("ad")]).astype(jnp.int32)

    def swap(x, mask):
        return lax.ppermute(x, "ep", [(i, i ^ mask) for i in range(n_ep)])

    def tie(x, y):
        return lax.optimization_barrier((x, y))

    def shift(x, step):
        return lax.ppermute(x, "ad", [(i, (i + step) % n_ad) for i in range(n_ad)])

    order = sorted(range(1, n_ad), key=lambda step: (step != n_ad // 2, step))
    token_part = token_parts_of(tokens, chosen_experts, router_gate_logits, token_tenant)
    *slabs, mark = prefetch(ids, gate_weight, up_weight, width // 2)
    high = 1 << (bits - 1)
    crossing = [swap(own, high) for own in token_part]

    def spread(part, crossed):
        blocks = {0: token_part[part], high: crossed}
        for bit in reversed(range(bits - 1)):
            for mask in list(blocks):
                blocks[mask | 1 << bit] = swap(blocks[mask], 1 << bit)
        return [blocks[mask] for mask in range(n_ep)]

    crossing[0], mark = tie(crossing[0], mark)
    blocks = spread(0, crossing[0])
    picked, pt, cols, table_rows, tslot = build_meta(
        blocks, ids, adapter_of_tenant, adapter_pool_slot, n_local, local_halves, row_count
    )
    *ahead, gate_sum, up_sum, factors, mark = first_part(
        blocks, mark, picked, gate_weight, up_weight, adapter_of_tenant, adapter_pool_slot, adapter_input_factors, slabs
    )
    crossing[1], mark = tie(crossing[1], mark)
    hidden, low, weights, *following = second_part(
        spread(1, crossing[1]), mark, picked, gate_weight, up_weight, ahead, (gate_sum, up_sum), ids, factors,
        tslot, table_rows, down_weight, n_ad, order[:2],
    )

    def onward(keep, came, first=1):
        for bit in range(first, bits):
            keep, send = split_sum(keep, came)
            came = swap(send, 1 << bit)
        return keep, came

    def other_of(low, bit):
        return lax.ppermute(low, "ad", [(i, i ^ 1 << bit) for i in range(n_ad)])

    def added(x, y):
        return (x.astype(F32) + y.astype(F32)).astype(BF16)

    far_steps = range(1, n_ad.bit_length() - 1)
    others = [other_of(low, bit) for bit in far_steps[:1]]
    left = local_halves - following[0].shape[0]
    keep, send, *later = down_first(ids, hidden, weights, pt, cols, down_weight, n_ad, order[1], left)
    others, keep, send, later = lax.optimization_barrier((others, keep, send, later))
    for bit in far_steps:
        low = added(low, others[0] if bit == 1 else other_of(low, bit))
    for bit in range(bits - 1):
        low = jnp.concatenate([low, swap(low, 1 << bit)], axis=0)
    crossed = swap(low, 1 << (bits - 1))
    keep, came = onward(keep, swap(send, 1), 1)
    keep, hidden = tie(keep, hidden)
    keep_rest, send_rest, base = down_rest(ids, hidden, following + later, pt, cols, down_weight, n_ad, (*order[1:], 0))
    came, crossed, keep_rest, send_rest, base = lax.optimization_barrier((came, crossed, keep_rest, send_rest, base))
    low = jnp.concatenate([low, crossed], axis=0)
    low = added(low, other_of(low, 0))
    (sums,) = cut_sum(keep, came, (0, span))
    results = [shift(sums, order[0])]
    keep_rest, came_rest = onward(keep_rest, swap(send_rest, 1))
    slot_count = adapter_output_factors.shape[0]
    flat_factors = adapter_output_factors.reshape(slot_count * EXPERT_COUNT * RANK, span)
    keep, send = adapter_part(ids, base, cols, 2 * n_local, local_halves, flat_factors, low)
    came_rest, results, keep, send = lax.optimization_barrier((came_rest, results, keep, send))
    came = swap(send, 1)
    if bits > 1:
        keep, send = split_sum(keep, came)
        came_rest, keep, send = lax.optimization_barrier((came_rest, keep, send))
        came = swap(send, 2)
    keep, came = onward(keep, came, 2)
    parts = cut_sum(keep_rest, came_rest, [span * i for i in range(n_ad - 1)])
    results += [shift(x, step) for x, step in zip(parts, order[1:])]
    return sum(x.astype(F32) for x in [keep, came] + results).astype(BF16)


def solution(mesh):
    placed = (
        P(("rep", "ep"), None),
        P(("rep", "ep"), None),
        P(("rep", "ep"), None),
        P(("rep", "ep")),
        P("rep"),
        P(),
        P("ep", None, "ad"),
        P("ep", None, "ad"),
        P("ep", "ad", None),
        P(None, "ep", None, "ad"),
        P("ep", None, None, "ad"),
    )
    return jax.shard_map(
        functools.partial(per_device, mesh.shape["ep"], mesh.shape["ad"]),
        mesh=mesh,
        in_specs=placed,
        out_specs=P(("rep", "ep"), "ad"),
        check_vma=False,
    )
```
